32 devices in a mesh: blk: 8 (over y, x, core), sims: 4 (over z).
Axes of the slice: x: 2, y: 2, z: 4, core: 2. Of those that a mesh axis runs over, the one named last changes fastest.
Arguments:
- rhs: float32 [4, 8, 256, 512], P(None, 'blk', None, 'sims'), parts along dimension 3, may hold values from -6 to 6
- lower_blocks: float32 [4, 8, 3, 256, 256], P(None, 'blk'), may hold values from -0.16875 to 0.16875
- col_index: int32 [4, 8, 3], P(None, 'blk'), may hold values from -1 to 30, as said below
- diag_inverse: float32 [4, 8, 256, 256], P(None, 'blk'), may hold values from -1.5 to 1.5, as said below
- turnout: float32 [4, 8, 256], P(None, 'blk'), may hold values from 0.2 to 5
- district_of: int32 [4, 8, 256], P(None, 'blk'), may hold values from 0 to 255, as said below
Outputs:
- solution: float32 [4, 8, 256, 512], P(None, 'blk', None, 'sims'), parts along dimension 3
- district_mean: float32 [256, 512], P('blk', 'sims'), parts along dimension 1
The draws below stay inside these ranges and needn't reach their ends.
There are 4 independent parts, one for each index of `sims`. The reference program is written for one: setup_inputs(seed, part) draws one part's arguments, and reference() takes and returns one part's arrays. A program takes and returns all parts, laid end to end along the dimension named above; an argument that names none is the same for every part. Nothing has to cross between parts.
Inputs may be any that keep to these rules, and one draw needn't show every extreme that they name: `col_index`: entry [r, p, k] belongs to block row i = r * 8 + p. Slot 0 holds i - 1 (-1 for i = 0); the other slots hold distinct columns from i - 4 to i - 2, or -1 where the block is absent. `diag_inverse`: each block is lower triangular. `district_of`: each district holds exactly 32 precincts.
All inputs are finite; a program needn't handle non-finite values.
Results may differ from the reference program's by a relative error of at most 0.0002.
Values sent between devices are 32-bit elements; how exact they have to be, the bound alone decides.
No kernel may reach another device: no remote copies, remote signals or barrier semaphores. Data moves between devices by JAX's collectives and lax.ppermute only.
A program may use at most 64 MiB of HBM per device.

```python
import math
import jax
import jax.numpy as jnp
from jax import lax

BS = 256
SIMS = 128
ROWS_DEV = 4
KMAX = 3
WIN = 4
NDIST = 256
N_BLK = 8


def draw_lower_blocks(key, part):
    shape_full = (ROWS_DEV, N_BLK, KMAX, BS, BS)
    values = jnp.clip(jax.random.normal(key, shape_full, jnp.float32), -4.0, 4.0) * (0.675 * BS ** (-0.5))
    return values.astype(jnp.float32)


def draw_col_index(key, part):
    first_key, second_key = jax.random.split(key)
    row_number = jnp.arange(ROWS_DEV, dtype=jnp.int32)[:, None] * N_BLK + jnp.arange(N_BLK, dtype=jnp.int32)[None, :]
    scores = jax.random.randint(first_key, (ROWS_DEV, N_BLK, WIN - 1), 0, 4096) * WIN + jnp.arange(WIN - 1, dtype=jnp.int32)
    ranking = jnp.argsort(scores, axis=-1).astype(jnp.int32)
    offsets = ranking[..., :KMAX - 1] + 2
    keep_flag = jax.random.randint(second_key, (ROWS_DEV, N_BLK, KMAX - 1), 0, 2)
    extra_columns = row_number[..., None] - offsets
    extra_columns = jnp.where((keep_flag == 1) & (extra_columns >= 0), extra_columns, -1)
    first_column = jnp.where(row_number >= 1, row_number - 1, -1)
    return jnp.concatenate([first_column[..., None], extra_columns], axis=-1).astype(jnp.int32)


def draw_diag_inverse(key, part):
    diag_key, lower_key = jax.random.split(key)
    diagonal = jax.random.uniform(diag_key, (ROWS_DEV, N_BLK, BS), jnp.float32, 0.6, 1.2)
    lower_part = jnp.clip(jax.random.normal(lower_key, (ROWS_DEV, N_BLK, BS, BS), jnp.float32), -4.0, 4.0) * (0.6 * BS ** (-0.5))
    strict_lower = jnp.tril(jnp.ones((BS, BS), jnp.float32), -1)
    identity = jnp.eye(BS, dtype=jnp.float32)
    return lower_part * strict_lower + identity * diagonal[..., :, None]


def draw_district_of(key, part):
    shuffled = jax.random.permutation(key, ROWS_DEV * N_BLK * BS).astype(jnp.int32)
    return (shuffled % NDIST).reshape(ROWS_DEV, N_BLK, BS).astype(jnp.int32)


def levels(key, extent, shards, low, high):
    def one(position, parts):
        steps = jax.random.uniform(jax.random.fold_in(jax.random.fold_in(key, 6), position), (parts,), jnp.float32, low / len(shards), high / len(shards))
        return jnp.repeat(jnp.exp(steps), extent[position] // parts).reshape((-1,) + (1,) * (len(extent) - position - 1))

    factor_of = one(*shards[0])
    for cut in shards[1:]:
        factor_of = factor_of * one(*cut)
    return factor_of


def scatter_about(own_key, shape, deviation, most, cuts=(), held_as=jnp.bfloat16):
    gain = levels(own_key, shape, cuts, -0.22, 0.18) if cuts else 1.0
    array = jax.random.normal(own_key, shape, jnp.float32) * deviation * gain
    return jnp.minimum(jnp.maximum(array, -most), most).astype(held_as)


def setup_inputs(seed: int = 0, part: int = 0) -> dict:
    splits = jax.random.split(jax.random.key(seed), 7)
    own_keys = jax.random.split(jax.random.fold_in(splits[6], part), 7)
    rhs = scatter_about(own_keys[0], (ROWS_DEV, N_BLK, BS, SIMS), 1.0, 6.0, ((1, 8),), jnp.float32)
    lower_blocks = draw_lower_blocks(jax.random.fold_in(splits[6], 71), part)
    col_index = draw_col_index(jax.random.fold_in(splits[6], 71), part)
    diag_inverse = draw_diag_inverse(jax.random.fold_in(splits[6], 71), part)
    turnout = jnp.clip(jnp.exp(math.log(5.0) - 3.218876 * jax.random.uniform(splits[4], (ROWS_DEV, N_BLK, BS), jnp.float32) ** levels(splits[4], (ROWS_DEV, N_BLK, BS), ((1, 8),), -0.2, 0.2)), 0.2, 5.0)
    district_of = draw_district_of(jax.random.fold_in(splits[6], 71), part)
    return {"rhs": rhs, "lower_blocks": lower_blocks, "col_index": col_index, "diag_inverse": diag_inverse, "turnout": turnout, "district_of": district_of}


precise = lax.Precision.HIGHEST


def reference(rhs, lower_blocks, col_index, diag_inverse, turnout, district_of):
    total_rows = ROWS_DEV * N_BLK
    rhs_rows = rhs.reshape(total_rows, BS, SIMS)
    factor_rows = lower_blocks.reshape(total_rows, KMAX, BS, BS)
    column_rows = col_index.reshape(total_rows, KMAX)
    inverse_rows = diag_inverse.reshape(total_rows, BS, BS)

    def advance(count, loop_state):
        solution, pending = loop_state
        row_now = (total_rows - 1 - count).astype(jnp.int32)
        solved = jnp.einsum('ab,as->bs', inverse_rows[row_now], rhs_rows[row_now] - pending[row_now], precision=precise)
        solution = solution.at[row_now].set(solved)
        for slot_index in range(KMAX):
            target = column_rows[row_now, slot_index]
            update_term = jnp.einsum('ab,as->bs', factor_rows[row_now, slot_index], solved, precision=precise)
            update_term = jnp.where(target >= 0, update_term, jnp.zeros_like(update_term))
            pending = pending.at[jnp.maximum(target, 0)].add(update_term)
        return solution, pending

    empty_rows = jnp.zeros((total_rows, BS, SIMS), jnp.float32)
    solution, _ = lax.fori_loop(0, total_rows, advance, (empty_rows, empty_rows))
    cell_rows = solution.reshape(total_rows * BS, SIMS)
    weights = turnout.reshape(total_rows * BS)
    district_ids = district_of.reshape(total_rows * BS)
    numerator = jax.ops.segment_sum(weights[:, None] * cell_rows, district_ids, num_segments=NDIST)
    denominator = jax.ops.segment_sum(weights, district_ids, num_segments=NDIST)
    return solution.reshape(ROWS_DEV, N_BLK, BS, SIMS), numerator / denominator[:, None]
```

```python
import functools

import jax
import jax.numpy as jnp
from jax import lax
from jax.experimental import pallas as pl
from jax.experimental.pallas import tpu as pltpu
from jax.sharding import PartitionSpec as P

NDIST = 256
F32 = jnp.float32
B16 = jnp.bfloat16
VMEM_BYTES = 20 * 1024 * 1024
SMEM_SPEC = pl.BlockSpec(memory_space=pltpu.SMEM)
VMEM_SPEC = pl.BlockSpec(memory_space=pltpu.VMEM)


def params():
    return pltpu.CompilerParams(vmem_limit_bytes=VMEM_BYTES)


def cost(flops, moved):
    return pl.CostEstimate(flops=flops, bytes_accessed=moved, transcendentals=0)


def halves(x):
    hi = x.astype(B16)
    lo = (x - hi.astype(F32)).astype(B16)
    return hi, lo


def dot(a, b):
    return jnp.dot(a, b, preferred_element_type=F32)


def dot3(x, y):
    rows = x[0].shape[0]
    both = dot(jnp.concatenate([x[0], x[1]], axis=0), y[0])
    return both[:rows] + both[rows:] + dot(x[0], y[1])


def setup_kernel(s, own_l, oth_l, own_d, oth_d, own_r, oth_r, gh, gl, mh, ml, rt):
    is_a = s[0] == 1
    bs = own_l.shape[1]
    half = rt.shape[0]

    def upper(k):
        return jnp.where(is_a, own_l[k], oth_l[k])

    def lower(k):
        return jnp.where(is_a, oth_l[k], own_l[k])

    def at_distance(block, row, first_col, d):
        found = jnp.zeros((bs, bs), F32)
        for k in range(1, own_l.shape[0]):
            col = s[first_col + k]
            found = jnp.where((col == row - d) & (col >= 0), block(k), found)
        return found

    row_a, row_b = s[1], s[2]
    col_a, col_b = 3, 3 + own_l.shape[0]
    da = halves(jnp.where(is_a, own_d[...], oth_d[...]))
    db = halves(jnp.where(is_a, oth_d[...], own_d[...]))
    la1 = halves(upper(0))
    lb1 = halves(jnp.where(s[col_b] >= 0, lower(0), 0.0))
    la2 = halves(at_distance(upper, row_a, col_a, 2))
    la3 = halves(at_distance(upper, row_a, col_a, 3))
    la4 = halves(at_distance(upper, row_a, col_a, 4))
    lb2 = halves(at_distance(lower, row_b, col_b, 2))
    lb3 = halves(at_distance(lower, row_b, col_b, 3))
    lb4 = halves(at_distance(lower, row_b, col_b, 4))
    for place, pair in enumerate((da, db, la1, la4, lb3, lb4)):
        mh[place] = pair[0]
        ml[place] = pair[1]

    def put(i, j, value):
        hi, lo = halves(value)
        gh[i * bs : (i + 1) * bs, j * bs : (j + 1) * bs] = hi
        gl[i * bs : (i + 1) * bs, j * bs : (j + 1) * bs] = lo

    w = halves(dot3(da, la1))
    b_hi = dot3(db, lb1)
    b_lo = dot3(db, lb2)
    put(1, 0, b_hi)
    put(1, 1, b_lo)
    put(0, 0, dot3(da, la2) - dot3(w, halves(b_hi)))
    put(0, 1, dot3(da, la3) - dot3(w, halves(b_lo)))
    ra = jnp.where(is_a, own_r[...], oth_r[...]).T
    rb = jnp.where(is_a, oth_r[...], own_r[...]).T
    rt[:, :bs] = jnp.where(is_a, ra[half:], ra[:half])
    rt[:, bs:] = jnp.where(is_a, rb[half:], rb[:half])


def near_kernel(has_near, has_far, r_ref, *refs):
    refs = list(refs)
    v = r_ref[...]
    if has_far:
        v = v - refs.pop(0)[...]
    if has_near:
        v = v - refs.pop(0)[...]
    gh, gl, near, v_out = refs
    v_out[...] = v
    near[...] = dot3(halves(v), (gh[...], gl[...]))


def far_kernel(s, v_ref, mh, ml, keep_in, give_in, far, keep, give):
    is_a = s[0] == 1
    active = s[1] == 1
    bs = mh.shape[1]

    def m(k):
        return mh[k], ml[k]

    xa = dot3(halves(v_ref[:, :bs]), m(0))
    xah = halves(xa)
    xb = dot3(halves(v_ref[:, bs:] - dot3(xah, m(2))), m(1))
    xbh = halves(xb)
    far[:, :bs] = dot3(xah, m(3)) + dot3(xbh, m(4))
    far[:, bs:] = dot3(xbh, m(5))
    keep[...] = jnp.where(active, jnp.where(is_a, xa, xb), keep_in[...])
    give[...] = jnp.where(active, jnp.where(is_a, xb, xa), give_in[...])


def district_kernel(rows_here, *refs):
    keeps = refs[:rows_here]
    gives = refs[rows_here : 2 * rows_here]
    own_w, oth_w, own_d, oth_d, out = refs[2 * rows_here :]
    half, bs = keeps[0].shape
    names = lax.broadcasted_iota(jnp.int32, (NDIST, bs), 0)
    total = jnp.zeros((NDIST, 2 * half), F32)
    for r in range(rows_here):
        for x, w, d in ((keeps[r], own_w, own_d), (gives[r], oth_w, oth_d)):
            wr = w[r : r + 1, :]
            member = (names == d[r : r + 1, :]).astype(F32).astype(B16)
            terms = jnp.concatenate(
                [x[...] * wr, jnp.broadcast_to(wr, (half, bs))], axis=0
            )
            for part in halves(terms):
                total = total + lax.dot_general(
                    member, part, (((1,), (1,)), ((), ())), preferred_element_type=F32
                )
    out[...] = total


def field_kernel(rows_here, s, *refs):
    keeps = refs[:rows_here]
    gots = refs[rows_here : 2 * rows_here]
    out = refs[2 * rows_here]
    is_a = s[0] == 1
    for r in range(rows_here):
        top = jnp.where(is_a, gots[r][...], keeps[r][...])
        bottom = jnp.where(is_a, keeps[r][...], gots[r][...])
        out[r, 0] = jnp.concatenate([top, bottom], axis=0).T


def mean_kernel(x, out):
    half = x.shape[2] // 2
    sums = [x[0], x[1]]
    for k in range(2, x.shape[0]):
        sums[k % 2] = sums[k % 2] + x[k]
    out[...] = jnp.concatenate([t[:, :half] / t[:, half:] for t in sums], axis=1)


def body(rhs, lower_blocks, col_index, diag_inverse, turnout, district_of):
    n = lax.axis_size("blk")
    p = lax.axis_index("blk").astype(jnp.int32)
    pairs = n // 2
    core = lax.rem(p, 2)
    chip = lax.div(p, 2)
    rows_here, _, bs, columns = rhs.shape
    slots = lower_blocks.shape[2]
    half = columns // 2
    count = rows_here * pairs

    def shaped(*shape, dtype=F32):
        return jax.ShapeDtypeStruct(shape, dtype)

    def swap(x):
        return lax.ppermute(x, "blk", [(i, i ^ 1) for i in range(n)])

    def pass_on(x, by):
        perm = [(i, (i - 2 * by) % n) for i in range(n)]
        return lax.ppermute(x, "blk", perm)

    own_col = col_index[:, 0]
    oth_col = swap(own_col)
    col_a = jnp.where(core == 1, own_col, oth_col)
    col_b = jnp.where(core == 1, oth_col, own_col)

    fixed = {}
    arrived = None
    for r in range(rows_here - 1, -1, -1):
        own = (lower_blocks[r, 0], diag_inverse[r, 0], rhs[r, 0])
        if arrived is not None:
            own, _ = lax.optimization_barrier((own, arrived))
        oth = tuple(swap(x) for x in own)
        arrived = oth
        row_b = r * n + 2 * chip
        scalars = jnp.concatenate(
            [jnp.stack([core, row_b + 1, row_b]), col_a[r], col_b[r]]
        ).astype(jnp.int32)
        fixed[r] = pl.pallas_call(
            setup_kernel,
            out_shape=(
                shaped(2 * bs, 2 * bs, dtype=B16),
                shaped(2 * bs, 2 * bs, dtype=B16),
                shaped(6, bs, bs, dtype=B16),
                shaped(6, bs, bs, dtype=B16),
                shaped(half, 2 * bs),
            ),
            in_specs=[SMEM_SPEC] + [VMEM_SPEC] * 6,
            out_specs=(VMEM_SPEC,) * 5,
            compiler_params=params(),
            cost_estimate=cost(14 * 3 * bs**3, 24 * bs * bs * 4),
            name="pair_setup",
        )(scalars, own[0], oth[0], own[1], oth[1], own[2], oth[2])

    own_w, own_d = turnout[:, 0], district_of[:, 0]
    oth_w, oth_d = swap(own_w), swap(own_d)

    keeps, gives = {}, {}
    near = far_now = far_next = None
    for step in range(count):
        k = count - 1 - step
        r = k // pairs
        gh, gl, mh, ml, rt = fixed[r]
        taken = [x for x in (far_now, near) if x is not None]
        near_out, v = pl.pallas_call(
            functools.partial(near_kernel, near is not None, far_now is not None),
            out_shape=(shaped(half, 2 * bs), shaped(half, 2 * bs)),
            in_specs=[VMEM_SPEC] * (3 + len(taken)),
            out_specs=(VMEM_SPEC,) * 2,
            compiler_params=params(),
            cost_estimate=cost(6 * half * 4 * bs * bs, 6 * half * bs * 4),
            name="near_terms",
        )(rt, *taken, gh, gl)
        near = pass_on(near_out, 1) if step + 1 < count else None
        if r not in keeps:
            keeps[r] = jnp.zeros((half, bs), F32)
            gives[r] = jnp.zeros((half, bs), F32)
        active = (chip == k % pairs).astype(jnp.int32)
        far_out, keeps[r], gives[r] = pl.pallas_call(
            far_kernel,
            out_shape=(shaped(half, 2 * bs), shaped(half, bs), shaped(half, bs)),
            in_specs=[SMEM_SPEC] + [VMEM_SPEC] * 5,
            out_specs=(VMEM_SPEC,) * 3,
            compiler_params=params(),
            cost_estimate=cost(6 * half * 6 * bs * bs, 8 * half * bs * 4),
            name="far_terms",
        )(jnp.stack([core, active]), v, mh, ml, keeps[r], gives[r])
        far_now = far_next
        far_next = pass_on(far_out, 2) if step + 2 < count else None

    order = range(rows_here)
    share = pl.pallas_call(
        functools.partial(district_kernel, rows_here),
        out_shape=shaped(NDIST, columns),
        in_specs=[VMEM_SPEC] * (2 * rows_here + 4),
        out_specs=VMEM_SPEC,
        compiler_params=params(),
        cost_estimate=cost(8 * rows_here * NDIST * bs * columns, 4 * rows_here * bs * columns),
        name="district_terms",
    )(
        *[keeps[r] for r in order],
        *[gives[r] for r in order],
        own_w, oth_w, own_d, oth_d,
    )
    parts = lax.all_to_all(share.reshape(n, NDIST // n, columns), "blk", 0, 0)
    gots = swap(jnp.stack([gives[r] for r in order]))
    field = pl.pallas_call(
        functools.partial(field_kernel, rows_here),
        out_shape=shaped(rows_here, 1, bs, columns),
        in_specs=[SMEM_SPEC] + [VMEM_SPEC] * (2 * rows_here),
        out_specs=VMEM_SPEC,
        compiler_params=params(),
        cost_estimate=cost(0, 8 * rows_here * bs * columns),
        name="field",
    )(core[None], *[keeps[r] for r in order], *[gots[r] for r in order])
    mean = pl.pallas_call(
        mean_kernel,
        out_shape=shaped(NDIST // n, columns),
        in_specs=[VMEM_SPEC],
        out_specs=VMEM_SPEC,
        compiler_params=params(),
        name="district_mean",
    )(parts)
    return field, mean


def solution(mesh):
    placed = (
        P(None, "blk", None, "sims"),
        P(None, "blk", None, None, None),
        P(None, "blk", None),
        P(None, "blk", None, None),
        P(None, "blk", None),
        P(None, "blk", None),
    )
    return jax.shard_map(
        body,
        mesh=mesh,
        in_specs=placed,
        out_specs=(P(None, "blk", None, "sims"), P("blk", "sims")),
        check_vma=False,
    )
```

```python
import functools

import jax
import jax.numpy as jnp
from jax import lax
from jax.experimental import pallas as pl
from jax.experimental.pallas import tpu as pltpu
from jax.sharding import PartitionSpec as P

NDIST = 256
PIECES = 4
F32 = jnp.float32
B16 = jnp.bfloat16
SMEM_SPEC = pl.BlockSpec(memory_space=pltpu.SMEM)
VMEM_SPEC = pl.BlockSpec(memory_space=pltpu.VMEM)


def params(mib):
    return pltpu.CompilerParams(vmem_limit_bytes=mib * 1024 * 1024)


def cost(flops, moved):
    return pl.CostEstimate(flops=flops, bytes_accessed=moved, transcendentals=0)


def shaped(*shape, dtype=F32):
    return jax.ShapeDtypeStruct(shape, dtype)


def halves(x):
    hi = x.astype(B16)
    lo = (x - hi.astype(F32)).astype(B16)
    return hi, lo


def dot(a, b):
    return jnp.dot(a, b, preferred_element_type=F32)


def dot3(x, y):
    rows = x[0].shape[0]
    both = dot(jnp.concatenate([x[0], x[1]], axis=0), y[0])
    return both[:rows] + both[rows:] + dot(x[0], y[1])


def pack_kernel(l_ref, d_ref, r_ref, out):
    slots, bs = l_ref.shape[2], l_ref.shape[3]
    for k in range(slots):
        out[k * bs : (k + 1) * bs] = l_ref[0, 0, k]
    out[slots * bs : (slots + 1) * bs] = d_ref[0, 0]
    out[(slots + 1) * bs :] = r_ref[0, 0].T


def setup_kernel(r, n, slots, ids, own_col, oth_col, own, oth, gh, gl, mh, ml, rt):
    is_a = ids[0] == 1
    bs = own.shape[1]
    half = rt.shape[0]
    row_b = r * n + 2 * ids[1]
    row_a = row_b + 1

    def upper(k):
        where = slice(k * bs, (k + 1) * bs)
        return jnp.where(is_a, own[where], oth[where])

    def lower(k):
        where = slice(k * bs, (k + 1) * bs)
        return jnp.where(is_a, oth[where], own[where])

    def upper_col(k):
        return jnp.where(is_a, own_col[r, k], oth_col[r, k])

    def lower_col(k):
        return jnp.where(is_a, oth_col[r, k], own_col[r, k])

    def at_distance(block, column, row, d):
        found = jnp.zeros((bs, bs), F32)
        for k in range(1, slots):
            col = column(k)
            found = jnp.where((col == row - d) & (col >= 0), block(k), found)
        return halves(found)

    da, db = halves(upper(slots)), halves(lower(slots))
    la1 = halves(upper(0))
    for place, pair in enumerate((da, db, la1)):
        mh[place] = pair[0]
        ml[place] = pair[1]
    la = [at_distance(upper, upper_col, row_a, d) for d in (2, 3, 4)]
    lb = [halves(jnp.where(lower_col(0) >= 0, lower(0), 0.0))]
    lb += [at_distance(lower, lower_col, row_b, d) for d in (2, 3, 4)]

    def put(i, j, value):
        hi, lo = halves(value)
        gh[i * bs : (i + 1) * bs, j * bs : (j + 1) * bs] = hi
        gl[i * bs : (i + 1) * bs, j * bs : (j + 1) * bs] = lo

    w = halves(dot3(da, la1))
    for j in range(4):
        from_b = dot3(db, lb[j])
        put(1, j, from_b)
        from_a = -dot3(w, halves(from_b))
        if j < 3:
            from_a = from_a + dot3(da, la[j])
        put(0, j, from_a)
    top = (slots + 1) * bs
    ra = jnp.where(is_a, own[top:], oth[top:])
    rb = jnp.where(is_a, oth[top:], own[top:])
    rt[:, :bs] = jnp.where(is_a, ra[half:], ra[:half])
    rt[:, bs:] = jnp.where(is_a, rb[half:], rb[:half])


def step_kernel(lead, count, pairs, split, has_near, has_far, ids, *refs):
    refs = list(refs)
    far = refs.pop(0)[...] if has_far else None
    near = refs.pop(0)[...] if has_near else None
    near_out, far_out, v_out = refs[-3:]
    choices = [refs[3 * i : 3 * i + 3] for i in range((len(refs) - 3) // 3)]
    width, pending = v_out.shape
    piece = lax.rem(ids[1] - lead % pairs + pairs, pairs)
    pair = lead + piece
    piece = jnp.minimum(piece, PIECES - 1)
    rows = pl.ds(pl.multiple_of(piece * width, width), width)

    def run(gh, gl, rt):
        v = rt[rows, :]
        if has_far:
            v = v - jnp.where(pair < count - 2, far, 0.0)
        if has_near:
            v = v - jnp.where(pair < count - 1, near, 0.0)
        v_out[...] = v
        terms = dot3(halves(v), (gh[...], gl[...]))
        near_out[...] = terms[:, :pending]
        far_out[...] = terms[:, pending:]

    if len(choices) == 1:
        run(*choices[0])
        return

    @pl.when(pair < split)
    def _():
        run(*choices[0])

    @pl.when(pair >= split)
    def _():
        run(*choices[1])


def finish_kernel(r, pairs, window, has_total, ids, *refs):
    values = refs[:window]
    mh, ml, own_w, oth_w, own_d, oth_d = refs[window : window + 6]
    refs = refs[window + 6 :]
    total = refs[0][...] if has_total else None
    refs = refs[1:] if has_total else refs
    keep, give = refs[:2]
    outs = refs[2:]
    is_a = ids[0] == 1
    bs = mh.shape[1]
    half = keep.shape[0]
    pieces = []
    for m in range(PIECES):
        v = values[pairs - 1 + m][...]
        for q in range(1, pairs):
            v = jnp.where(ids[1] == q, values[pairs - 1 - q + m][...], v)
        pieces.append(v)
    v = jnp.concatenate(pieces, axis=0)

    def m(k):
        return mh[k], ml[k]

    xa = dot3(halves(v[:, :bs]), m(0))
    xb = dot3(halves(v[:, bs:] - dot3(halves(xa), m(2))), m(1))
    kept, given = jnp.where(is_a, xa, xb), jnp.where(is_a, xb, xa)
    keep[...] = kept
    give[...] = given
    if total is None:
        total = jnp.zeros((NDIST, 2 * half), F32)
    names = lax.broadcasted_iota(jnp.int32, (NDIST, bs), 0)
    for x, w, d in ((kept, own_w, own_d), (given, oth_w, oth_d)):
        wr = w[r : r + 1, :]
        member = (names == d[r : r + 1, :]).astype(F32).astype(B16)
        terms = jnp.concatenate([x * wr, jnp.broadcast_to(wr, (half, bs))], axis=0)
        for part in halves(terms):
            total = total + lax.dot_general(
                member, part, (((1,), (1,)), ((), ())), preferred_element_type=F32
            )
    if len(outs) == 1:
        outs[0][...] = total
        return
    parts, held = outs[:-1], outs[-1]
    held[...] = total
    rows = NDIST // pairs
    for by, part in enumerate(parts):
        chip = lax.rem(ids[1] + by, pairs)
        part[...] = held[pl.ds(pl.multiple_of(chip * rows, rows), rows), :]


def add_kernel(ids, *refs):
    mine, theirs = refs[-2:]
    total = refs[0][...]
    for part in refs[1:-2]:
        total = total + part[...]
    rows = mine.shape[0]
    is_a = ids[0] == 1
    mine[...] = jnp.where(is_a, total[rows:], total[:rows])
    theirs[...] = jnp.where(is_a, total[:rows], total[rows:])


def mean_kernel(ids, mine, got, out):
    half = out.shape[1] // 2
    own, oth = (x[:, :half] / x[:, half:] for x in (mine, got))
    is_a = ids[0] == 1
    out[...] = jnp.concatenate(
        [jnp.where(is_a, oth, own), jnp.where(is_a, own, oth)], axis=1
    )


def field_kernel(rows_here, ids, *refs):
    keeps = refs[:rows_here]
    gots = refs[rows_here : 2 * rows_here]
    out = refs[2 * rows_here]
    is_a = ids[0] == 1
    for r in range(rows_here):
        top = jnp.where(is_a, gots[r][...], keeps[r][...])
        bottom = jnp.where(is_a, keeps[r][...], gots[r][...])
        out[r, 0] = jnp.concatenate([top, bottom], axis=0).T


def body(rhs, lower_blocks, col_index, diag_inverse, turnout, district_of):
    n = lax.axis_size("blk")
    p = lax.axis_index("blk").astype(jnp.int32)
    pairs = n // 2
    ids = jnp.stack([lax.rem(p, 2), lax.div(p, 2)])
    rows_here, _, bs, columns = rhs.shape
    slots = lower_blocks.shape[2]
    half = columns // 2
    width = half // PIECES
    count = rows_here * pairs

    def swap(x):
        return lax.ppermute(x, "blk", [(i, i ^ 1) for i in range(n)])

    def pass_on(x, by):
        perm = [(i, (i - 2 * by) % n) for i in range(n)]
        return lax.ppermute(x, "blk", perm)

    own_col = col_index[:, 0]
    oth_col = swap(own_col)
    fixed = {}
    arrived = None
    packed_rows = (slots + 1) * bs + columns
    for r in range(rows_here - 1, -1, -1):
        own = pl.pallas_call(
            pack_kernel,
            out_shape=shaped(packed_rows, bs),
            grid=(1,),
            in_specs=[
                pl.BlockSpec((1, 1, slots, bs, bs), lambda i, r=r: (r, 0, 0, 0, 0)),
                pl.BlockSpec((1, 1, bs, bs), lambda i, r=r: (r, 0, 0, 0)),
                pl.BlockSpec((1, 1, bs, columns), lambda i, r=r: (r, 0, 0, 0)),
            ],
            out_specs=pl.BlockSpec((packed_rows, bs), lambda i: (0, 0)),
            compiler_params=params(8),
            cost_estimate=cost(0, 8 * packed_rows * bs),
            name="pack",
        )(lower_blocks, diag_inverse, rhs)
        if arrived is not None:
            own, _ = lax.optimization_barrier((own, arrived))
        oth = swap(own)
        arrived = oth
        fixed[r] = pl.pallas_call(
            functools.partial(setup_kernel, r, n, slots),
            out_shape=(
                shaped(2 * bs, 4 * bs, dtype=B16),
                shaped(2 * bs, 4 * bs, dtype=B16),
                shaped(3, bs, bs, dtype=B16),
                shaped(3, bs, bs, dtype=B16),
                shaped(half, 2 * bs),
            ),
            in_specs=[SMEM_SPEC] * 3 + [VMEM_SPEC] * 2,
            out_specs=(VMEM_SPEC,) * 5,
            compiler_params=params(12),
            cost_estimate=cost(24 * 3 * bs**3, 24 * bs * bs * 4),
            name="pair_setup",
        )(ids, own_col, oth_col, own, oth)

    own_w, own_d = turnout[:, 0], district_of[:, 0]
    oth_w, oth_d = swap(own_w), swap(own_d)

    def finish(r, values, total):
        _, _, mh, ml, _ = fixed[r]
        window = [values[count - 1 - (r * pairs + pairs - 1) + i] for i in range(pairs + PIECES - 1)]
        sums, scratch = (shaped(NDIST, columns),), []
        if r == 0:
            sums = (shaped(NDIST // pairs, columns),) * pairs
            scratch = [pltpu.VMEM((NDIST, columns), F32)]
        extra = [] if total is None else [total]
        return pl.pallas_call(
            functools.partial(finish_kernel, r, pairs, len(window), total is not None),
            out_shape=(shaped(half, bs), shaped(half, bs)) + sums,
            in_specs=[SMEM_SPEC] + [VMEM_SPEC] * (len(window) + 6 + len(extra)),
            out_specs=(VMEM_SPEC,) * (2 + len(sums)),
            scratch_shapes=scratch,
            compiler_params=params(8),
            cost_estimate=cost(6 * 3 * half * bs * bs, 16 * bs * bs),
            name="finish",
        )(ids, *window, mh, ml, own_w, oth_w, own_d, oth_d, *extra)

    keeps, gots = {}, {}
    values = []
    total = None
    near = far_now = far_next = None
    steps = count + PIECES - 1
    for step in range(steps):
        lead = count - 1 - step
        first = max(lead, 0) // pairs
        last = min(lead + PIECES - 1, count - 1) // pairs
        taken = [x for x in (far_now, near) if x is not None]
        operands = []
        for r in range(first, last + 1):
            gh, gl, _, _, rt = fixed[r]
            operands += [gh, gl, rt]
        near_out, far_out, v = pl.pallas_call(
            functools.partial(
                step_kernel, lead, count, pairs, last * pairs,
                near is not None, far_now is not None,
            ),
            out_shape=(shaped(width, 2 * bs),) * 3,
            in_specs=[SMEM_SPEC] + [VMEM_SPEC] * (len(taken) + len(operands)),
            out_specs=(VMEM_SPEC,) * 3,
            compiler_params=params(8),
            cost_estimate=cost(6 * width * 8 * bs * bs, 10 * width * bs * 4),
            name="hop_terms",
        )(ids, *taken, *operands)
        values.append(v)
        near = pass_on(near_out, 1) if step + 1 < steps else None
        far_now = far_next
        far_next = pass_on(far_out, 2) if step + 2 < steps else None
        if lead <= 0 or (lead + PIECES - 1) % pairs != 0:
            continue
        r = (lead + PIECES - 1) // pairs
        if r < rows_here:
            keeps[r], give, total = finish(r, values, total)
            gots[r] = swap(give)

    keeps[0], give, *parts = finish(0, values, total)
    parts = [parts[0]] + [pass_on(parts[by], -by) for by in range(1, pairs)]
    gots[0] = swap(give)
    mine, theirs = pl.pallas_call(
        add_kernel,
        out_shape=(shaped(NDIST // n, columns),) * 2,
        in_specs=[SMEM_SPEC] + [VMEM_SPEC] * pairs,
        out_specs=(VMEM_SPEC,) * 2,
        compiler_params=params(4),
        name="district_add",
    )(ids, *parts)
    got = swap(theirs)
    order = range(rows_here)
    field = pl.pallas_call(
        functools.partial(field_kernel, rows_here),
        out_shape=shaped(rows_here, 1, bs, columns),
        in_specs=[SMEM_SPEC] + [VMEM_SPEC] * (2 * rows_here),
        out_specs=VMEM_SPEC,
        compiler_params=params(4),
        cost_estimate=cost(0, 8 * rows_here * bs * columns),
        name="field",
    )(ids, *[keeps[r] for r in order], *[gots[r] for r in order])
    mean = pl.pallas_call(
        mean_kernel,
        out_shape=shaped(NDIST // n, columns),
        in_specs=[SMEM_SPEC] + [VMEM_SPEC] * 2,
        out_specs=VMEM_SPEC,
        compiler_params=params(4),
        name="district_mean",
    )(ids, mine, got)
    return field, mean


def solution(mesh):
    placed = (
        P(None, "blk", None, "sims"),
        P(None, "blk", None, None, None),
        P(None, "blk", None),
        P(None, "blk", None, None),
        P(None, "blk", None),
        P(None, "blk", None),
    )
    return jax.shard_map(
        body,
        mesh=mesh,
        in_specs=placed,
        out_specs=(P(None, "blk", None, "sims"), P("blk", "sims")),
        check_vma=False,
    )
```

```python
import functools

import jax
import jax.numpy as jnp
from jax import lax
from jax.experimental import pallas as pl
from jax.experimental.pallas import tpu as pltpu
from jax.sharding import PartitionSpec as P

NDIST = 256
F32 = jnp.float32
B16 = jnp.bfloat16
SMEM_SPEC = pl.BlockSpec(memory_space=pltpu.SMEM)
VMEM_SPEC = pl.BlockSpec(memory_space=pltpu.VMEM)
HBM_SPEC = pl.BlockSpec(memory_space=pltpu.HBM)


def params(mib):
    return pltpu.CompilerParams(vmem_limit_bytes=mib * 1024 * 1024)


def cost(flops, moved):
    return pl.CostEstimate(flops=flops, bytes_accessed=moved, transcendentals=0)


def shaped(*shape, dtype=F32):
    return jax.ShapeDtypeStruct(shape, dtype)


def halves(x):
    hi = x.astype(B16)
    lo = (x - hi.astype(F32)).astype(B16)
    return hi, lo


def dot(a, b):
    return jnp.dot(a, b, preferred_element_type=F32)


def dot3(x, y):
    rows = x[0].shape[0]
    both = dot(jnp.concatenate([x[0], x[1]], axis=0), y[0])
    return both[:rows] + both[rows:] + dot(x[0], y[1])


def packed_places(slots, bs, columns):
    rhs_at = (slots + 1) * bs
    col_at = rhs_at + columns
    turnout_at = col_at + 8 * slots
    district_at = turnout_at + 8
    return rhs_at, col_at, turnout_at, district_at, district_at + 8


def pack_kernel(r, cols, turnout, district, l_ref, d_ref, r_ref, out, held, sems):
    slots, bs = l_ref.shape[2], l_ref.shape[3]
    columns = r_ref.shape[3]
    rhs_at, col_at, turnout_at, district_at, _ = packed_places(slots, bs, columns)
    copies = [pltpu.make_async_copy(r_ref.at[r, 0], held, sems.at[slots + 1])]
    for k in range(slots):
        copies.append(
            pltpu.make_async_copy(l_ref.at[r, 0, k], out.at[pl.ds(k * bs, bs)], sems.at[k])
        )
    copies.append(
        pltpu.make_async_copy(d_ref.at[r, 0], out.at[pl.ds(slots * bs, bs)], sems.at[slots])
    )
    for copy in copies:
        copy.start()
    for k in range(slots):
        at = col_at + 8 * k
        out[at : at + 8] = jnp.full((8, bs), cols[r, k].astype(F32))
    out[turnout_at : turnout_at + 8] = jnp.broadcast_to(turnout[r], (8, bs))
    out[district_at : district_at + 8] = jnp.broadcast_to(
        district[r].astype(F32), (8, bs)
    )
    copies[0].wait()
    out[rhs_at:col_at] = held[...].T
    for copy in copies[1:]:
        copy.wait()


def setup_kernel(r, n, slots, columns, ids, own, oth, gh, gl, mh, ml, rt):
    is_a = ids[0] == 1
    bs = own.shape[1]
    half = columns // 2
    rhs_at, col_at, _, _, _ = packed_places(slots, bs, columns)
    row_b = r * n + 2 * ids[1]
    row_a = row_b + 1

    def upper(at, size):
        return jnp.where(is_a, own[at : at + size], oth[at : at + size])

    def lower(at, size):
        return jnp.where(is_a, oth[at : at + size], own[at : at + size])

    def at_distance(side, row, d):
        found = jnp.zeros((bs, bs), F32)
        column = (row - d).astype(F32)
        for k in range(1, slots):
            col = side(col_at + 8 * k, 1)
            here = (col == column) & (col >= 0.0)
            found = jnp.where(here, side(k * bs, bs), found)
        return halves(found)

    da, db = halves(upper(slots * bs, bs)), halves(lower(slots * bs, bs))
    la1 = halves(upper(0, bs))
    lb1 = halves(jnp.where(lower(col_at, 1) >= 0.0, lower(0, bs), 0.0))
    la2, la3, la4 = (at_distance(upper, row_a, d) for d in (2, 3, 4))
    lb2, lb3, lb4 = (at_distance(lower, row_b, d) for d in (2, 3, 4))
    for place, pair in enumerate((da, db, la1, la4, lb3, lb4)):
        mh[place] = pair[0]
        ml[place] = pair[1]

    def put(i, j, value):
        hi, lo = halves(value)
        gh[i * bs : (i + 1) * bs, j * bs : (j + 1) * bs] = hi
        gl[i * bs : (i + 1) * bs, j * bs : (j + 1) * bs] = lo

    w = halves(dot3(da, la1))
    for j, (la, lb) in enumerate(((la2, lb1), (la3, lb2))):
        from_b = dot3(db, lb)
        put(1, j, from_b)
        put(0, j, dot3(da, la) - dot3(w, halves(from_b)))
    ra, rb = upper(rhs_at, columns), lower(rhs_at, columns)
    rt[:, :bs] = jnp.where(is_a, ra[half:], ra[:half])
    rt[:, bs:] = jnp.where(is_a, rb[half:], rb[:half])


def near_kernel(chip, ids, r_ref, *refs):
    taken = refs[:-4]
    gh, gl, near, v_out = refs[-4:]

    @pl.when(ids[1] == chip)
    def _():
        v = r_ref[...]
        for x in taken:
            v = v - x[...]
        v_out[...] = v
        near[...] = dot3(halves(v), (gh[...], gl[...]))


def far_kernel(chip, slots, pairs, has_far, is_last, ids, v_ref, mh, ml, own, oth, *refs):
    keep_in, give_in, total_in, keep, give, total = refs[:6]
    refs = list(refs[6:])
    far = refs.pop(0) if has_far else None
    bs = mh.shape[1]
    half = keep.shape[0]
    _, _, turnout_at, district_at, _ = packed_places(slots, bs, 2 * half)
    is_a = ids[0] == 1

    def m(k):
        return mh[k], ml[k]

    @pl.when(ids[1] == chip)
    def _():
        xa = dot3(halves(v_ref[:, :bs]), m(0))
        xah = halves(xa)
        xb = dot3(halves(v_ref[:, bs:] - dot3(xah, m(2))), m(1))
        if has_far:
            xbh = halves(xb)
            far[:, :bs] = dot3(xah, m(3)) + dot3(xbh, m(4))
            far[:, bs:] = dot3(xbh, m(5))
        kept, given = jnp.where(is_a, xa, xb), jnp.where(is_a, xb, xa)
        keep[...] = kept
        give[...] = given
        names = lax.broadcasted_iota(jnp.int32, (NDIST, bs), 0).astype(F32)
        sums = total_in[...]
        for x, pack in ((kept, own), (given, oth)):
            weight = pack[turnout_at : turnout_at + 1]
            member = names == pack[district_at : district_at + 1]
            member = member.astype(F32).astype(B16)
            terms = jnp.concatenate(
                [x * weight, jnp.broadcast_to(weight, (half, bs))], axis=0
            )
            for part in halves(terms):
                sums = sums + lax.dot_general(
                    member, part, (((1,), (1,)), ((), ())), preferred_element_type=F32
                )
        total[...] = sums

    @pl.when(ids[1] != chip)
    def _():
        keep[...] = keep_in[...]
        give[...] = give_in[...]
        total[...] = total_in[...]

    if is_last:
        rows = NDIST // pairs
        for by, part in enumerate(refs):
            to = lax.rem(ids[1] + by, pairs)
            part[...] = total[pl.ds(pl.multiple_of(to * rows, rows), rows), :]


def add_kernel(ids, *refs):
    mine, theirs = refs[-2:]
    total = refs[0][...]
    for part in refs[1:-2]:
        total = total + part[...]
    rows = mine.shape[0]
    is_a = ids[0] == 1
    mine[...] = jnp.where(is_a, total[rows:], total[:rows])
    theirs[...] = jnp.where(is_a, total[:rows], total[rows:])


def mean_kernel(ids, mine, got, out):
    half = out.shape[1] // 2
    own, oth = (x[:, :half] / x[:, half:] for x in (mine, got))
    is_a = ids[0] == 1
    out[...] = jnp.concatenate(
        [jnp.where(is_a, oth, own), jnp.where(is_a, own, oth)], axis=1
    )


def field_kernel(rows_here, ids, *refs):
    keeps = refs[:rows_here]
    gots = refs[rows_here : 2 * rows_here]
    out = refs[2 * rows_here]
    is_a = ids[0] == 1
    for r in range(rows_here):
        top = jnp.where(is_a, gots[r][...], keeps[r][...])
        bottom = jnp.where(is_a, keeps[r][...], gots[r][...])
        out[r, 0] = jnp.concatenate([top, bottom], axis=0).T


def body(rhs, lower_blocks, col_index, diag_inverse, turnout, district_of):
    n = lax.axis_size("blk")
    p = lax.axis_index("blk").astype(jnp.int32)
    pairs = n // 2
    ids = jnp.stack([lax.rem(p, 2), lax.div(p, 2)])
    rows_here, _, bs, columns = rhs.shape
    slots = lower_blocks.shape[2]
    half = columns // 2
    count = rows_here * pairs
    packed_rows = packed_places(slots, bs, columns)[-1]

    def swap(x):
        return lax.ppermute(x, "blk", [(i, i ^ 1) for i in range(n)])

    def shift(x, by):
        return lax.ppermute(x, "blk", [(i, (i + 2 * by) % n) for i in range(n)])

    def pass_on(x, chip, by):
        perm = [(2 * chip + c, (2 * (chip - by) + c) % n) for c in range(2)]
        return lax.ppermute(x, "blk", perm)

    def pack(r):
        return pl.pallas_call(
            functools.partial(pack_kernel, r),
            out_shape=shaped(packed_rows, bs),
            in_specs=[SMEM_SPEC, VMEM_SPEC, VMEM_SPEC] + [HBM_SPEC] * 3,
            out_specs=VMEM_SPEC,
            scratch_shapes=[
                pltpu.VMEM((bs, columns), F32),
                pltpu.SemaphoreType.DMA((slots + 2,)),
            ],
            compiler_params=params(4),
            cost_estimate=cost(0, 8 * packed_rows * bs),
            name="pack",
        )(col_index[:, 0], turnout, district_of, lower_blocks, diag_inverse, rhs)

    def setup(r, own, oth):
        return pl.pallas_call(
            functools.partial(setup_kernel, r, n, slots, columns),
            out_shape=(
                shaped(2 * bs, 2 * bs, dtype=B16),
                shaped(2 * bs, 2 * bs, dtype=B16),
                shaped(6, bs, bs, dtype=B16),
                shaped(6, bs, bs, dtype=B16),
                shaped(half, 2 * bs),
            ),
            in_specs=[SMEM_SPEC] + [VMEM_SPEC] * 2,
            out_specs=(VMEM_SPEC,) * 5,
            compiler_params=params(10),
            cost_estimate=cost(14 * 3 * bs**3, 24 * bs * bs * 4),
            name="pair_setup",
        )(ids, own, oth)

    packs = {}
    own = pack(rows_here - 1)
    packs[rows_here - 1] = (own, swap(own))
    fixed = {rows_here - 1: setup(rows_here - 1, *packs[rows_here - 1])}

    keeps, gots = {}, {}
    keep = give = jnp.zeros((half, bs), F32)
    total = jnp.zeros((NDIST, columns), F32)
    near = far_now = far_next = None
    for step in range(count):
        k = count - 1 - step
        r, chip = k // pairs, k % pairs
        gh, gl, mh, ml, rt = fixed[r]
        taken = [x for x in (far_now, near) if x is not None]
        near_out, v = pl.pallas_call(
            functools.partial(near_kernel, chip),
            out_shape=(shaped(half, 2 * bs), shaped(half, 2 * bs)),
            in_specs=[SMEM_SPEC] + [VMEM_SPEC] * (3 + len(taken)),
            out_specs=(VMEM_SPEC,) * 2,
            compiler_params=params(4),
            cost_estimate=cost(6 * half * 4 * bs * bs, 6 * half * bs * 4),
            name="near_terms",
        )(ids, rt, *taken, gh, gl)
        near = pass_on(near_out, chip, 1) if k > 0 else None
        if chip == pairs - 1 and r > 0:
            own, _ = lax.optimization_barrier((pack(r - 1), near_out))
            packs[r - 1] = (own, swap(own))
            fixed[r - 1] = setup(r - 1, *packs[r - 1])
        has_far, is_last = k >= 2, k == 0
        outs = (shaped(half, bs), shaped(half, bs), shaped(NDIST, columns))
        if has_far:
            outs += (shaped(half, 2 * bs),)
        if is_last:
            outs += (shaped(NDIST // pairs, columns),) * pairs
        keep, give, total, *more = pl.pallas_call(
            functools.partial(far_kernel, chip, slots, pairs, has_far, is_last),
            out_shape=outs,
            in_specs=[SMEM_SPEC] + [VMEM_SPEC] * 8,
            out_specs=(VMEM_SPEC,) * len(outs),
            compiler_params=params(6),
            cost_estimate=cost(6 * half * 6 * bs * bs, 8 * half * bs * 4),
            name="far_terms",
        )(ids, v, mh, ml, *packs[r], keep, give, total)
        far_now = far_next
        far_next = pass_on(more[0], chip, 2) if has_far else None
        if chip == 0:
            keeps[r] = keep
            gots[r] = swap(give)

    parts = [more[0]] + [shift(more[by], by) for by in range(1, pairs)]
    mine, theirs = pl.pallas_call(
        add_kernel,
        out_shape=(shaped(NDIST // n, columns),) * 2,
        in_specs=[SMEM_SPEC] + [VMEM_SPEC] * pairs,
        out_specs=(VMEM_SPEC,) * 2,
        compiler_params=params(4),
        name="district_add",
    )(ids, *parts)
    got = swap(theirs)
    order = range(rows_here)
    field = pl.pallas_call(
        functools.partial(field_kernel, rows_here),
        out_shape=shaped(rows_here, 1, bs, columns),
        in_specs=[SMEM_SPEC] + [VMEM_SPEC] * (2 * rows_here),
        out_specs=VMEM_SPEC,
        compiler_params=params(4),
        cost_estimate=cost(0, 8 * rows_here * bs * columns),
        name="field",
    )(ids, *[keeps[r] for r in order], *[gots[r] for r in order])
    mean = pl.pallas_call(
        mean_kernel,
        out_shape=shaped(NDIST // n, columns),
        in_specs=[SMEM_SPEC] + [VMEM_SPEC] * 2,
        out_specs=VMEM_SPEC,
        compiler_params=params(4),
        name="district_mean",
    )(ids, mine, got)
    return field, mean


def solution(mesh):
    placed = (
        P(None, "blk", None, "sims"),
        P(None, "blk", None, None, None),
        P(None, "blk", None),
        P(None, "blk", None, None),
        P(None, "blk", None),
        P(None, "blk", None),
    )
    return jax.shard_map(
        body,
        mesh=mesh,
        in_specs=placed,
        out_specs=(P(None, "blk", None, "sims"), P("blk", "sims")),
        check_vma=False,
    )
```

```python
import functools

import jax
import jax.numpy as jnp
from jax import lax
from jax.experimental import pallas as pl
from jax.experimental.pallas import tpu as pltpu
from jax.sharding import PartitionSpec as P

NDIST = 256
F32 = jnp.float32
B16 = jnp.bfloat16
SMEM_SPEC = pl.BlockSpec(memory_space=pltpu.SMEM)
VMEM_SPEC = pl.BlockSpec(memory_space=pltpu.VMEM)
HBM_SPEC = pl.BlockSpec(memory_space=pltpu.HBM)


def params(mib):
    return pltpu.CompilerParams(vmem_limit_bytes=mib * 1024 * 1024)


def cost(flops, moved):
    return pl.CostEstimate(flops=flops, bytes_accessed=moved, transcendentals=0)


def shaped(*shape, dtype=F32):
    return jax.ShapeDtypeStruct(shape, dtype)


def halves(x):
    hi = x.astype(B16)
    lo = (x - hi.astype(F32)).astype(B16)
    return hi, lo


def dot(a, b):
    return jnp.dot(a, b, preferred_element_type=F32)


def dot3(x, y):
    rows = x[0].shape[0]
    both = dot(jnp.concatenate([x[0], x[1]], axis=0), y[0])
    return both[:rows] + both[rows:] + dot(x[0], y[1])


def packed_places(slots, bs, columns):
    rhs_at = (slots + 1) * bs
    col_at = rhs_at + columns
    turnout_at = col_at + 8 * slots
    district_at = turnout_at + 8
    return rhs_at, col_at, turnout_at, district_at, district_at + 8


def chip_now():
    return lax.div(lax.axis_index("blk").astype(jnp.int32), 2)


def upper_here():
    return lax.rem(lax.axis_index("blk").astype(jnp.int32), 2) == 1


def pack_kernel(rows, cols, turnout, district, l_ref, d_ref, r_ref, *refs):
    outs = refs[: len(rows)]
    held, sems = refs[len(rows) :]
    slots, bs = l_ref.shape[2], l_ref.shape[3]
    columns = r_ref.shape[3]
    rhs_at, col_at, turnout_at, district_at, _ = packed_places(slots, bs, columns)
    copies = []

    def copy(source, target):
        copies.append(pltpu.make_async_copy(source, target, sems.at[len(copies)]))
        copies[-1].start()

    for i, r in enumerate(rows):
        copy(r_ref.at[r, 0], held.at[i])
    for out, r in zip(outs, rows):
        for k in range(slots):
            copy(l_ref.at[r, 0, k], out.at[pl.ds(k * bs, bs)])
        copy(d_ref.at[r, 0], out.at[pl.ds(slots * bs, bs)])
    for out, r in zip(outs, rows):
        for k in range(slots):
            at = col_at + 8 * k
            out[at : at + 8] = jnp.full((8, bs), cols[k, 0, r].astype(F32))
        out[turnout_at : turnout_at + 8] = jnp.broadcast_to(turnout[r], (8, bs))
        out[district_at : district_at + 8] = jnp.broadcast_to(
            district[r].astype(F32), (8, bs)
        )
    for i, out in enumerate(outs):
        copies[i].wait()
        out[rhs_at:col_at] = held[i].T
    for started in copies[len(rows) :]:
        started.wait()


def put(high, low, i, j, value):
    bs = value.shape[0]
    hi, lo = halves(value)
    high[i * bs : (i + 1) * bs, j * bs : (j + 1) * bs] = hi
    low[i * bs : (i + 1) * bs, j * bs : (j + 1) * bs] = lo


def blocks_of(r, n, slots, columns, own, oth):
    is_a = upper_here()
    bs = own.shape[1]
    _, col_at, _, _, _ = packed_places(slots, bs, columns)
    row_b = r * n + 2 * chip_now()
    row_a = row_b + 1

    def upper(at, size):
        return jnp.where(is_a, own[at : at + size], oth[at : at + size])

    def lower(at, size):
        return jnp.where(is_a, oth[at : at + size], own[at : at + size])

    def at_distance(side, row, d):
        found = jnp.zeros((bs, bs), F32)
        column = (row - d).astype(F32)
        for k in range(1, slots):
            col = side(col_at + 8 * k, 1)
            here = (col == column) & (col >= 0.0)
            found = jnp.where(here, side(k * bs, bs), found)
        return halves(found)

    return upper, lower, lambda d: at_distance(upper, row_a, d), lambda d: at_distance(lower, row_b, d)


def near_setup_kernel(r, n, slots, columns, own, oth, gh, gl, mh, ml, rt):
    bs = own.shape[1]
    half = columns // 2
    rhs_at, col_at, _, _, _ = packed_places(slots, bs, columns)
    upper, lower, upper_at, lower_at = blocks_of(r, n, slots, columns, own, oth)
    is_a = upper_here()
    da, db = halves(upper(slots * bs, bs)), halves(lower(slots * bs, bs))
    la1 = halves(upper(0, bs))
    lb1 = halves(jnp.where(lower(col_at, 1) >= 0.0, lower(0, bs), 0.0))
    w = dot3(da, la1)
    wh = halves(w)
    for place, pair in enumerate((da, db, la1, wh)):
        mh[place] = pair[0]
        ml[place] = pair[1]
    for j, (la, lb) in enumerate(((upper_at(2), lb1), (upper_at(3), lower_at(2)))):
        from_b = dot3(db, lb)
        put(gh, gl, 1, j, from_b)
        put(gh, gl, 0, j, dot3(da, la) - dot3(wh, halves(from_b)))
    ra, rb = upper(rhs_at, columns), lower(rhs_at, columns)
    rt[:, :bs] = jnp.where(is_a, ra[half:], ra[:half])
    rt[:, bs:] = jnp.where(is_a, rb[half:], rb[:half])


def far_setup_kernel(r, n, slots, columns, own, oth, mh, ml, fh, fl):
    _, _, upper_at, lower_at = blocks_of(r, n, slots, columns, own, oth)
    da, db, w = ((mh[k], ml[k]) for k in (0, 1, 3))
    for j, lb in enumerate((lower_at(3), lower_at(4))):
        from_b = dot3(db, lb)
        put(fh, fl, 1, j, from_b)
        from_a = -dot3(w, halves(from_b))
        if j == 0:
            from_a = from_a + dot3(da, upper_at(4))
        put(fh, fl, 0, j, from_a)


def place_of(lead, pairs, pieces):
    ahead = lax.rem(chip_now() - lead % pairs + pairs, pairs)
    piece = jnp.minimum(lax.div(ahead, 2), pieces - 1)
    return piece, lead + ahead


def choose(choices, pair, split, run):
    if len(choices) == 1:
        run(*choices[0])
        return

    @pl.when(pair < split)
    def _():
        run(*choices[0])

    @pl.when(pair >= split)
    def _():
        run(*choices[1])


def near_kernel(lead, pairs, pieces, split, received, has_near, *refs):
    taken = refs[:received]
    outs = refs[-2:] if has_near else refs[-1:]
    refs = refs[received : -len(outs)]
    each = 3 if has_near else 1
    choices = [refs[i : i + each] for i in range(0, len(refs), each)]
    v_out = outs[0]
    width = v_out.shape[0]
    piece, pair = place_of(lead, pairs, pieces)
    rows = pl.ds(pl.multiple_of(piece * width, width), width)

    def run(rt, gh=None, gl=None):
        v = rt[rows, :]
        for x in taken:
            v = v - x[...]
        v_out[...] = v
        if has_near:
            outs[1][...] = dot3(halves(v), (gh[...], gl[...]))

    choose(choices, pair, split, run)


def far_kernel(lead, pairs, pieces, split, v_ref, *refs):
    out = refs[-1]
    refs = refs[:-1]
    _, pair = place_of(lead, pairs, pieces)

    def run(fh, fl):
        out[...] = dot3(halves(v_ref[...]), (fh[...], fl[...]))

    choose([refs[i : i + 2] for i in range(0, len(refs), 2)], pair, split, run)


def finish_kernel(slots, pairs, pieces, window, has_total, is_last, *refs):
    values = refs[:window]
    mh, ml, own, oth = refs[window : window + 4]
    refs = refs[window + 4 :]
    start = refs[0][...] if has_total else None
    keep, give, *outs = refs[1:] if has_total else refs
    chip, is_a = chip_now(), upper_here()
    bs = mh.shape[1]
    half = keep.shape[0]
    _, _, turnout_at, district_at, _ = packed_places(slots, bs, 2 * half)
    parts = []
    for m in range(pieces):
        v = values[pairs - 1 + 2 * m][...]
        for q in range(1, pairs):
            v = jnp.where(chip == q, values[pairs - 1 - q + 2 * m][...], v)
        parts.append(v)
    v = jnp.concatenate(parts, axis=0)

    def m(k):
        return mh[k], ml[k]

    xa = dot3(halves(v[:, :bs]), m(0))
    xb = dot3(halves(v[:, bs:] - dot3(halves(xa), m(2))), m(1))
    kept, given = jnp.where(is_a, xa, xb), jnp.where(is_a, xb, xa)
    keep[...] = kept
    give[...] = given
    names = lax.broadcasted_iota(jnp.int32, (NDIST, bs), 0).astype(F32)
    sums = jnp.zeros((NDIST, 2 * half), F32) if start is None else start
    for x, pack in ((kept, own), (given, oth)):
        weight = pack[turnout_at : turnout_at + 1]
        member = names == pack[district_at : district_at + 1]
        member = member.astype(F32).astype(B16)
        terms = jnp.concatenate([x * weight, jnp.broadcast_to(weight, (half, bs))], axis=0)
        for part in halves(terms):
            sums = sums + lax.dot_general(
                member, part, (((1,), (1,)), ((), ())), preferred_element_type=F32
            )
    if not is_last:
        outs[0][...] = sums
        return
    held = outs.pop()
    held[...] = sums
    rows = NDIST // pairs
    for by, part in enumerate(outs):
        to = lax.rem(chip + by, pairs)
        part[...] = held[pl.ds(pl.multiple_of(to * rows, rows), rows), :]


def add_kernel(*refs):
    mine, theirs = refs[-2:]
    total = refs[0][...]
    for part in refs[1:-2]:
        total = total + part[...]
    rows = mine.shape[0]
    is_a = upper_here()
    mine[...] = jnp.where(is_a, total[rows:], total[:rows])
    theirs[...] = jnp.where(is_a, total[:rows], total[rows:])


def mean_kernel(mine, got, out):
    half = out.shape[1] // 2
    own, oth = (x[:, :half] / x[:, half:] for x in (mine, got))
    is_a = upper_here()
    out[...] = jnp.concatenate(
        [jnp.where(is_a, oth, own), jnp.where(is_a, own, oth)], axis=1
    )


def field_kernel(rows_here, *refs):
    keeps = refs[:rows_here]
    gots = refs[rows_here : 2 * rows_here]
    out = refs[2 * rows_here]
    is_a = upper_here()
    for r in range(rows_here):
        top = jnp.where(is_a, gots[r][...], keeps[r][...])
        bottom = jnp.where(is_a, keeps[r][...], gots[r][...])
        out[r, 0] = jnp.concatenate([top, bottom], axis=0).T


def body(rhs, lower_blocks, col_index, diag_inverse, turnout, district_of):
    n = lax.axis_size("blk")
    pairs = n // 2
    pieces = max(pairs // 2, 1)
    rows_here, _, bs, columns = rhs.shape
    slots = lower_blocks.shape[2]
    half = columns // 2
    width = half // pieces
    count = rows_here * pairs
    packed_rows = packed_places(slots, bs, columns)[-1]
    wide = shaped(width, 2 * bs)
    square = shaped(2 * bs, 2 * bs, dtype=B16)

    def call(kernel, name, outs, operands, mib, flops=0, moved=0, **more):
        several = isinstance(outs, tuple)
        return pl.pallas_call(
            kernel,
            out_shape=outs,
            in_specs=more.pop("in_specs", [VMEM_SPEC] * len(operands)),
            out_specs=(VMEM_SPEC,) * len(outs) if several else VMEM_SPEC,
            compiler_params=params(mib),
            cost_estimate=cost(flops, moved),
            name=name,
            **more,
        )(*operands)

    def swap(x):
        return lax.ppermute(x, "blk", [(i, i ^ 1) for i in range(n)])

    def shift(x, by):
        return lax.ppermute(x, "blk", [(i, (i + 2 * by) % n) for i in range(n)])

    def pass_on(x, lead, by):
        perm = []
        for k in range(lead, lead + 2 * pieces, 2):
            if by <= k < count:
                sender, target = k % pairs, (k - by) % pairs
                perm += [(2 * sender + c, 2 * target + c) for c in range(2)]
        return lax.ppermute(x, "blk", perm)

    def pack(rows):
        return call(
            functools.partial(pack_kernel, rows),
            "pack",
            (shaped(packed_rows, bs),) * len(rows),
            (jnp.transpose(col_index, (2, 1, 0)), turnout, district_of, lower_blocks, diag_inverse, rhs),
            56,
            moved=8 * packed_rows * bs * len(rows),
            in_specs=[SMEM_SPEC, VMEM_SPEC, VMEM_SPEC] + [HBM_SPEC] * 3,
            scratch_shapes=[
                pltpu.VMEM((len(rows), bs, columns), F32),
                pltpu.SemaphoreType.DMA((len(rows) * (slots + 2),)),
            ],
        )

    def setup(r):
        args = (r, n, slots, columns)
        held = shaped(4, bs, bs, dtype=B16)
        gh, gl, mh, ml, rt = call(
            functools.partial(near_setup_kernel, *args),
            "near_setup",
            (square, square, held, held, shaped(half, 2 * bs)),
            packs[r],
            10,
            14 * 3 * bs**3,
            24 * bs * bs * 4,
        )
        fh, fl = call(
            functools.partial(far_setup_kernel, *args),
            "far_setup",
            (square, square),
            (*packs[r], mh, ml),
            10,
            10 * 3 * bs**3,
            24 * bs * bs * 4,
        )
        return gh, gl, mh, ml, rt, fh, fl

    def finish(r, values, total):
        first = count - 1 - (r * pairs + pairs - 1)
        window = values[first : first + pairs + 2 * (pieces - 1)]
        is_last = r == 0
        outs = (shaped(half, bs), shaped(half, bs))
        outs += (shaped(NDIST // pairs, columns),) * pairs if is_last else (shaped(NDIST, columns),)
        extra = () if total is None else (total,)
        return call(
            functools.partial(
                finish_kernel, slots, pairs, pieces, len(window), total is not None, is_last
            ),
            "finish",
            outs,
            (*window, *fixed[r][2:4], *packs[r], *extra),
            8,
            6 * 3 * half * bs * bs,
            16 * bs * bs,
            scratch_shapes=[pltpu.VMEM((NDIST, columns), F32)] if is_last else [],
        )

    top = rows_here - 1
    packs, fixed = {}, {}
    (own,) = pack((top,))
    packs[top] = (own, swap(own))
    packed = pack(tuple(range(top))) if top else ()
    fixed[top] = setup(top)

    keeps, gots = {}, {}
    values = []
    total = near = far_now = far_next = None
    steps = count + 2 * (pieces - 1)
    for step in range(steps):
        lead = count - 1 - step
        low = max(lead, 0) // pairs
        high = min(lead + 2 * (pieces - 1), count - 1) // pairs
        rows = range(low, high + 1)
        taken = [x for x in (far_now, near) if x is not None]
        has_near = step + 1 < steps
        has_far = step + 2 < steps
        operands = []
        for r in rows:
            gh, gl, _, _, rt, _, _ = fixed[r]
            operands += [rt, gh, gl] if has_near else [rt]
        place = (lead, pairs, pieces, high * pairs)
        v, *near_out = call(
            functools.partial(near_kernel, *place, len(taken), has_near),
            "near_terms",
            (wide, wide) if has_near else (wide,),
            (*taken, *operands),
            4,
            6 * width * 4 * bs * bs,
            6 * width * bs * 4,
        )
        values.append(v)
        near = pass_on(near_out[0], lead, 1) if has_near else None
        if has_near and (lead + 1) % pairs == 0 and 0 < lead // pairs:
            r = lead // pairs - 1
            own, _ = lax.optimization_barrier((packed[r], near_out[0]))
            packs[r] = (own, swap(own))
            fixed[r] = setup(r)
        far_now, far_next = far_next, None
        if has_far:
            operands = [x for r in rows for x in fixed[r][5:]]
            far_out = call(
                functools.partial(far_kernel, *place),
                "far_terms",
                wide,
                (v, *operands),
                4,
                6 * width * 4 * bs * bs,
                6 * width * bs * 4,
            )
            far_next = pass_on(far_out, lead, 2)
        done = lead + 2 * (pieces - 1)
        if done % pairs == 0 and 0 < done // pairs <= top:
            r = done // pairs
            keeps[r], give, total = finish(r, values, total)
            gots[r] = swap(give)
            near, total = lax.optimization_barrier((near, total))

    keeps[0], give, *parts = finish(0, values, total)
    gots[0] = swap(give)
    parts = [parts[0]] + [shift(parts[by], by) for by in range(1, pairs)]
    order = range(rows_here)
    field = call(
        functools.partial(field_kernel, rows_here),
        "field",
        shaped(rows_here, 1, bs, columns),
        (*[keeps[r] for r in order], *[gots[r] for r in order]),
        4,
        0,
        8 * rows_here * bs * columns,
    )
    parts, field = lax.optimization_barrier((parts, field))
    held = shaped(NDIST // n, columns)
    mine, theirs = call(add_kernel, "district_add", (held, held), tuple(parts), 4)
    mean = call(mean_kernel, "district_mean", held, (mine, swap(theirs)), 4)
    return field, mean


def solution(mesh):
    placed = (
        P(None, "blk", None, "sims"),
        P(None, "blk", None, None, None),
        P(None, "blk", None),
        P(None, "blk", None, None),
        P(None, "blk", None),
        P(None, "blk", None),
    )
    return jax.shard_map(
        body,
        mesh=mesh,
        in_specs=placed,
        out_specs=(P(None, "blk", None, "sims"), P("blk", "sims")),
        check_vma=False,
    )
```

```python
import functools

import jax
import jax.numpy as jnp
from jax import lax
from jax.experimental import pallas as pl
from jax.experimental.pallas import tpu as pltpu
from jax.sharding import PartitionSpec as P

NDIST = 256
F32 = jnp.float32
B16 = jnp.bfloat16
SMEM_SPEC = pl.BlockSpec(memory_space=pltpu.SMEM)
VMEM_SPEC = pl.BlockSpec(memory_space=pltpu.VMEM)
HBM_SPEC = pl.BlockSpec(memory_space=pltpu.HBM)


def params(mib):
    return pltpu.CompilerParams(vmem_limit_bytes=mib * 1024 * 1024)


def cost(flops, moved):
    return pl.CostEstimate(flops=flops, bytes_accessed=moved, transcendentals=0)


def shaped(*shape, dtype=F32):
    return jax.ShapeDtypeStruct(shape, dtype)


def halves(x):
    hi = x.astype(B16)
    lo = (x - hi.astype(F32)).astype(B16)
    return hi, lo


def dot(a, b):
    return jnp.dot(a, b, preferred_element_type=F32)


def dot3(x, y):
    rows = x[0].shape[0]
    both = dot(jnp.concatenate([x[0], x[1]], axis=0), y[0])
    return both[:rows] + both[rows:] + dot(x[0], y[1])


def packed_places(slots, bs, columns):
    rhs_at = (slots + 1) * bs
    col_at = rhs_at + columns
    turnout_at = col_at + 8 * slots
    district_at = turnout_at + 8
    return rhs_at, col_at, turnout_at, district_at, district_at + 8


def chip_now():
    return lax.div(lax.axis_index("blk").astype(jnp.int32), 2)


def upper_here():
    return lax.rem(lax.axis_index("blk").astype(jnp.int32), 2) == 1


def pack_kernel(rows, cols, turnout, district, l_ref, d_ref, r_ref, *refs):
    outs = refs[: len(rows)]
    held, tail, sems = refs[len(rows) :]
    slots, bs = l_ref.shape[2], l_ref.shape[3]
    columns = r_ref.shape[3]
    rhs_at, col_at, turnout_at, district_at, end = packed_places(slots, bs, columns)
    copies = []

    def copy(source, target):
        copies.append(pltpu.make_async_copy(source, target, sems.at[len(copies)]))
        copies[-1].start()

    for i, r in enumerate(rows):
        copy(r_ref.at[r, 0], held.at[i])
    for out, r in zip(outs, rows):
        for k in range(slots):
            copy(l_ref.at[r, 0, k], out.at[pl.ds(k * bs, bs)])
        copy(d_ref.at[r, 0], out.at[pl.ds(slots * bs, bs)])
    for i, r in enumerate(rows):
        for k in range(slots):
            at = col_at - rhs_at + 8 * k
            tail[i, at : at + 8] = jnp.full((8, bs), cols[k, 0, r].astype(F32))
        at = turnout_at - rhs_at
        tail[i, at : at + 8] = jnp.broadcast_to(turnout[r], (8, bs))
        at = district_at - rhs_at
        tail[i, at : at + 8] = jnp.broadcast_to(district[r].astype(F32), (8, bs))
    for i, out in enumerate(outs):
        copies[i].wait()
        tail[i, :columns] = held[i].T
        copy(tail.at[i], out.at[pl.ds(rhs_at, end - rhs_at)])
    for started in copies[len(rows) :]:
        started.wait()


def put(high, low, i, j, value):
    bs = value.shape[0]
    hi, lo = halves(value)
    high[i * bs : (i + 1) * bs, j * bs : (j + 1) * bs] = hi
    low[i * bs : (i + 1) * bs, j * bs : (j + 1) * bs] = lo


def blocks_of(r, n, slots, columns, own, oth):
    is_a = upper_here()
    bs = own.shape[1]
    _, col_at, _, _, _ = packed_places(slots, bs, columns)
    row_b = r * n + 2 * chip_now()
    row_a = row_b + 1

    def upper(at, size):
        return jnp.where(is_a, own[at : at + size], oth[at : at + size])

    def lower(at, size):
        return jnp.where(is_a, oth[at : at + size], own[at : at + size])

    def at_distance(side, row, d):
        found = jnp.zeros((bs, bs), F32)
        column = (row - d).astype(F32)
        for k in range(1, slots):
            col = side(col_at + 8 * k, 1)
            here = (col == column) & (col >= 0.0)
            found = jnp.where(here, side(k * bs, bs), found)
        return halves(found)

    return upper, lower, lambda d: at_distance(upper, row_a, d), lambda d: at_distance(lower, row_b, d)


def near_setup_kernel(r, n, slots, columns, own, oth, gh, gl, mh, ml, rt):
    bs = own.shape[1]
    half = columns // 2
    rhs_at, col_at, _, _, _ = packed_places(slots, bs, columns)
    upper, lower, upper_at, lower_at = blocks_of(r, n, slots, columns, own, oth)
    is_a = upper_here()
    da, db = halves(upper(slots * bs, bs)), halves(lower(slots * bs, bs))
    la1 = halves(upper(0, bs))
    lb1 = halves(jnp.where(lower(col_at, 1) >= 0.0, lower(0, bs), 0.0))
    w = dot3(da, la1)
    wh = halves(w)
    for place, pair in enumerate((da, db, la1, wh)):
        mh[place] = pair[0]
        ml[place] = pair[1]
    for j, (la, lb) in enumerate(((upper_at(2), lb1), (upper_at(3), lower_at(2)))):
        from_b = dot3(db, lb)
        put(gh, gl, 1, j, from_b)
        put(gh, gl, 0, j, dot3(da, la) - dot3(wh, halves(from_b)))
    ra, rb = upper(rhs_at, columns), lower(rhs_at, columns)
    rt[:, :bs] = jnp.where(is_a, ra[half:], ra[:half])
    rt[:, bs:] = jnp.where(is_a, rb[half:], rb[:half])


def far_setup_kernel(r, n, slots, columns, own, oth, mh, ml, fh, fl):
    _, _, upper_at, lower_at = blocks_of(r, n, slots, columns, own, oth)
    da, db, w = ((mh[k], ml[k]) for k in (0, 1, 3))
    for j, lb in enumerate((lower_at(3), lower_at(4))):
        from_b = dot3(db, lb)
        put(fh, fl, 1, j, from_b)
        from_a = -dot3(w, halves(from_b))
        if j == 0:
            from_a = from_a + dot3(da, upper_at(4))
        put(fh, fl, 0, j, from_a)


def place_of(lead, pairs, pieces):
    ahead = lax.rem(chip_now() - lead % pairs + pairs, pairs)
    piece = jnp.minimum(lax.div(ahead, 2), pieces - 1)
    return piece, lead + ahead


def choose(choices, pair, split, run):
    if len(choices) == 1:
        run(*choices[0])
        return

    @pl.when(pair < split)
    def _():
        run(*choices[0])

    @pl.when(pair >= split)
    def _():
        run(*choices[1])


def near_kernel(lead, pairs, pieces, split, received, has_near, *refs):
    taken = refs[:received]
    outs = refs[-2:] if has_near else refs[-1:]
    refs = refs[received : -len(outs)]
    each = 3 if has_near else 1
    choices = [refs[i : i + each] for i in range(0, len(refs), each)]
    v_out = outs[0]
    width = v_out.shape[0]
    piece, pair = place_of(lead, pairs, pieces)
    rows = pl.ds(pl.multiple_of(piece * width, width), width)

    def run(rt, gh=None, gl=None):
        v = rt[rows, :]
        for x in taken:
            v = v - x[...]
        v_out[...] = v
        if has_near:
            outs[1][...] = dot3(halves(v), (gh[...], gl[...]))

    choose(choices, pair, split, run)


def far_kernel(lead, pairs, pieces, split, v_ref, *refs):
    out = refs[-1]
    refs = refs[:-1]
    _, pair = place_of(lead, pairs, pieces)

    def run(fh, fl):
        out[...] = dot3(halves(v_ref[...]), (fh[...], fl[...]))

    choose([refs[i : i + 2] for i in range(0, len(refs), 2)], pair, split, run)


def finish_kernel(slots, pairs, pieces, window, has_total, is_last, *refs):
    values = refs[:window]
    mh, ml, own, oth = refs[window : window + 4]
    refs = refs[window + 4 :]
    start = refs[0][...] if has_total else None
    keep, give, *outs = refs[1:] if has_total else refs
    chip, is_a = chip_now(), upper_here()
    bs = mh.shape[1]
    half = keep.shape[0]
    _, _, turnout_at, district_at, _ = packed_places(slots, bs, 2 * half)
    parts = []
    for m in range(pieces):
        v = values[pairs - 1 + 2 * m][...]
        for q in range(1, pairs):
            v = jnp.where(chip == q, values[pairs - 1 - q + 2 * m][...], v)
        parts.append(v)
    v = jnp.concatenate(parts, axis=0)

    def m(k):
        return mh[k], ml[k]

    xa = dot3(halves(v[:, :bs]), m(0))
    xb = dot3(halves(v[:, bs:] - dot3(halves(xa), m(2))), m(1))
    kept, given = jnp.where(is_a, xa, xb), jnp.where(is_a, xb, xa)
    keep[...] = kept
    give[...] = given
    names = lax.broadcasted_iota(jnp.int32, (NDIST, bs), 0).astype(F32)
    sums = jnp.zeros((NDIST, 2 * half), F32) if start is None else start
    for x, pack in ((kept, own), (given, oth)):
        weight = pack[turnout_at : turnout_at + 1]
        member = names == pack[district_at : district_at + 1]
        member = member.astype(F32).astype(B16)
        terms = jnp.concatenate([x * weight, jnp.broadcast_to(weight, (half, bs))], axis=0)
        for part in halves(terms):
            sums = sums + lax.dot_general(
                member, part, (((1,), (1,)), ((), ())), preferred_element_type=F32
            )
    if not is_last:
        outs[0][...] = sums
        return
    held = outs.pop()
    held[...] = sums
    rows = NDIST // pairs
    for by, part in enumerate(outs):
        to = lax.rem(chip + by, pairs)
        part[...] = held[pl.ds(pl.multiple_of(to * rows, rows), rows), :]


def add_kernel(*refs):
    mine, theirs = refs[-2:]
    total = refs[0][...]
    for part in refs[1:-2]:
        total = total + part[...]
    rows = mine.shape[0]
    is_a = upper_here()
    mine[...] = jnp.where(is_a, total[rows:], total[:rows])
    theirs[...] = jnp.where(is_a, total[:rows], total[rows:])


def mean_kernel(mine, got, out):
    half = out.shape[1] // 2
    own, oth = (x[:, :half] / x[:, half:] for x in (mine, got))
    is_a = upper_here()
    out[...] = jnp.concatenate(
        [jnp.where(is_a, oth, own), jnp.where(is_a, own, oth)], axis=1
    )


def field_kernel(rows_here, *refs):
    keeps = refs[:rows_here]
    gots = refs[rows_here : 2 * rows_here]
    out = refs[2 * rows_here]
    is_a = upper_here()
    for r in range(rows_here):
        top = jnp.where(is_a, gots[r][...], keeps[r][...])
        bottom = jnp.where(is_a, keeps[r][...], gots[r][...])
        out[r, 0] = jnp.concatenate([top, bottom], axis=0).T


def body(rhs, lower_blocks, col_index, diag_inverse, turnout, district_of):
    n = lax.axis_size("blk")
    pairs = n // 2
    pieces = 1
    rows_here, _, bs, columns = rhs.shape
    slots = lower_blocks.shape[2]
    half = columns // 2
    width = half // pieces
    count = rows_here * pairs
    packed_rows = packed_places(slots, bs, columns)[-1]
    wide = shaped(width, 2 * bs)
    square = shaped(2 * bs, 2 * bs, dtype=B16)

    def call(kernel, name, outs, operands, mib, flops=0, moved=0, **more):
        several = isinstance(outs, tuple)
        return pl.pallas_call(
            kernel,
            out_shape=outs,
            in_specs=more.pop("in_specs", [VMEM_SPEC] * len(operands)),
            out_specs=more.pop("out_specs", (VMEM_SPEC,) * len(outs) if several else VMEM_SPEC),
            compiler_params=params(mib),
            cost_estimate=cost(flops, moved),
            name=name,
            **more,
        )(*operands)

    def swap(x):
        return lax.ppermute(x, "blk", [(i, i ^ 1) for i in range(n)])

    def shift(x, by):
        return lax.ppermute(x, "blk", [(i, (i + 2 * by) % n) for i in range(n)])

    def pack(rows):
        return call(
            functools.partial(pack_kernel, rows),
            "pack",
            (shaped(packed_rows, bs),) * len(rows),
            (jnp.transpose(col_index, (2, 1, 0)), turnout, district_of, lower_blocks, diag_inverse, rhs),
            56,
            moved=8 * packed_rows * bs * len(rows),
            in_specs=[SMEM_SPEC, VMEM_SPEC, VMEM_SPEC] + [HBM_SPEC] * 3,
            out_specs=(HBM_SPEC,) * len(rows),
            scratch_shapes=[
                pltpu.VMEM((len(rows), bs, columns), F32),
                pltpu.VMEM((len(rows), packed_rows - (slots + 1) * bs, bs), F32),
                pltpu.SemaphoreType.DMA((len(rows) * (slots + 3),)),
            ],
        )

    def setup(r):
        args = (r, n, slots, columns)
        held = shaped(4, bs, bs, dtype=B16)
        gh, gl, mh, ml, rt = call(
            functools.partial(near_setup_kernel, *args),
            "near_setup",
            (square, square, held, held, shaped(half, 2 * bs)),
            packs[r],
            10,
            14 * 3 * bs**3,
            24 * bs * bs * 4,
        )
        fh, fl = call(
            functools.partial(far_setup_kernel, *args),
            "far_setup",
            (square, square),
            (*packs[r], mh, ml),
            10,
            10 * 3 * bs**3,
            24 * bs * bs * 4,
        )
        return gh, gl, mh, ml, rt, fh, fl

    def finish(r, values, total):
        first = count - 1 - (r * pairs + pairs - 1)
        window = values[first : first + pairs + 2 * (pieces - 1)]
        is_last = r == 0
        outs = (shaped(half, bs), shaped(half, bs))
        outs += (shaped(NDIST // pairs, columns),) * pairs if is_last else (shaped(NDIST, columns),)
        extra = () if total is None else (total,)
        return call(
            functools.partial(
                finish_kernel, slots, pairs, pieces, len(window), total is not None, is_last
            ),
            "finish",
            outs,
            (*window, *fixed[r][2:4], *packs[r], *extra),
            8,
            6 * 3 * half * bs * bs,
            16 * bs * bs,
            scratch_shapes=[pltpu.VMEM((NDIST, columns), F32)] if is_last else [],
        )

    top = rows_here - 1
    packs, fixed = {}, {}
    (own,) = pack((top,))
    packs[top] = (own, swap(own))
    packed = pack(tuple(range(top))) if top else ()
    fixed[top] = setup(top)

    keeps, gots = {}, {}
    values = []
    total = near = far_now = far_next = None
    steps = count + 2 * (pieces - 1)
    for step in range(steps):
        lead = count - 1 - step
        low = max(lead, 0) // pairs
        high = min(lead + 2 * (pieces - 1), count - 1) // pairs
        rows = range(low, high + 1)
        taken = [x for x in (far_now, near) if x is not None]
        has_near = step + 1 < steps
        has_far = step + 2 < steps
        operands = []
        for r in rows:
            gh, gl, _, _, rt, _, _ = fixed[r]
            operands += [rt, gh, gl] if has_near else [rt]
        place = (lead, pairs, pieces, high * pairs)
        v, *near_out = call(
            functools.partial(near_kernel, *place, len(taken), has_near),
            "near_terms",
            (wide, wide) if has_near else (wide,),
            (*taken, *operands),
            4,
            6 * width * 4 * bs * bs,
            6 * width * bs * 4,
        )
        values.append(v)
        near = shift(near_out[0], -1) if has_near else None
        if has_near and (lead + 1) % pairs == 0 and 0 < lead // pairs:
            r = lead // pairs - 1
            own, _ = lax.optimization_barrier((packed[r], near_out[0]))
            packs[r] = (own, swap(own))
            fixed[r] = setup(r)
        far_now, far_next = far_next, None
        if has_far:
            operands = [x for r in rows for x in fixed[r][5:]]
            far_out = call(
                functools.partial(far_kernel, *place),
                "far_terms",
                wide,
                (v, *operands),
                4,
                6 * width * 4 * bs * bs,
                6 * width * bs * 4,
            )
            far_next = shift(far_out, -2)
        done = lead + 2 * (pieces - 1)
        if done % pairs == 0 and 0 < done // pairs <= top:
            r = done // pairs
            keeps[r], give, total = finish(r, values, total)
            gots[r] = swap(give)
            near, total = lax.optimization_barrier((near, total))

    keeps[0], give, *parts = finish(0, values, total)
    gots[0] = swap(give)
    parts = [parts[0]] + [shift(parts[by], by) for by in range(1, pairs)]
    order = range(rows_here)
    field = call(
        functools.partial(field_kernel, rows_here),
        "field",
        shaped(rows_here, 1, bs, columns),
        (*[keeps[r] for r in order], *[gots[r] for r in order]),
        4,
        0,
        8 * rows_here * bs * columns,
    )
    parts, field = lax.optimization_barrier((parts, field))
    held = shaped(NDIST // n, columns)
    mine, theirs = call(add_kernel, "district_add", (held, held), tuple(parts), 4)
    mean = call(mean_kernel, "district_mean", held, (mine, swap(theirs)), 4)
    return field, mean


def solution(mesh):
    placed = (
        P(None, "blk", None, "sims"),
        P(None, "blk", None, None, None),
        P(None, "blk", None),
        P(None, "blk", None, None),
        P(None, "blk", None),
        P(None, "blk", None),
    )
    return jax.shard_map(
        body,
        mesh=mesh,
        in_specs=placed,
        out_specs=(P(None, "blk", None, "sims"), P("blk", "sims")),
        check_vma=False,
    )
```

```python
import functools

import jax
import jax.numpy as jnp
from jax import lax
from jax.experimental import pallas as pl
from jax.experimental.pallas import tpu as pltpu
from jax.sharding import PartitionSpec as P

NDIST = 256
F32 = jnp.float32
B16 = jnp.bfloat16
SMEM_SPEC = pl.BlockSpec(memory_space=pltpu.SMEM)
VMEM_SPEC = pl.BlockSpec(memory_space=pltpu.VMEM)
HBM_SPEC = pl.BlockSpec(memory_space=pltpu.HBM)


def params(mib):
    return pltpu.CompilerParams(vmem_limit_bytes=mib * 1024 * 1024)


def cost(flops, moved):
    return pl.CostEstimate(flops=flops, bytes_accessed=moved, transcendentals=0)


def shaped(*shape, dtype=F32):
    return jax.ShapeDtypeStruct(shape, dtype)


def halves(x):
    hi = x.astype(B16)
    lo = (x - hi.astype(F32)).astype(B16)
    return hi, lo


def dot(a, b):
    return jnp.dot(a, b, preferred_element_type=F32)


def dot3(x, y):
    rows = x[0].shape[0]
    both = dot(jnp.concatenate([x[0], x[1]], axis=0), y[0])
    return both[:rows] + both[rows:] + dot(x[0], y[1])


def packed_places(slots, bs, columns):
    rhs_at = (slots + 1) * bs
    col_at = rhs_at + columns
    turnout_at = col_at + 8 * slots
    district_at = turnout_at + 8
    return rhs_at, col_at, turnout_at, district_at, district_at + 8


def chip_now():
    return lax.div(lax.axis_index("blk").astype(jnp.int32), 2)


def upper_here():
    return lax.rem(lax.axis_index("blk").astype(jnp.int32), 2) == 1


def pack_kernel(rows, cols, turnout, district, l_ref, d_ref, r_ref, *refs):
    outs = refs[: len(rows)]
    held, sems = refs[len(rows) :]
    slots, bs = l_ref.shape[2], l_ref.shape[3]
    columns = r_ref.shape[3]
    rhs_at, col_at, turnout_at, district_at, _ = packed_places(slots, bs, columns)
    copies = []

    def copy(source, target):
        copies.append(pltpu.make_async_copy(source, target, sems.at[len(copies)]))
        copies[-1].start()

    for i, r in enumerate(rows):
        copy(r_ref.at[r, 0], held.at[i])
    for out, r in zip(outs, rows):
        for k in range(slots):
            copy(l_ref.at[r, 0, k], out.at[pl.ds(k * bs, bs)])
        copy(d_ref.at[r, 0], out.at[pl.ds(slots * bs, bs)])
    for out, r in zip(outs, rows):
        for k in range(slots):
            at = col_at + 8 * k
            out[at : at + 8] = jnp.full((8, bs), cols[k, 0, r].astype(F32))
        out[turnout_at : turnout_at + 8] = jnp.broadcast_to(turnout[r], (8, bs))
        out[district_at : district_at + 8] = jnp.broadcast_to(
            district[r].astype(F32), (8, bs)
        )
    for i, out in enumerate(outs):
        copies[i].wait()
        out[rhs_at:col_at] = held[i].T
    for started in copies[len(rows) :]:
        started.wait()


def put(high, low, i, j, value):
    bs = value.shape[0]
    hi, lo = halves(value)
    high[i * bs : (i + 1) * bs, j * bs : (j + 1) * bs] = hi
    low[i * bs : (i + 1) * bs, j * bs : (j + 1) * bs] = lo


def blocks_of(r, n, slots, columns, own, oth):
    is_a = upper_here()
    bs = own.shape[1]
    _, col_at, _, _, _ = packed_places(slots, bs, columns)
    row_b = r * n + 2 * chip_now()
    row_a = row_b + 1

    def upper(at, size):
        return jnp.where(is_a, own[at : at + size], oth[at : at + size])

    def lower(at, size):
        return jnp.where(is_a, oth[at : at + size], own[at : at + size])

    def at_distance(side, row, d):
        found = jnp.zeros((bs, bs), F32)
        column = (row - d).astype(F32)
        for k in range(1, slots):
            col = side(col_at + 8 * k, 1)
            here = (col == column) & (col >= 0.0)
            found = jnp.where(here, side(k * bs, bs), found)
        return halves(found)

    return upper, lower, lambda d: at_distance(upper, row_a, d), lambda d: at_distance(lower, row_b, d)


def near_setup_kernel(r, n, slots, columns, own, oth, gh, gl, mh, ml, rt):
    bs = own.shape[1]
    half = columns // 2
    rhs_at, col_at, _, _, _ = packed_places(slots, bs, columns)
    upper, lower, upper_at, lower_at = blocks_of(r, n, slots, columns, own, oth)
    is_a = upper_here()
    da, db = halves(upper(slots * bs, bs)), halves(lower(slots * bs, bs))
    la1 = halves(upper(0, bs))
    lb1 = halves(jnp.where(lower(col_at, 1) >= 0.0, lower(0, bs), 0.0))
    w = dot3(da, la1)
    wh = halves(w)
    for place, pair in enumerate((da, db, la1, wh)):
        mh[place] = pair[0]
        ml[place] = pair[1]
    for j, (la, lb) in enumerate(((upper_at(2), lb1), (upper_at(3), lower_at(2)))):
        from_b = dot3(db, lb)
        put(gh, gl, 1, j, from_b)
        put(gh, gl, 0, j, dot3(da, la) - dot3(wh, halves(from_b)))
    ra, rb = upper(rhs_at, columns), lower(rhs_at, columns)
    rt[:, :bs] = jnp.where(is_a, ra[half:], ra[:half])
    rt[:, bs:] = jnp.where(is_a, rb[half:], rb[:half])


def far_setup_kernel(r, n, slots, columns, own, oth, mh, ml, fh, fl):
    _, _, upper_at, lower_at = blocks_of(r, n, slots, columns, own, oth)
    da, db, w = ((mh[k], ml[k]) for k in (0, 1, 3))
    for j, lb in enumerate((lower_at(3), lower_at(4))):
        from_b = dot3(db, lb)
        put(fh, fl, 1, j, from_b)
        from_a = -dot3(w, halves(from_b))
        if j == 0:
            from_a = from_a + dot3(da, upper_at(4))
        put(fh, fl, 0, j, from_a)


def place_of(lead, pairs, pieces):
    ahead = lax.rem(chip_now() - lead % pairs + pairs, pairs)
    piece = jnp.minimum(lax.div(ahead, 2), pieces - 1)
    return piece, lead + ahead


def choose(choices, pair, split, run):
    if len(choices) == 1:
        run(*choices[0])
        return

    @pl.when(pair < split)
    def _():
        run(*choices[0])

    @pl.when(pair >= split)
    def _():
        run(*choices[1])


def near_kernel(lead, pairs, pieces, split, ordered, received, has_near, *refs):
    refs = refs[ordered:]
    taken = refs[:received]
    outs = refs[-2:] if has_near else refs[-1:]
    refs = refs[received : -len(outs)]
    each = 3 if has_near else 1
    choices = [refs[i : i + each] for i in range(0, len(refs), each)]
    v_out = outs[0]
    width = v_out.shape[0]
    piece, pair = place_of(lead, pairs, pieces)
    rows = pl.ds(pl.multiple_of(piece * width, width), width)

    def run(rt, gh=None, gl=None):
        v = rt[rows, :]
        for x in taken:
            v = v - x[...]
        v_out[...] = v
        if has_near:
            outs[1][...] = dot3(halves(v), (gh[...], gl[...]))

    choose(choices, pair, split, run)


def far_kernel(lead, pairs, pieces, split, v_ref, *refs):
    out = refs[-1]
    refs = refs[:-1]
    _, pair = place_of(lead, pairs, pieces)

    def run(fh, fl):
        out[...] = dot3(halves(v_ref[...]), (fh[...], fl[...]))

    choose([refs[i : i + 2] for i in range(0, len(refs), 2)], pair, split, run)


def finish_kernel(slots, pairs, pieces, window, has_total, is_last, *refs):
    values = refs[:window]
    mh, ml, own, oth = refs[window : window + 4]
    refs = refs[window + 4 :]
    start = refs[0][...] if has_total else None
    keep, give, *outs = refs[1:] if has_total else refs
    chip, is_a = chip_now(), upper_here()
    bs = mh.shape[1]
    half = keep.shape[0]
    _, _, turnout_at, district_at, _ = packed_places(slots, bs, 2 * half)
    parts = []
    for m in range(pieces):
        v = values[pairs - 1 + 2 * m][...]
        for q in range(1, pairs):
            v = jnp.where(chip == q, values[pairs - 1 - q + 2 * m][...], v)
        parts.append(v)
    v = jnp.concatenate(parts, axis=0)

    def m(k):
        return mh[k], ml[k]

    xa = dot3(halves(v[:, :bs]), m(0))
    xb = dot3(halves(v[:, bs:] - dot3(halves(xa), m(2))), m(1))
    kept, given = jnp.where(is_a, xa, xb), jnp.where(is_a, xb, xa)
    keep[...] = kept
    give[...] = given
    names = lax.broadcasted_iota(jnp.int32, (NDIST, bs), 0).astype(F32)
    sums = jnp.zeros((NDIST, 2 * half), F32) if start is None else start
    for x, pack in ((kept, own), (given, oth)):
        weight = pack[turnout_at : turnout_at + 1]
        member = names == pack[district_at : district_at + 1]
        member = member.astype(F32).astype(B16)
        terms = jnp.concatenate([x * weight, jnp.broadcast_to(weight, (half, bs))], axis=0)
        for part in halves(terms):
            sums = sums + lax.dot_general(
                member, part, (((1,), (1,)), ((), ())), preferred_element_type=F32
            )
    if not is_last:
        outs[0][...] = sums
        return
    held = outs.pop()
    held[...] = sums
    rows = NDIST // pairs
    for by, part in enumerate(outs):
        to = lax.rem(chip + by, pairs)
        part[...] = held[pl.ds(pl.multiple_of(to * rows, rows), rows), :]


def add_kernel(*refs):
    mine, theirs = refs[-2:]
    total = refs[0][...]
    for part in refs[1:-2]:
        total = total + part[...]
    rows = mine.shape[0]
    is_a = upper_here()
    mine[...] = jnp.where(is_a, total[rows:], total[:rows])
    theirs[...] = jnp.where(is_a, total[:rows], total[rows:])


def mean_kernel(mine, got, out):
    half = out.shape[1] // 2
    own, oth = (x[:, :half] / x[:, half:] for x in (mine, got))
    is_a = upper_here()
    out[...] = jnp.concatenate(
        [jnp.where(is_a, oth, own), jnp.where(is_a, own, oth)], axis=1
    )


def field_kernel(rows_here, *refs):
    keeps = refs[:rows_here]
    gots = refs[rows_here : 2 * rows_here]
    out = refs[2 * rows_here]
    is_a = upper_here()
    for r in range(rows_here):
        top = jnp.where(is_a, gots[r][...], keeps[r][...])
        bottom = jnp.where(is_a, keeps[r][...], gots[r][...])
        out[r, 0] = jnp.concatenate([top, bottom], axis=0).T


def body(rhs, lower_blocks, col_index, diag_inverse, turnout, district_of):
    n = lax.axis_size("blk")
    pairs = n // 2
    pieces = 1
    rows_here, _, bs, columns = rhs.shape
    slots = lower_blocks.shape[2]
    half = columns // 2
    width = half // pieces
    count = rows_here * pairs
    packed_rows = packed_places(slots, bs, columns)[-1]
    wide = shaped(width, 2 * bs)
    square = shaped(2 * bs, 2 * bs, dtype=B16)

    def call(kernel, name, outs, operands, mib, flops=0, moved=0, **more):
        several = isinstance(outs, tuple)
        return pl.pallas_call(
            kernel,
            out_shape=outs,
            in_specs=more.pop("in_specs", [VMEM_SPEC] * len(operands)),
            out_specs=(VMEM_SPEC,) * len(outs) if several else VMEM_SPEC,
            compiler_params=params(mib),
            cost_estimate=cost(flops, moved),
            name=name,
            **more,
        )(*operands)

    def swap(x):
        return lax.ppermute(x, "blk", [(i, i ^ 1) for i in range(n)])

    def shift(x, by):
        return lax.ppermute(x, "blk", [(i, (i + 2 * by) % n) for i in range(n)])

    def pass_on(x, lead, by):
        perm = []
        for k in range(lead, lead + 2 * pieces, 2):
            if by <= k < count:
                sender, target = k % pairs, (k - by) % pairs
                perm += [(2 * sender + c, 2 * target + c) for c in range(2)]
        return lax.ppermute(x, "blk", perm)

    def pack(rows, turnout=turnout):
        return call(
            functools.partial(pack_kernel, rows),
            "pack",
            (shaped(packed_rows, bs),) * len(rows),
            (jnp.transpose(col_index, (2, 1, 0)), turnout, district_of, lower_blocks, diag_inverse, rhs),
            56,
            moved=8 * packed_rows * bs * len(rows),
            in_specs=[SMEM_SPEC, VMEM_SPEC, VMEM_SPEC] + [HBM_SPEC] * 3,
            scratch_shapes=[
                pltpu.VMEM((len(rows), bs, columns), F32),
                pltpu.SemaphoreType.DMA((len(rows) * (slots + 2),)),
            ],
        )

    def setup(r):
        args = (r, n, slots, columns)
        held = shaped(4, bs, bs, dtype=B16)
        gh, gl, mh, ml, rt = call(
            functools.partial(near_setup_kernel, *args),
            "near_setup",
            (square, square, held, held, shaped(half, 2 * bs)),
            packs[r],
            10,
            14 * 3 * bs**3,
            24 * bs * bs * 4,
        )
        fh, fl = call(
            functools.partial(far_setup_kernel, *args),
            "far_setup",
            (square, square),
            (*packs[r], mh, ml),
            10,
            10 * 3 * bs**3,
            24 * bs * bs * 4,
        )
        return gh, gl, mh, ml, rt, fh, fl

    def finish(r, values, total):
        first = count - 1 - (r * pairs + pairs - 1)
        window = values[first : first + pairs + 2 * (pieces - 1)]
        is_last = r == 0
        outs = (shaped(half, bs), shaped(half, bs))
        outs += (shaped(NDIST // pairs, columns),) * pairs if is_last else (shaped(NDIST, columns),)
        extra = () if total is None else (total,)
        return call(
            functools.partial(
                finish_kernel, slots, pairs, pieces, len(window), total is not None, is_last
            ),
            "finish",
            outs,
            (*window, *fixed[r][2:4], *packs[r], *extra),
            8,
            6 * 3 * half * bs * bs,
            16 * bs * bs,
            scratch_shapes=[pltpu.VMEM((NDIST, columns), F32)] if is_last else [],
        )

    top = rows_here - 1
    packs, fixed = {}, {}
    (own,) = pack((top,))
    packs[top] = (own, swap(own))
    fixed[top] = setup(top)
    later, _ = lax.optimization_barrier((turnout, fixed[top][4]))
    packed = pack(tuple(range(top)), later) if top else ()

    keeps, gots = {}, {}
    values = []
    ordered = ()
    total = near = far_now = far_next = None
    steps = count + 2 * (pieces - 1)
    for step in range(steps):
        lead = count - 1 - step
        low = max(lead, 0) // pairs
        high = min(lead + 2 * (pieces - 1), count - 1) // pairs
        rows = range(low, high + 1)
        taken = [x for x in (far_now, near) if x is not None]
        has_near = step + 1 < steps
        has_far = step + 2 < steps
        operands = []
        for r in rows:
            gh, gl, _, _, rt, _, _ = fixed[r]
            operands += [rt, gh, gl] if has_near else [rt]
        place = (lead, pairs, pieces, high * pairs)
        v, *near_out = call(
            functools.partial(near_kernel, *place, len(ordered), len(taken), has_near),
            "near_terms",
            (wide, wide) if has_near else (wide,),
            (*ordered, *taken, *operands),
            4,
            6 * width * 4 * bs * bs,
            6 * width * bs * 4,
        )
        values.append(v)
        near = pass_on(near_out[0], lead, 1) if has_near else None
        if has_near and (lead + 1) % pairs == 0 and 0 < lead // pairs:
            r = lead // pairs - 1
            own, _ = lax.optimization_barrier((packed[r], near_out[0]))
            packs[r] = (own, swap(own))
            fixed[r] = setup(r)
        far_now, far_next, ordered = far_next, None, ()
        if has_far:
            operands = [x for r in rows for x in fixed[r][5:]]
            far_out = call(
                functools.partial(far_kernel, *place),
                "far_terms",
                wide,
                (v, *operands),
                4,
                6 * width * 4 * bs * bs,
                6 * width * bs * 4,
            )
            far_next = pass_on(far_out, lead, 2)
            ordered = (far_out,)
        done = lead + 2 * (pieces - 1)
        if done % pairs == 0 and 0 < done // pairs <= top:
            r = done // pairs
            keeps[r], give, total = finish(r, values, total)
            gots[r] = swap(give)
            near, total = lax.optimization_barrier((near, total))

    keeps[0], give, *parts = finish(0, values, total)
    gots[0] = swap(give)
    parts = [parts[0]] + [shift(parts[by], by) for by in range(1, pairs)]
    order = range(rows_here)
    field = call(
        functools.partial(field_kernel, rows_here),
        "field",
        shaped(rows_here, 1, bs, columns),
        (*[keeps[r] for r in order], *[gots[r] for r in order]),
        4,
        0,
        8 * rows_here * bs * columns,
    )
    parts, field = lax.optimization_barrier((parts, field))
    held = shaped(NDIST // n, columns)
    mine, theirs = call(add_kernel, "district_add", (held, held), tuple(parts), 4)
    mean = call(mean_kernel, "district_mean", held, (mine, swap(theirs)), 4)
    return field, mean


def solution(mesh):
    placed = (
        P(None, "blk", None, "sims"),
        P(None, "blk", None, None, None),
        P(None, "blk", None),
        P(None, "blk", None, None),
        P(None, "blk", None),
        P(None, "blk", None),
    )
    return jax.shard_map(
        body,
        mesh=mesh,
        in_specs=placed,
        out_specs=(P(None, "blk", None, "sims"), P("blk", "sims")),
        check_vma=False,
    )
```

```python
import functools

import jax
import jax.numpy as jnp
from jax import lax
from jax.experimental import pallas as pl
from jax.experimental.pallas import tpu as pltpu
from jax.sharding import PartitionSpec as P

NDIST = 256
F32 = jnp.float32
B16 = jnp.bfloat16
SMEM_SPEC = pl.BlockSpec(memory_space=pltpu.SMEM)
VMEM_SPEC = pl.BlockSpec(memory_space=pltpu.VMEM)
HBM_SPEC = pl.BlockSpec(memory_space=pltpu.HBM)


def params(mib):
    return pltpu.CompilerParams(vmem_limit_bytes=mib * 1024 * 1024)


def cost(flops, moved):
    return pl.CostEstimate(flops=flops, bytes_accessed=moved, transcendentals=0)


def shaped(*shape, dtype=F32):
    return jax.ShapeDtypeStruct(shape, dtype)


def halves(x):
    hi = x.astype(B16)
    lo = (x - hi.astype(F32)).astype(B16)
    return hi, lo


def dot(a, b):
    return jnp.dot(a, b, preferred_element_type=F32)


def dot3(x, y):
    rows = x[0].shape[0]
    both = dot(jnp.concatenate([x[0], x[1]], axis=0), y[0])
    return both[:rows] + both[rows:] + dot(x[0], y[1])


def packed_places(slots, bs, columns):
    rhs_at = (slots + 1) * bs
    col_at = rhs_at + columns
    turnout_at = col_at + 8 * slots
    district_at = turnout_at + 8
    return rhs_at, col_at, turnout_at, district_at, district_at + 8


def chip_now():
    return lax.div(lax.axis_index("blk").astype(jnp.int32), 2)


def upper_here():
    return lax.rem(lax.axis_index("blk").astype(jnp.int32), 2) == 1


def pack_kernel(rows, cols, turnout, district, l_ref, d_ref, r_ref, *refs):
    outs = refs[: len(rows)]
    held, sems = refs[len(rows) :]
    slots, bs = l_ref.shape[2], l_ref.shape[3]
    columns = r_ref.shape[3]
    rhs_at, col_at, turnout_at, district_at, _ = packed_places(slots, bs, columns)
    copies = []

    def copy(source, target):
        copies.append(pltpu.make_async_copy(source, target, sems.at[len(copies)]))
        copies[-1].start()

    for i, r in enumerate(rows):
        copy(r_ref.at[r, 0], held.at[i])
    for out, r in zip(outs, rows):
        for k in range(slots):
            copy(l_ref.at[r, 0, k], out.at[pl.ds(k * bs, bs)])
        copy(d_ref.at[r, 0], out.at[pl.ds(slots * bs, bs)])
    for out, r in zip(outs, rows):
        for k in range(slots):
            at = col_at + 8 * k
            out[at : at + 8] = jnp.full((8, bs), cols[k, 0, r].astype(F32))
        out[turnout_at : turnout_at + 8] = jnp.broadcast_to(turnout[r], (8, bs))
        out[district_at : district_at + 8] = jnp.broadcast_to(
            district[r].astype(F32), (8, bs)
        )
    for i, out in enumerate(outs):
        copies[i].wait()
        out[rhs_at:col_at] = held[i].T
    for started in copies[len(rows) :]:
        started.wait()


def put(high, low, i, j, value):
    bs = value.shape[0]
    hi, lo = halves(value)
    high[i * bs : (i + 1) * bs, j * bs : (j + 1) * bs] = hi
    low[i * bs : (i + 1) * bs, j * bs : (j + 1) * bs] = lo


def blocks_of(r, n, slots, columns, own, oth):
    is_a = upper_here()
    bs = own.shape[1]
    _, col_at, _, _, _ = packed_places(slots, bs, columns)
    row_b = r * n + 2 * chip_now()
    row_a = row_b + 1

    def upper(at, size):
        return jnp.where(is_a, own[at : at + size], oth[at : at + size])

    def lower(at, size):
        return jnp.where(is_a, oth[at : at + size], own[at : at + size])

    def at_distance(side, row, d):
        found = jnp.zeros((bs, bs), F32)
        column = (row - d).astype(F32)
        for k in range(1, slots):
            col = side(col_at + 8 * k, 1)
            here = (col == column) & (col >= 0.0)
            found = jnp.where(here, side(k * bs, bs), found)
        return halves(found)

    return upper, lower, lambda d: at_distance(upper, row_a, d), lambda d: at_distance(lower, row_b, d)


def near_setup_kernel(r, n, slots, columns, own, oth, gh, gl, mh, ml, rt):
    bs = own.shape[1]
    half = columns // 2
    rhs_at, col_at, _, _, _ = packed_places(slots, bs, columns)
    upper, lower, upper_at, lower_at = blocks_of(r, n, slots, columns, own, oth)
    is_a = upper_here()
    da, db = halves(upper(slots * bs, bs)), halves(lower(slots * bs, bs))
    la1 = halves(upper(0, bs))
    lb1 = halves(jnp.where(lower(col_at, 1) >= 0.0, lower(0, bs), 0.0))
    w = dot3(da, la1)
    wh = halves(w)
    for place, pair in enumerate((da, db, la1, wh)):
        mh[place] = pair[0]
        ml[place] = pair[1]
    for j, (la, lb) in enumerate(((upper_at(2), lb1), (upper_at(3), lower_at(2)))):
        from_b = dot3(db, lb)
        put(gh, gl, 1, j, from_b)
        put(gh, gl, 0, j, dot3(da, la) - dot3(wh, halves(from_b)))
    ra, rb = upper(rhs_at, columns), lower(rhs_at, columns)
    rt[:, :bs] = jnp.where(is_a, ra[half:], ra[:half])
    rt[:, bs:] = jnp.where(is_a, rb[half:], rb[:half])


def far_setup_kernel(r, n, slots, columns, own, oth, mh, ml, fh, fl):
    _, _, upper_at, lower_at = blocks_of(r, n, slots, columns, own, oth)
    da, db, w = ((mh[k], ml[k]) for k in (0, 1, 3))
    for j, lb in enumerate((lower_at(3), lower_at(4))):
        from_b = dot3(db, lb)
        put(fh, fl, 1, j, from_b)
        from_a = -dot3(w, halves(from_b))
        if j == 0:
            from_a = from_a + dot3(da, upper_at(4))
        put(fh, fl, 0, j, from_a)


def place_of(lead, pairs, pieces):
    ahead = lax.rem(chip_now() - lead % pairs + pairs, pairs)
    piece = jnp.minimum(lax.div(ahead, 2), pieces - 1)
    return piece, lead + ahead


def choose(choices, pair, split, run):
    if len(choices) == 1:
        run(*choices[0])
        return

    @pl.when(pair < split)
    def _():
        run(*choices[0])

    @pl.when(pair >= split)
    def _():
        run(*choices[1])


def near_kernel(lead, pairs, pieces, split, ordered, received, has_near, *refs):
    refs = refs[ordered:]
    taken = refs[:received]
    outs = refs[-2:] if has_near else refs[-1:]
    refs = refs[received : -len(outs)]
    each = 3 if has_near else 1
    choices = [refs[i : i + each] for i in range(0, len(refs), each)]
    v_out = outs[0]
    width = v_out.shape[0]
    piece, pair = place_of(lead, pairs, pieces)
    rows = pl.ds(pl.multiple_of(piece * width, width), width)

    def run(rt, gh=None, gl=None):
        v = rt[rows, :]
        for x in taken:
            v = v - x[...]
        v_out[...] = v
        if has_near:
            outs[1][...] = dot3(halves(v), (gh[...], gl[...]))

    choose(choices, pair, split, run)


def far_kernel(lead, pairs, pieces, split, v_ref, *refs):
    out = refs[-1]
    refs = refs[:-1]
    _, pair = place_of(lead, pairs, pieces)

    def run(fh, fl):
        out[...] = dot3(halves(v_ref[...]), (fh[...], fl[...]))

    choose([refs[i : i + 2] for i in range(0, len(refs), 2)], pair, split, run)


def finish_kernel(slots, pairs, pieces, window, has_total, is_last, *refs):
    values = refs[:window]
    mh, ml, own, oth = refs[window : window + 4]
    refs = refs[window + 4 :]
    start = refs[0][...] if has_total else None
    keep, give, *outs = refs[1:] if has_total else refs
    chip, is_a = chip_now(), upper_here()
    bs = mh.shape[1]
    half = keep.shape[0]
    _, _, turnout_at, district_at, _ = packed_places(slots, bs, 2 * half)
    parts = []
    for m in range(pieces):
        v = values[pairs - 1 + 2 * m][...]
        for q in range(1, pairs):
            v = jnp.where(chip == q, values[pairs - 1 - q + 2 * m][...], v)
        parts.append(v)
    v = jnp.concatenate(parts, axis=0)

    def m(k):
        return mh[k], ml[k]

    xa = dot3(halves(v[:, :bs]), m(0))
    xb = dot3(halves(v[:, bs:] - dot3(halves(xa), m(2))), m(1))
    kept, given = jnp.where(is_a, xa, xb), jnp.where(is_a, xb, xa)
    keep[...] = kept
    give[...] = given
    names = lax.broadcasted_iota(jnp.int32, (NDIST, bs), 0).astype(F32)
    sums = jnp.zeros((NDIST, 2 * half), F32) if start is None else start
    for x, pack in ((kept, own), (given, oth)):
        weight = pack[turnout_at : turnout_at + 1]
        member = names == pack[district_at : district_at + 1]
        member = member.astype(F32).astype(B16)
        terms = jnp.concatenate([x * weight, jnp.broadcast_to(weight, (half, bs))], axis=0)
        for part in halves(terms):
            sums = sums + lax.dot_general(
                member, part, (((1,), (1,)), ((), ())), preferred_element_type=F32
            )
    if not is_last:
        outs[0][...] = sums
        return
    held = outs.pop()
    held[...] = sums
    rows = NDIST // pairs
    for by, part in enumerate(outs):
        to = lax.rem(chip + by, pairs)
        part[...] = held[pl.ds(pl.multiple_of(to * rows, rows), rows), :]


def add_kernel(*refs):
    mine, theirs = refs[-2:]
    total = refs[0][...]
    for part in refs[1:-2]:
        total = total + part[...]
    rows = mine.shape[0]
    is_a = upper_here()
    mine[...] = jnp.where(is_a, total[rows:], total[:rows])
    theirs[...] = jnp.where(is_a, total[:rows], total[rows:])


def mean_kernel(mine, got, out):
    half = out.shape[1] // 2
    own, oth = (x[:, :half] / x[:, half:] for x in (mine, got))
    is_a = upper_here()
    out[...] = jnp.concatenate(
        [jnp.where(is_a, oth, own), jnp.where(is_a, own, oth)], axis=1
    )


def field_kernel(rows_here, *refs):
    keeps = refs[:rows_here]
    gots = refs[rows_here : 2 * rows_here]
    out = refs[2 * rows_here]
    is_a = upper_here()
    for r in range(rows_here):
        top = jnp.where(is_a, gots[r][...], keeps[r][...])
        bottom = jnp.where(is_a, keeps[r][...], gots[r][...])
        out[r, 0] = jnp.concatenate([top, bottom], axis=0).T


def body(rhs, lower_blocks, col_index, diag_inverse, turnout, district_of):
    n = lax.axis_size("blk")
    pairs = n // 2
    pieces = 1
    rows_here, _, bs, columns = rhs.shape
    slots = lower_blocks.shape[2]
    half = columns // 2
    width = half // pieces
    count = rows_here * pairs
    packed_rows = packed_places(slots, bs, columns)[-1]
    wide = shaped(width, 2 * bs)
    square = shaped(2 * bs, 2 * bs, dtype=B16)

    def call(kernel, name, outs, operands, mib, flops=0, moved=0, **more):
        several = isinstance(outs, tuple)
        return pl.pallas_call(
            kernel,
            out_shape=outs,
            in_specs=more.pop("in_specs", [VMEM_SPEC] * len(operands)),
            out_specs=(VMEM_SPEC,) * len(outs) if several else VMEM_SPEC,
            compiler_params=params(mib),
            cost_estimate=cost(flops, moved),
            name=name,
            **more,
        )(*operands)

    def swap(x):
        return lax.ppermute(x, "blk", [(i, i ^ 1) for i in range(n)])

    def shift(x, by):
        return lax.ppermute(x, "blk", [(i, (i + 2 * by) % n) for i in range(n)])

    def pass_on(x, lead, by):
        perm = []
        for k in range(lead, lead + 2 * pieces, 2):
            if by <= k < count:
                sender, target = k % pairs, (k - by) % pairs
                perm += [(2 * sender + c, 2 * target + c) for c in range(2)]
        return lax.ppermute(x, "blk", perm)

    def pack(rows, turnout=turnout):
        return call(
            functools.partial(pack_kernel, rows),
            "pack",
            (shaped(packed_rows, bs),) * len(rows),
            (jnp.transpose(col_index, (2, 1, 0)), turnout, district_of, lower_blocks, diag_inverse, rhs),
            56,
            moved=8 * packed_rows * bs * len(rows),
            in_specs=[SMEM_SPEC, VMEM_SPEC, VMEM_SPEC] + [HBM_SPEC] * 3,
            scratch_shapes=[
                pltpu.VMEM((len(rows), bs, columns), F32),
                pltpu.SemaphoreType.DMA((len(rows) * (slots + 2),)),
            ],
        )

    def setup(r):
        args = (r, n, slots, columns)
        held = shaped(4, bs, bs, dtype=B16)
        gh, gl, mh, ml, rt = call(
            functools.partial(near_setup_kernel, *args),
            "near_setup",
            (square, square, held, held, shaped(half, 2 * bs)),
            packs[r],
            10,
            14 * 3 * bs**3,
            24 * bs * bs * 4,
        )
        fh, fl = call(
            functools.partial(far_setup_kernel, *args),
            "far_setup",
            (square, square),
            (*packs[r], mh, ml),
            10,
            10 * 3 * bs**3,
            24 * bs * bs * 4,
        )
        return gh, gl, mh, ml, rt, fh, fl

    def finish(r, values, total):
        first = count - 1 - (r * pairs + pairs - 1)
        window = values[first : first + pairs + 2 * (pieces - 1)]
        is_last = r == 0
        outs = (shaped(half, bs), shaped(half, bs))
        outs += (shaped(NDIST // pairs, columns),) * pairs if is_last else (shaped(NDIST, columns),)
        extra = () if total is None else (total,)
        return call(
            functools.partial(
                finish_kernel, slots, pairs, pieces, len(window), total is not None, is_last
            ),
            "finish",
            outs,
            (*window, *fixed[r][2:4], *packs[r], *extra),
            8,
            6 * 3 * half * bs * bs,
            16 * bs * bs,
            scratch_shapes=[pltpu.VMEM((NDIST, columns), F32)] if is_last else [],
        )

    top = rows_here - 1
    packs, fixed = {}, {}
    (own,) = pack((top,))
    packs[top] = (own, swap(own))
    later, _ = lax.optimization_barrier((turnout, own))
    packed = pack(tuple(range(top)), later) if top else ()
    fixed[top] = setup(top)

    keeps, gots = {}, {}
    values = []
    ordered, waiting = (), []
    total = near = far_now = far_next = None
    steps = count + 2 * (pieces - 1)
    for step in range(steps):
        lead = count - 1 - step
        low = max(lead, 0) // pairs
        high = min(lead + 2 * (pieces - 1), count - 1) // pairs
        rows = range(low, high + 1)
        taken = [x for x in (far_now, near) if x is not None]
        has_near = step + 1 < steps
        has_far = step + 2 < steps
        operands = []
        for r in rows:
            gh, gl, _, _, rt, _, _ = fixed[r]
            operands += [rt, gh, gl] if has_near else [rt]
        place = (lead, pairs, pieces, high * pairs)
        v, *near_out = call(
            functools.partial(near_kernel, *place, len(ordered), len(taken), has_near),
            "near_terms",
            (wide, wide) if has_near else (wide,),
            (*ordered, *taken, *operands),
            4,
            6 * width * 4 * bs * bs,
            6 * width * bs * 4,
        )
        values.append(v)
        near = pass_on(near_out[0], lead, 1) if has_near else None
        far_now, far_next, ordered = far_next, None, ()
        if has_far:
            operands = [x for r in rows for x in fixed[r][5:]]
            far_out = call(
                functools.partial(far_kernel, *place),
                "far_terms",
                wide,
                (v, *operands),
                4,
                6 * width * 4 * bs * bs,
                6 * width * bs * 4,
            )
            ordered = (far_out,)
            r, chip = lead // pairs, lead % pairs
            if chip == pairs - 1 and r > 0:
                own, _ = lax.optimization_barrier((packed[r - 1], far_out))
                packs[r - 1] = (own, swap(own))
                fixed[r - 1] = setup(r - 1)
            if waiting:
                far_out, *_ = lax.optimization_barrier((far_out, *waiting))
            waiting = []
            if r > 0 and chip == pairs - 2:
                waiting = [fixed[r - 1][4]]
            if r > 0 and chip == pairs - 3:
                waiting = [fixed[r - 1][5]]
            far_next = pass_on(far_out, lead, 2)
        done = lead + 2 * (pieces - 1)
        if done % pairs == 0 and 0 < done // pairs <= top:
            r = done // pairs
            keeps[r], give, total = finish(r, values, total)
            gots[r] = swap(give)
            waiting = [total]

    keeps[0], give, *parts = finish(0, values, total)
    gots[0] = swap(give)
    parts = [parts[0]] + [shift(parts[by], by) for by in range(1, pairs)]
    order = range(rows_here)
    field = call(
        functools.partial(field_kernel, rows_here),
        "field",
        shaped(rows_here, 1, bs, columns),
        (*[keeps[r] for r in order], *[gots[r] for r in order]),
        4,
        0,
        8 * rows_here * bs * columns,
    )
    parts, field = lax.optimization_barrier((parts, field))
    held = shaped(NDIST // n, columns)
    mine, theirs = call(add_kernel, "district_add", (held, held), tuple(parts), 4)
    mean = call(mean_kernel, "district_mean", held, (mine, swap(theirs)), 4)
    return field, mean


def solution(mesh):
    placed = (
        P(None, "blk", None, "sims"),
        P(None, "blk", None, None, None),
        P(None, "blk", None),
        P(None, "blk", None, None),
        P(None, "blk", None),
        P(None, "blk", None),
    )
    return jax.shard_map(
        body,
        mesh=mesh,
        in_specs=placed,
        out_specs=(P(None, "blk", None, "sims"), P("blk", "sims")),
        check_vma=False,
    )
```

```python
import functools

import jax
import jax.numpy as jnp
from jax import lax
from jax.experimental import pallas as pl
from jax.experimental.pallas import tpu as pltpu
from jax.sharding import PartitionSpec as P

NDIST = 256
F32 = jnp.float32
B16 = jnp.bfloat16
SMEM_SPEC = pl.BlockSpec(memory_space=pltpu.SMEM)
VMEM_SPEC = pl.BlockSpec(memory_space=pltpu.VMEM)
HBM_SPEC = pl.BlockSpec(memory_space=pltpu.HBM)


def params(mib):
    return pltpu.CompilerParams(vmem_limit_bytes=mib * 1024 * 1024)


def cost(flops, moved):
    return pl.CostEstimate(flops=flops, bytes_accessed=moved, transcendentals=0)


def shaped(*shape, dtype=F32):
    return jax.ShapeDtypeStruct(shape, dtype)


def halves(x):
    hi = x.astype(B16)
    lo = (x - hi.astype(F32)).astype(B16)
    return hi, lo


def dot(a, b):
    return jnp.dot(a, b, preferred_element_type=F32)


def dot3(x, y):
    rows = x[0].shape[0]
    both = dot(jnp.concatenate([x[0], x[1]], axis=0), y[0])
    return both[:rows] + both[rows:] + dot(x[0], y[1])


def packed_places(slots, bs, columns):
    rhs_at = (slots + 1) * bs
    col_at = rhs_at + columns
    turnout_at = col_at + 8 * slots
    district_at = turnout_at + 8
    return rhs_at, col_at, turnout_at, district_at, district_at + 8


def chip_now():
    return lax.div(lax.axis_index("blk").astype(jnp.int32), 2)


def upper_here():
    return lax.rem(lax.axis_index("blk").astype(jnp.int32), 2) == 1


def pack_kernel(rows, cols, turnout, district, l_ref, d_ref, r_ref, *refs):
    outs = refs[: len(rows)]
    held, sems = refs[len(rows) :]
    slots, bs = l_ref.shape[2], l_ref.shape[3]
    columns = r_ref.shape[3]
    rhs_at, col_at, turnout_at, district_at, _ = packed_places(slots, bs, columns)
    copies = []

    def copy(source, target):
        copies.append(pltpu.make_async_copy(source, target, sems.at[len(copies)]))
        copies[-1].start()

    for i, r in enumerate(rows):
        copy(r_ref.at[r, 0], held.at[i])
    for out, r in zip(outs, rows):
        for k in range(slots):
            copy(l_ref.at[r, 0, k], out.at[pl.ds(k * bs, bs)])
        copy(d_ref.at[r, 0], out.at[pl.ds(slots * bs, bs)])
    for out, r in zip(outs, rows):
        for k in range(slots):
            at = col_at + 8 * k
            out[at : at + 8] = jnp.full((8, bs), cols[k, 0, r].astype(F32))
        out[turnout_at : turnout_at + 8] = jnp.broadcast_to(turnout[r], (8, bs))
        out[district_at : district_at + 8] = jnp.broadcast_to(
            district[r].astype(F32), (8, bs)
        )
    for i, out in enumerate(outs):
        copies[i].wait()
        out[rhs_at:col_at] = held[i].T
    for started in copies[len(rows) :]:
        started.wait()


def put(high, low, i, j, value):
    bs = value.shape[0]
    hi, lo = halves(value)
    high[i * bs : (i + 1) * bs, j * bs : (j + 1) * bs] = hi
    low[i * bs : (i + 1) * bs, j * bs : (j + 1) * bs] = lo


def blocks_of(r, n, slots, columns, own, oth):
    is_a = upper_here()
    bs = own.shape[1]
    _, col_at, _, _, _ = packed_places(slots, bs, columns)
    row_b = r * n + 2 * chip_now()
    row_a = row_b + 1

    def upper(at, size):
        return jnp.where(is_a, own[at : at + size], oth[at : at + size])

    def lower(at, size):
        return jnp.where(is_a, oth[at : at + size], own[at : at + size])

    def at_distance(side, row, d):
        found = jnp.zeros((bs, bs), F32)
        column = (row - d).astype(F32)
        for k in range(1, slots):
            col = side(col_at + 8 * k, 1)
            here = (col == column) & (col >= 0.0)
            found = jnp.where(here, side(k * bs, bs), found)
        return halves(found)

    return upper, lower, lambda d: at_distance(upper, row_a, d), lambda d: at_distance(lower, row_b, d)


def near_setup_kernel(r, n, slots, columns, own, oth, gh, gl, mh, ml, rt):
    bs = own.shape[1]
    half = columns // 2
    rhs_at, col_at, _, _, _ = packed_places(slots, bs, columns)
    upper, lower, upper_at, lower_at = blocks_of(r, n, slots, columns, own, oth)
    is_a = upper_here()
    da, db = halves(upper(slots * bs, bs)), halves(lower(slots * bs, bs))
    la1 = halves(upper(0, bs))
    lb1 = halves(jnp.where(lower(col_at, 1) >= 0.0, lower(0, bs), 0.0))
    w = dot3(da, la1)
    wh = halves(w)
    for place, pair in enumerate((da, db, la1, wh)):
        mh[place] = pair[0]
        ml[place] = pair[1]
    for j, (la, lb) in enumerate(((upper_at(2), lb1), (upper_at(3), lower_at(2)))):
        from_b = dot3(db, lb)
        put(gh, gl, 1, j, from_b)
        put(gh, gl, 0, j, dot3(da, la) - dot3(wh, halves(from_b)))
    ra, rb = upper(rhs_at, columns), lower(rhs_at, columns)
    rt[:, :bs] = jnp.where(is_a, ra[half:], ra[:half])
    rt[:, bs:] = jnp.where(is_a, rb[half:], rb[:half])


def far_setup_kernel(r, n, slots, columns, own, oth, mh, ml, fh, fl):
    _, _, upper_at, lower_at = blocks_of(r, n, slots, columns, own, oth)
    da, db, w = ((mh[k], ml[k]) for k in (0, 1, 3))
    for j, lb in enumerate((lower_at(3), lower_at(4))):
        from_b = dot3(db, lb)
        put(fh, fl, 1, j, from_b)
        from_a = -dot3(w, halves(from_b))
        if j == 0:
            from_a = from_a + dot3(da, upper_at(4))
        put(fh, fl, 0, j, from_a)


def place_of(lead, pairs, pieces):
    ahead = lax.rem(chip_now() - lead % pairs + pairs, pairs)
    piece = jnp.minimum(lax.div(ahead, 2), pieces - 1)
    return piece, lead + ahead


def choose(choices, pair, split, run):
    if len(choices) == 1:
        run(*choices[0])
        return

    @pl.when(pair < split)
    def _():
        run(*choices[0])

    @pl.when(pair >= split)
    def _():
        run(*choices[1])


def near_kernel(lead, pairs, pieces, split, ordered, received, has_near, *refs):
    refs = refs[ordered:]
    taken = refs[:received]
    outs = refs[-2:] if has_near else refs[-1:]
    refs = refs[received : -len(outs)]
    each = 3 if has_near else 1
    choices = [refs[i : i + each] for i in range(0, len(refs), each)]
    v_out = outs[0]
    width = v_out.shape[0]
    piece, pair = place_of(lead, pairs, pieces)
    rows = pl.ds(pl.multiple_of(piece * width, width), width)

    def run(rt, gh=None, gl=None):
        v = rt[rows, :]
        for x in taken:
            v = v - x[...]
        v_out[...] = v
        if has_near:
            outs[1][...] = dot3(halves(v), (gh[...], gl[...]))

    choose(choices, pair, split, run)


def far_kernel(lead, pairs, pieces, split, v_ref, *refs):
    out = refs[-1]
    refs = refs[:-1]
    _, pair = place_of(lead, pairs, pieces)

    def run(fh, fl):
        out[...] = dot3(halves(v_ref[...]), (fh[...], fl[...]))

    choose([refs[i : i + 2] for i in range(0, len(refs), 2)], pair, split, run)


def finish_kernel(slots, pairs, pieces, window, has_total, is_last, *refs):
    values = refs[:window]
    mh, ml, own, oth = refs[window : window + 4]
    refs = refs[window + 4 :]
    start = refs[0][...] if has_total else None
    keep, give, *outs = refs[1:] if has_total else refs
    chip, is_a = chip_now(), upper_here()
    bs = mh.shape[1]
    half = keep.shape[0]
    _, _, turnout_at, district_at, _ = packed_places(slots, bs, 2 * half)
    parts = []
    for m in range(pieces):
        v = values[pairs - 1 + 2 * m][...]
        for q in range(1, pairs):
            v = jnp.where(chip == q, values[pairs - 1 - q + 2 * m][...], v)
        parts.append(v)
    v = jnp.concatenate(parts, axis=0)

    def m(k):
        return mh[k], ml[k]

    xa = dot3(halves(v[:, :bs]), m(0))
    xb = dot3(halves(v[:, bs:] - dot3(halves(xa), m(2))), m(1))
    kept, given = jnp.where(is_a, xa, xb), jnp.where(is_a, xb, xa)
    keep[...] = kept
    give[...] = given
    names = lax.broadcasted_iota(jnp.int32, (NDIST, bs), 0).astype(F32)
    sums = jnp.zeros((NDIST, 2 * half), F32) if start is None else start
    for x, pack in ((kept, own), (given, oth)):
        weight = pack[turnout_at : turnout_at + 1]
        member = names == pack[district_at : district_at + 1]
        member = member.astype(F32).astype(B16)
        terms = jnp.concatenate([x * weight, jnp.broadcast_to(weight, (half, bs))], axis=0)
        for part in halves(terms):
            sums = sums + lax.dot_general(
                member, part, (((1,), (1,)), ((), ())), preferred_element_type=F32
            )
    if not is_last:
        outs[0][...] = sums
        return
    held = outs.pop()
    held[...] = sums
    rows = NDIST // pairs
    for by, part in enumerate(outs):
        to = lax.rem(chip + by, pairs)
        part[...] = held[pl.ds(pl.multiple_of(to * rows, rows), rows), :]


def add_kernel(*refs):
    mine, theirs = refs[-2:]
    total = refs[0][...]
    for part in refs[1:-2]:
        total = total + part[...]
    rows = mine.shape[0]
    is_a = upper_here()
    mine[...] = jnp.where(is_a, total[rows:], total[:rows])
    theirs[...] = jnp.where(is_a, total[:rows], total[rows:])


def mean_kernel(mine, got, out):
    half = out.shape[1] // 2
    own, oth = (x[:, :half] / x[:, half:] for x in (mine, got))
    is_a = upper_here()
    out[...] = jnp.concatenate(
        [jnp.where(is_a, oth, own), jnp.where(is_a, own, oth)], axis=1
    )


def field_kernel(rows_here, *refs):
    keeps = refs[:rows_here]
    gots = refs[rows_here : 2 * rows_here]
    out = refs[2 * rows_here]
    is_a = upper_here()
    for r in range(rows_here):
        top = jnp.where(is_a, gots[r][...], keeps[r][...])
        bottom = jnp.where(is_a, keeps[r][...], gots[r][...])
        out[r, 0] = jnp.concatenate([top, bottom], axis=0).T


def body(rhs, lower_blocks, col_index, diag_inverse, turnout, district_of):
    n = lax.axis_size("blk")
    pairs = n // 2
    pieces = 1
    rows_here, _, bs, columns = rhs.shape
    slots = lower_blocks.shape[2]
    half = columns // 2
    width = half // pieces
    count = rows_here * pairs
    packed_rows = packed_places(slots, bs, columns)[-1]
    wide = shaped(width, 2 * bs)
    square = shaped(2 * bs, 2 * bs, dtype=B16)

    def call(kernel, name, outs, operands, mib, flops=0, moved=0, **more):
        several = isinstance(outs, tuple)
        return pl.pallas_call(
            kernel,
            out_shape=outs,
            in_specs=more.pop("in_specs", [VMEM_SPEC] * len(operands)),
            out_specs=(VMEM_SPEC,) * len(outs) if several else VMEM_SPEC,
            compiler_params=params(mib),
            cost_estimate=cost(flops, moved),
            name=name,
            **more,
        )(*operands)

    def swap(x):
        return lax.ppermute(x, "blk", [(i, i ^ 1) for i in range(n)])

    def shift(x, by):
        return lax.ppermute(x, "blk", [(i, (i + 2 * by) % n) for i in range(n)])

    def pass_on(x, lead, by):
        perm = []
        for k in range(lead, lead + 2 * pieces, 2):
            if by <= k < count:
                sender, target = k % pairs, (k - by) % pairs
                perm += [(2 * sender + c, 2 * target + c) for c in range(2)]
        return lax.ppermute(x, "blk", perm)

    def pack(rows, turnout=turnout):
        return call(
            functools.partial(pack_kernel, rows),
            "pack",
            (shaped(packed_rows, bs),) * len(rows),
            (jnp.transpose(col_index, (2, 1, 0)), turnout, district_of, lower_blocks, diag_inverse, rhs),
            56,
            moved=8 * packed_rows * bs * len(rows),
            in_specs=[SMEM_SPEC, VMEM_SPEC, VMEM_SPEC] + [HBM_SPEC] * 3,
            scratch_shapes=[
                pltpu.VMEM((len(rows), bs, columns), F32),
                pltpu.SemaphoreType.DMA((len(rows) * (slots + 2),)),
            ],
        )

    def setup(r):
        args = (r, n, slots, columns)
        held = shaped(4, bs, bs, dtype=B16)
        gh, gl, mh, ml, rt = call(
            functools.partial(near_setup_kernel, *args),
            "near_setup",
            (square, square, held, held, shaped(half, 2 * bs)),
            packs[r],
            10,
            14 * 3 * bs**3,
            24 * bs * bs * 4,
        )
        fh, fl = call(
            functools.partial(far_setup_kernel, *args),
            "far_setup",
            (square, square),
            (*packs[r], mh, ml),
            10,
            10 * 3 * bs**3,
            24 * bs * bs * 4,
        )
        return gh, gl, mh, ml, rt, fh, fl

    def finish(r, values, total):
        first = count - 1 - (r * pairs + pairs - 1)
        window = values[first : first + pairs + 2 * (pieces - 1)]
        is_last = r == 0
        outs = (shaped(half, bs), shaped(half, bs))
        outs += (shaped(NDIST // pairs, columns),) * pairs if is_last else (shaped(NDIST, columns),)
        extra = () if total is None else (total,)
        return call(
            functools.partial(
                finish_kernel, slots, pairs, pieces, len(window), total is not None, is_last
            ),
            "finish",
            outs,
            (*window, *fixed[r][2:4], *packs[r], *extra),
            8,
            6 * 3 * half * bs * bs,
            16 * bs * bs,
            scratch_shapes=[pltpu.VMEM((NDIST, columns), F32)] if is_last else [],
        )

    top = rows_here - 1
    packs, fixed = {}, {}
    (own,) = pack((top,))
    packs[top] = (own, swap(own))
    later, _ = lax.optimization_barrier((turnout, own))
    packed = pack(tuple(range(top)), later) if top else ()
    for r in range(top - 1, -1, -1):
        packs[r] = (packed[r], swap(packed[r]))
    fixed[top] = setup(top)

    keeps, gots = {}, {}
    values = []
    ordered = ()
    total = near = far_now = far_next = None
    steps = count + 2 * (pieces - 1)
    for step in range(steps):
        lead = count - 1 - step
        low = max(lead, 0) // pairs
        high = min(lead + 2 * (pieces - 1), count - 1) // pairs
        rows = range(low, high + 1)
        taken = [x for x in (far_now, near) if x is not None]
        has_near = step + 1 < steps
        has_far = step + 2 < steps
        operands = []
        for r in rows:
            gh, gl, _, _, rt, _, _ = fixed[r]
            operands += [rt, gh, gl] if has_near else [rt]
        place = (lead, pairs, pieces, high * pairs)
        v, *near_out = call(
            functools.partial(near_kernel, *place, len(ordered), len(taken), has_near),
            "near_terms",
            (wide, wide) if has_near else (wide,),
            (*ordered, *taken, *operands),
            4,
            6 * width * 4 * bs * bs,
            6 * width * bs * 4,
        )
        values.append(v)
        near = pass_on(near_out[0], lead, 1) if has_near else None
        far_now, far_next, ordered = far_next, None, ()
        if has_far:
            operands = [x for r in rows for x in fixed[r][5:]]
            far_out = call(
                functools.partial(far_kernel, *place),
                "far_terms",
                wide,
                (v, *operands),
                4,
                6 * width * 4 * bs * bs,
                6 * width * bs * 4,
            )
            ordered = (far_out,)
            r, chip = lead // pairs, lead % pairs
            if chip == pairs - 1 and r > 0:
                fixed[r - 1] = setup(r - 1)
            far_next = pass_on(far_out, lead, 2)
        done = lead + 2 * (pieces - 1)
        if done % pairs == 0 and 0 < done // pairs <= top:
            r = done // pairs
            keeps[r], give, total = finish(r, values, total)
            gots[r] = swap(give)
            near, total = lax.optimization_barrier((near, total))

    keeps[0], give, *parts = finish(0, values, total)
    gots[0] = swap(give)
    parts = [parts[0]] + [shift(parts[by], by) for by in range(1, pairs)]
    order = range(rows_here)
    field = call(
        functools.partial(field_kernel, rows_here),
        "field",
        shaped(rows_here, 1, bs, columns),
        (*[keeps[r] for r in order], *[gots[r] for r in order]),
        4,
        0,
        8 * rows_here * bs * columns,
    )
    parts, field = lax.optimization_barrier((parts, field))
    held = shaped(NDIST // n, columns)
    mine, theirs = call(add_kernel, "district_add", (held, held), tuple(parts), 4)
    mean = call(mean_kernel, "district_mean", held, (mine, swap(theirs)), 4)
    return field, mean


def solution(mesh):
    placed = (
        P(None, "blk", None, "sims"),
        P(None, "blk", None, None, None),
        P(None, "blk", None),
        P(None, "blk", None, None),
        P(None, "blk", None),
        P(None, "blk", None),
    )
    return jax.shard_map(
        body,
        mesh=mesh,
        in_specs=placed,
        out_specs=(P(None, "blk", None, "sims"), P("blk", "sims")),
        check_vma=False,
    )
```

```python
import functools

import jax
import jax.numpy as jnp
from jax import lax
from jax.experimental import pallas as pl
from jax.experimental.pallas import tpu as pltpu
from jax.sharding import PartitionSpec as P

NDIST = 256
F32 = jnp.float32
B16 = jnp.bfloat16
SMEM_SPEC = pl.BlockSpec(memory_space=pltpu.SMEM)
VMEM_SPEC = pl.BlockSpec(memory_space=pltpu.VMEM)
HBM_SPEC = pl.BlockSpec(memory_space=pltpu.HBM)


def params(mib):
    return pltpu.CompilerParams(vmem_limit_bytes=mib * 1024 * 1024)


def cost(flops, moved):
    return pl.CostEstimate(flops=flops, bytes_accessed=moved, transcendentals=0)


def shaped(*shape, dtype=F32):
    return jax.ShapeDtypeStruct(shape, dtype)


def halves(x):
    hi = x.astype(B16)
    lo = (x - hi.astype(F32)).astype(B16)
    return hi, lo


def dot(a, b):
    return jnp.dot(a, b, preferred_element_type=F32)


def dot3(x, y):
    rows = x[0].shape[0]
    both = dot(jnp.concatenate([x[0], x[1]], axis=0), y[0])
    return both[:rows] + both[rows:] + dot(x[0], y[1])


def packed_places(slots, bs, columns):
    rhs_at = (slots + 1) * bs
    col_at = rhs_at + columns
    turnout_at = col_at + 8 * slots
    district_at = turnout_at + 8
    return rhs_at, col_at, turnout_at, district_at, district_at + 8


def chip_now():
    return lax.div(lax.axis_index("blk").astype(jnp.int32), 2)


def upper_here():
    return lax.rem(lax.axis_index("blk").astype(jnp.int32), 2) == 1


def pack_kernel(rows, cols, turnout, district, l_ref, d_ref, r_ref, *refs):
    outs = refs[: len(rows)]
    held, sems = refs[len(rows) :]
    slots, bs = l_ref.shape[2], l_ref.shape[3]
    columns = r_ref.shape[3]
    rhs_at, col_at, turnout_at, district_at, _ = packed_places(slots, bs, columns)
    copies = []

    def copy(source, target):
        copies.append(pltpu.make_async_copy(source, target, sems.at[len(copies)]))
        copies[-1].start()

    for i, r in enumerate(rows):
        copy(r_ref.at[r, 0], held.at[i])
    for out, r in zip(outs, rows):
        for k in range(slots):
            copy(l_ref.at[r, 0, k], out.at[pl.ds(k * bs, bs)])
        copy(d_ref.at[r, 0], out.at[pl.ds(slots * bs, bs)])
    for out, r in zip(outs, rows):
        for k in range(slots):
            at = col_at + 8 * k
            out[at : at + 8] = jnp.full((8, bs), cols[k, 0, r].astype(F32))
        out[turnout_at : turnout_at + 8] = jnp.broadcast_to(turnout[r], (8, bs))
        out[district_at : district_at + 8] = jnp.broadcast_to(
            district[r].astype(F32), (8, bs)
        )
    for i, out in enumerate(outs):
        copies[i].wait()
        out[rhs_at:col_at] = held[i].T
    for started in copies[len(rows) :]:
        started.wait()


def put(high, low, i, j, value):
    bs = value.shape[0]
    hi, lo = halves(value)
    high[i * bs : (i + 1) * bs, j * bs : (j + 1) * bs] = hi
    low[i * bs : (i + 1) * bs, j * bs : (j + 1) * bs] = lo


def blocks_of(r, n, slots, columns, own, oth):
    is_a = upper_here()
    bs = own.shape[1]
    _, col_at, _, _, _ = packed_places(slots, bs, columns)
    row_b = r * n + 2 * chip_now()
    row_a = row_b + 1

    def upper(at, size):
        return jnp.where(is_a, own[at : at + size], oth[at : at + size])

    def lower(at, size):
        return jnp.where(is_a, oth[at : at + size], own[at : at + size])

    def at_distance(side, row, d):
        found = jnp.zeros((bs, bs), F32)
        column = (row - d).astype(F32)
        for k in range(1, slots):
            col = side(col_at + 8 * k, 1)
            here = (col == column) & (col >= 0.0)
            found = jnp.where(here, side(k * bs, bs), found)
        return halves(found)

    return upper, lower, lambda d: at_distance(upper, row_a, d), lambda d: at_distance(lower, row_b, d)


def near_setup_kernel(r, n, slots, columns, own, oth, gh, gl, mh, ml, rt):
    bs = own.shape[1]
    half = columns // 2
    rhs_at, col_at, _, _, _ = packed_places(slots, bs, columns)
    upper, lower, upper_at, lower_at = blocks_of(r, n, slots, columns, own, oth)
    is_a = upper_here()
    da, db = halves(upper(slots * bs, bs)), halves(lower(slots * bs, bs))
    la1 = halves(upper(0, bs))
    lb1 = halves(jnp.where(lower(col_at, 1) >= 0.0, lower(0, bs), 0.0))
    w = dot3(da, la1)
    wh = halves(w)
    for place, pair in enumerate((da, db, la1, wh)):
        mh[place] = pair[0]
        ml[place] = pair[1]
    for j, (la, lb) in enumerate(((upper_at(2), lb1), (upper_at(3), lower_at(2)))):
        from_b = dot3(db, lb)
        put(gh, gl, 1, j, from_b)
        put(gh, gl, 0, j, dot3(da, la) - dot3(wh, halves(from_b)))
    ra, rb = upper(rhs_at, columns), lower(rhs_at, columns)
    rt[:, :bs] = jnp.where(is_a, ra[half:], ra[:half])
    rt[:, bs:] = jnp.where(is_a, rb[half:], rb[:half])


def far_setup_kernel(r, n, slots, columns, own, oth, mh, ml, fh, fl):
    _, _, upper_at, lower_at = blocks_of(r, n, slots, columns, own, oth)
    da, db, w = ((mh[k], ml[k]) for k in (0, 1, 3))
    for j, lb in enumerate((lower_at(3), lower_at(4))):
        from_b = dot3(db, lb)
        put(fh, fl, 1, j, from_b)
        from_a = -dot3(w, halves(from_b))
        if j == 0:
            from_a = from_a + dot3(da, upper_at(4))
        put(fh, fl, 0, j, from_a)


def place_of(lead, pairs, pieces):
    ahead = lax.rem(chip_now() - lead % pairs + pairs, pairs)
    piece = jnp.minimum(lax.div(ahead, 2), pieces - 1)
    return piece, lead + ahead


def choose(choices, pair, split, run):
    if len(choices) == 1:
        run(*choices[0])
        return

    @pl.when(pair < split)
    def _():
        run(*choices[0])

    @pl.when(pair >= split)
    def _():
        run(*choices[1])


def near_kernel(lead, pairs, pieces, split, ordered, received, has_near, *refs):
    refs = refs[ordered:]
    taken = refs[:received]
    outs = refs[-2:] if has_near else refs[-1:]
    refs = refs[received : -len(outs)]
    each = 3 if has_near else 1
    choices = [refs[i : i + each] for i in range(0, len(refs), each)]
    v_out = outs[0]
    width = v_out.shape[0]
    piece, pair = place_of(lead, pairs, pieces)
    rows = pl.ds(pl.multiple_of(piece * width, width), width)

    def run(rt, gh=None, gl=None):
        v = rt[rows, :]
        for x in taken:
            v = v - x[...]
        v_out[...] = v
        if has_near:
            outs[1][...] = dot3(halves(v), (gh[...], gl[...]))

    choose(choices, pair, split, run)


def far_kernel(lead, pairs, pieces, split, v_ref, *refs):
    out = refs[-1]
    refs = refs[:-1]
    _, pair = place_of(lead, pairs, pieces)

    def run(fh, fl):
        out[...] = dot3(halves(v_ref[...]), (fh[...], fl[...]))

    choose([refs[i : i + 2] for i in range(0, len(refs), 2)], pair, split, run)


def finish_kernel(slots, pairs, pieces, window, has_total, is_last, *refs):
    values = refs[:window]
    mh, ml, own, oth = refs[window : window + 4]
    refs = refs[window + 4 :]
    start = refs[0][...] if has_total else None
    keep, give, *outs = refs[1:] if has_total else refs
    chip, is_a = chip_now(), upper_here()
    bs = mh.shape[1]
    half = keep.shape[0]
    _, _, turnout_at, district_at, _ = packed_places(slots, bs, 2 * half)
    parts = []
    for m in range(pieces):
        v = values[pairs - 1 + 2 * m][...]
        for q in range(1, pairs):
            v = jnp.where(chip == q, values[pairs - 1 - q + 2 * m][...], v)
        parts.append(v)
    v = jnp.concatenate(parts, axis=0)

    def m(k):
        return mh[k], ml[k]

    xa = dot3(halves(v[:, :bs]), m(0))
    xb = dot3(halves(v[:, bs:] - dot3(halves(xa), m(2))), m(1))
    kept, given = jnp.where(is_a, xa, xb), jnp.where(is_a, xb, xa)
    keep[...] = kept
    give[...] = given
    names = lax.broadcasted_iota(jnp.int32, (NDIST, bs), 0).astype(F32)
    sums = jnp.zeros((NDIST, 2 * half), F32) if start is None else start
    for x, pack in ((kept, own), (given, oth)):
        weight = pack[turnout_at : turnout_at + 1]
        member = names == pack[district_at : district_at + 1]
        member = member.astype(F32).astype(B16)
        terms = jnp.concatenate([x * weight, jnp.broadcast_to(weight, (half, bs))], axis=0)
        for part in halves(terms):
            sums = sums + lax.dot_general(
                member, part, (((1,), (1,)), ((), ())), preferred_element_type=F32
            )
    if not is_last:
        outs[0][...] = sums
        return
    held = outs.pop()
    held[...] = sums
    rows = NDIST // pairs
    for by, part in enumerate(outs):
        to = lax.rem(chip + by, pairs)
        part[...] = held[pl.ds(pl.multiple_of(to * rows, rows), rows), :]


def add_kernel(*refs):
    mine, theirs = refs[-2:]
    total = refs[0][...]
    for part in refs[1:-2]:
        total = total + part[...]
    rows = mine.shape[0]
    is_a = upper_here()
    mine[...] = jnp.where(is_a, total[rows:], total[:rows])
    theirs[...] = jnp.where(is_a, total[:rows], total[rows:])


def mean_kernel(mine, got, out):
    half = out.shape[1] // 2
    own, oth = (x[:, :half] / x[:, half:] for x in (mine, got))
    is_a = upper_here()
    out[...] = jnp.concatenate(
        [jnp.where(is_a, oth, own), jnp.where(is_a, own, oth)], axis=1
    )


def field_kernel(rows_here, *refs):
    keeps = refs[:rows_here]
    gots = refs[rows_here : 2 * rows_here]
    out = refs[2 * rows_here]
    is_a = upper_here()
    for r in range(rows_here):
        top = jnp.where(is_a, gots[r][...], keeps[r][...])
        bottom = jnp.where(is_a, keeps[r][...], gots[r][...])
        out[r, 0] = jnp.concatenate([top, bottom], axis=0).T


def body(rhs, lower_blocks, col_index, diag_inverse, turnout, district_of):
    n = lax.axis_size("blk")
    pairs = n // 2
    pieces = 1
    rows_here, _, bs, columns = rhs.shape
    slots = lower_blocks.shape[2]
    half = columns // 2
    width = half // pieces
    count = rows_here * pairs
    packed_rows = packed_places(slots, bs, columns)[-1]
    wide = shaped(width, 2 * bs)
    square = shaped(2 * bs, 2 * bs, dtype=B16)

    def call(kernel, name, outs, operands, mib, flops=0, moved=0, **more):
        several = isinstance(outs, tuple)
        return pl.pallas_call(
            kernel,
            out_shape=outs,
            in_specs=more.pop("in_specs", [VMEM_SPEC] * len(operands)),
            out_specs=(VMEM_SPEC,) * len(outs) if several else VMEM_SPEC,
            compiler_params=params(mib),
            cost_estimate=cost(flops, moved),
            name=name,
            **more,
        )(*operands)

    def swap(x):
        return lax.ppermute(x, "blk", [(i, i ^ 1) for i in range(n)])

    def shift(x, by):
        return lax.ppermute(x, "blk", [(i, (i + 2 * by) % n) for i in range(n)])

    def pass_on(x, lead, by):
        ring = [(lead - i) % pairs for i in range(0, 3, by)]
        target = {q: q for q in range(pairs)}
        target.update(zip(ring, ring[1:] + ring[:1]))
        perm = [(2 * q + c, 2 * to + c) for q, to in target.items() for c in range(2)]
        return lax.ppermute(x, "blk", perm)

    def pack(rows, turnout=turnout):
        return call(
            functools.partial(pack_kernel, rows),
            "pack",
            (shaped(packed_rows, bs),) * len(rows),
            (jnp.transpose(col_index, (2, 1, 0)), turnout, district_of, lower_blocks, diag_inverse, rhs),
            56,
            moved=8 * packed_rows * bs * len(rows),
            in_specs=[SMEM_SPEC, VMEM_SPEC, VMEM_SPEC] + [HBM_SPEC] * 3,
            scratch_shapes=[
                pltpu.VMEM((len(rows), bs, columns), F32),
                pltpu.SemaphoreType.DMA((len(rows) * (slots + 2),)),
            ],
        )

    def setup(r):
        args = (r, n, slots, columns)
        held = shaped(4, bs, bs, dtype=B16)
        gh, gl, mh, ml, rt = call(
            functools.partial(near_setup_kernel, *args),
            "near_setup",
            (square, square, held, held, shaped(half, 2 * bs)),
            packs[r],
            10,
            14 * 3 * bs**3,
            24 * bs * bs * 4,
        )
        fh, fl = call(
            functools.partial(far_setup_kernel, *args),
            "far_setup",
            (square, square),
            (*packs[r], mh, ml),
            10,
            10 * 3 * bs**3,
            24 * bs * bs * 4,
        )
        return gh, gl, mh, ml, rt, fh, fl

    def finish(r, values, total):
        first = count - 1 - (r * pairs + pairs - 1)
        window = values[first : first + pairs + 2 * (pieces - 1)]
        is_last = r == 0
        outs = (shaped(half, bs), shaped(half, bs))
        outs += (shaped(NDIST // pairs, columns),) * pairs if is_last else (shaped(NDIST, columns),)
        extra = () if total is None else (total,)
        return call(
            functools.partial(
                finish_kernel, slots, pairs, pieces, len(window), total is not None, is_last
            ),
            "finish",
            outs,
            (*window, *fixed[r][2:4], *packs[r], *extra),
            8,
            6 * 3 * half * bs * bs,
            16 * bs * bs,
            scratch_shapes=[pltpu.VMEM((NDIST, columns), F32)] if is_last else [],
        )

    top = rows_here - 1
    packs, fixed = {}, {}
    (own,) = pack((top,))
    packs[top] = (own, swap(own))
    later, _ = lax.optimization_barrier((turnout, own))
    packed = pack(tuple(range(top)), later) if top else ()
    for r in range(top - 1, -1, -1):
        packs[r] = (packed[r], swap(packed[r]))
    fixed[top] = setup(top)

    keeps, gots = {}, {}
    values = []
    ordered = ()
    total = near = far_now = far_next = None
    steps = count + 2 * (pieces - 1)
    for step in range(steps):
        lead = count - 1 - step
        low = max(lead, 0) // pairs
        high = min(lead + 2 * (pieces - 1), count - 1) // pairs
        rows = range(low, high + 1)
        taken = [x for x in (far_now, near) if x is not None]
        has_near = step + 1 < steps
        has_far = step + 2 < steps
        operands = []
        for r in rows:
            gh, gl, _, _, rt, _, _ = fixed[r]
            operands += [rt, gh, gl] if has_near else [rt]
        place = (lead, pairs, pieces, high * pairs)
        v, *near_out = call(
            functools.partial(near_kernel, *place, len(ordered), len(taken), has_near),
            "near_terms",
            (wide, wide) if has_near else (wide,),
            (*ordered, *taken, *operands),
            4,
            6 * width * 4 * bs * bs,
            6 * width * bs * 4,
        )
        values.append(v)
        near = pass_on(near_out[0], lead, 1) if has_near else None
        far_now, far_next, ordered = far_next, None, ()
        if has_far:
            operands = [x for r in rows for x in fixed[r][5:]]
            far_out = call(
                functools.partial(far_kernel, *place),
                "far_terms",
                wide,
                (v, *operands),
                4,
                6 * width * 4 * bs * bs,
                6 * width * bs * 4,
            )
            ordered = (far_out,)
            r, chip = lead // pairs, lead % pairs
            if chip == pairs - 1 and r > 0:
                fixed[r - 1] = setup(r - 1)
            far_next = pass_on(far_out, lead, 2)
        done = lead + 2 * (pieces - 1)
        if done % pairs == 0 and 0 < done // pairs <= top:
            r = done // pairs
            keeps[r], give, total = finish(r, values, total)
            gots[r] = swap(give)
            near, total = lax.optimization_barrier((near, total))

    keeps[0], give, *parts = finish(0, values, total)
    gots[0] = swap(give)
    parts = [parts[0]] + [shift(parts[by], by) for by in range(1, pairs)]
    order = range(rows_here)
    field = call(
        functools.partial(field_kernel, rows_here),
        "field",
        shaped(rows_here, 1, bs, columns),
        (*[keeps[r] for r in order], *[gots[r] for r in order]),
        4,
        0,
        8 * rows_here * bs * columns,
    )
    parts, field = lax.optimization_barrier((parts, field))
    held = shaped(NDIST // n, columns)
    mine, theirs = call(add_kernel, "district_add", (held, held), tuple(parts), 4)
    mean = call(mean_kernel, "district_mean", held, (mine, swap(theirs)), 4)
    return field, mean


def solution(mesh):
    placed = (
        P(None, "blk", None, "sims"),
        P(None, "blk", None, None, None),
        P(None, "blk", None),
        P(None, "blk", None, None),
        P(None, "blk", None),
        P(None, "blk", None),
    )
    return jax.shard_map(
        body,
        mesh=mesh,
        in_specs=placed,
        out_specs=(P(None, "blk", None, "sims"), P("blk", "sims")),
        check_vma=False,
    )
```

```python
import functools

import jax
import jax.numpy as jnp
from jax import lax
from jax.experimental import pallas as pl
from jax.experimental.pallas import tpu as pltpu
from jax.sharding import PartitionSpec as P

NDIST = 256
F32 = jnp.float32
B16 = jnp.bfloat16
SMEM_SPEC = pl.BlockSpec(memory_space=pltpu.SMEM)
VMEM_SPEC = pl.BlockSpec(memory_space=pltpu.VMEM)
HBM_SPEC = pl.BlockSpec(memory_space=pltpu.HBM)


def params(mib):
    return pltpu.CompilerParams(vmem_limit_bytes=mib * 1024 * 1024)


def cost(flops, moved):
    return pl.CostEstimate(flops=flops, bytes_accessed=moved, transcendentals=0)


def shaped(*shape, dtype=F32):
    return jax.ShapeDtypeStruct(shape, dtype)


def halves(x):
    hi = x.astype(B16)
    lo = (x - hi.astype(F32)).astype(B16)
    return hi, lo


def dot(a, b):
    return jnp.dot(a, b, preferred_element_type=F32)


def dot3(x, y):
    rows = x[0].shape[0]
    both = dot(jnp.concatenate([x[0], x[1]], axis=0), y[0])
    return both[:rows] + both[rows:] + dot(x[0], y[1])


def packed_places(slots, bs, columns):
    rhs_at = (slots + 1) * bs
    col_at = rhs_at + columns
    turnout_at = col_at + 8 * slots
    district_at = turnout_at + 8
    return rhs_at, col_at, turnout_at, district_at, district_at + 8


def chip_now():
    return lax.div(lax.axis_index("blk").astype(jnp.int32), 2)


def upper_here():
    return lax.rem(lax.axis_index("blk").astype(jnp.int32), 2) == 1


def pack_kernel(rows, cols, turnout, district, l_ref, d_ref, r_ref, *refs):
    outs = refs[: len(rows)]
    held, passing, sems = refs[len(rows) :]
    slots, bs = l_ref.shape[2], l_ref.shape[3]
    columns = r_ref.shape[3]
    rhs_at, col_at, turnout_at, district_at, end = packed_places(slots, bs, columns)
    places = [pl.ds(k * bs, bs) for k in range(slots + 1)]
    tail = pl.ds(rhs_at, end - rhs_at)
    made = []

    def copy(source, target):
        made.append(pltpu.make_async_copy(source, target, sems.at[len(made)]))
        made[-1].start()
        return made[-1]

    arrivals = []
    for i, r in enumerate(rows):
        blocks = [l_ref.at[r, 0, k] for k in range(slots)] + [d_ref.at[r, 0]]
        first = copy(r_ref.at[r, 0], held.at[i])
        rest = [copy(x, passing.at[i, at]) for x, at in zip(blocks, places)]
        arrivals.append((first, rest))
    for i, r in enumerate(rows):
        for k in range(slots):
            at = col_at + 8 * k
            passing[i, at : at + 8] = jnp.full((8, bs), cols[k, 0, r].astype(F32))
        passing[i, turnout_at : turnout_at + 8] = jnp.broadcast_to(turnout[r], (8, bs))
        passing[i, district_at : district_at + 8] = jnp.broadcast_to(
            district[r].astype(F32), (8, bs)
        )
    leaving = []
    for i, (first, rest) in enumerate(arrivals):
        first.wait()
        passing[i, rhs_at:col_at] = held[i].T
        leaving.append(copy(passing.at[i, tail], outs[i].at[tail]))
        for arriving, at in zip(rest, places):
            arriving.wait()
            leaving.append(copy(passing.at[i, at], outs[i].at[at]))
    for x in leaving:
        x.wait()


def put(high, low, i, j, value):
    bs = value.shape[0]
    hi, lo = halves(value)
    high[i * bs : (i + 1) * bs, j * bs : (j + 1) * bs] = hi
    low[i * bs : (i + 1) * bs, j * bs : (j + 1) * bs] = lo


def blocks_of(r, n, slots, columns, own, oth):
    is_a = upper_here()
    bs = own.shape[1]
    _, col_at, _, _, _ = packed_places(slots, bs, columns)
    row_b = r * n + 2 * chip_now()
    row_a = row_b + 1

    def upper(at, size):
        return jnp.where(is_a, own[at : at + size], oth[at : at + size])

    def lower(at, size):
        return jnp.where(is_a, oth[at : at + size], own[at : at + size])

    def at_distance(side, row, d):
        found = jnp.zeros((bs, bs), F32)
        column = (row - d).astype(F32)
        for k in range(1, slots):
            col = side(col_at + 8 * k, 1)
            here = (col == column) & (col >= 0.0)
            found = jnp.where(here, side(k * bs, bs), found)
        return halves(found)

    return upper, lower, lambda d: at_distance(upper, row_a, d), lambda d: at_distance(lower, row_b, d)


def near_setup_kernel(r, n, slots, columns, own, oth, gh, gl, mh, ml, rt):
    bs = own.shape[1]
    half = columns // 2
    rhs_at, col_at, _, _, _ = packed_places(slots, bs, columns)
    upper, lower, upper_at, lower_at = blocks_of(r, n, slots, columns, own, oth)
    is_a = upper_here()
    da, db = halves(upper(slots * bs, bs)), halves(lower(slots * bs, bs))
    la1 = halves(upper(0, bs))
    lb1 = halves(jnp.where(lower(col_at, 1) >= 0.0, lower(0, bs), 0.0))
    w = dot3(da, la1)
    wh = halves(w)
    for place, pair in enumerate((da, db, la1, wh)):
        mh[place] = pair[0]
        ml[place] = pair[1]
    for j, (la, lb) in enumerate(((upper_at(2), lb1), (upper_at(3), lower_at(2)))):
        from_b = dot3(db, lb)
        put(gh, gl, 1, j, from_b)
        put(gh, gl, 0, j, dot3(da, la) - dot3(wh, halves(from_b)))
    ra, rb = upper(rhs_at, columns), lower(rhs_at, columns)
    rt[:, :bs] = jnp.where(is_a, ra[half:], ra[:half])
    rt[:, bs:] = jnp.where(is_a, rb[half:], rb[:half])


def far_setup_kernel(r, n, slots, columns, own, oth, mh, ml, fh, fl):
    _, _, upper_at, lower_at = blocks_of(r, n, slots, columns, own, oth)
    da, db, w = ((mh[k], ml[k]) for k in (0, 1, 3))
    for j, lb in enumerate((lower_at(3), lower_at(4))):
        from_b = dot3(db, lb)
        put(fh, fl, 1, j, from_b)
        from_a = -dot3(w, halves(from_b))
        if j == 0:
            from_a = from_a + dot3(da, upper_at(4))
        put(fh, fl, 0, j, from_a)


def place_of(lead, pairs, pieces):
    ahead = lax.rem(chip_now() - lead % pairs + pairs, pairs)
    piece = jnp.minimum(lax.div(ahead, 2), pieces - 1)
    return piece, lead + ahead


def choose(choices, pair, split, run):
    if len(choices) == 1:
        run(*choices[0])
        return

    @pl.when(pair < split)
    def _():
        run(*choices[0])

    @pl.when(pair >= split)
    def _():
        run(*choices[1])


def near_kernel(lead, pairs, pieces, split, ordered, received, has_near, *refs):
    refs = refs[ordered:]
    taken = refs[:received]
    outs = refs[-2:] if has_near else refs[-1:]
    refs = refs[received : -len(outs)]
    each = 3 if has_near else 1
    choices = [refs[i : i + each] for i in range(0, len(refs), each)]
    v_out = outs[0]
    width = v_out.shape[0]
    piece, pair = place_of(lead, pairs, pieces)
    rows = pl.ds(pl.multiple_of(piece * width, width), width)

    def run(rt, gh=None, gl=None):
        v = rt[rows, :]
        for x in taken:
            v = v - x[...]
        v_out[...] = v
        if has_near:
            outs[1][...] = dot3(halves(v), (gh[...], gl[...]))

    choose(choices, pair, split, run)


def far_kernel(lead, pairs, pieces, split, v_ref, *refs):
    out = refs[-1]
    refs = refs[:-1]
    _, pair = place_of(lead, pairs, pieces)

    def run(fh, fl):
        out[...] = dot3(halves(v_ref[...]), (fh[...], fl[...]))

    choose([refs[i : i + 2] for i in range(0, len(refs), 2)], pair, split, run)


def finish_kernel(slots, pairs, pieces, window, has_total, is_last, *refs):
    values = refs[:window]
    mh, ml, own, oth = refs[window : window + 4]
    refs = refs[window + 4 :]
    start = refs[0][...] if has_total else None
    keep, give, *outs = refs[1:] if has_total else refs
    chip, is_a = chip_now(), upper_here()
    bs = mh.shape[1]
    half = keep.shape[0]
    _, _, turnout_at, district_at, _ = packed_places(slots, bs, 2 * half)
    parts = []
    for m in range(pieces):
        v = values[pairs - 1 + 2 * m][...]
        for q in range(1, pairs):
            v = jnp.where(chip == q, values[pairs - 1 - q + 2 * m][...], v)
        parts.append(v)
    v = jnp.concatenate(parts, axis=0)

    def m(k):
        return mh[k], ml[k]

    xa = dot3(halves(v[:, :bs]), m(0))
    xb = dot3(halves(v[:, bs:] - dot3(halves(xa), m(2))), m(1))
    kept, given = jnp.where(is_a, xa, xb), jnp.where(is_a, xb, xa)
    keep[...] = kept
    give[...] = given
    names = lax.broadcasted_iota(jnp.int32, (NDIST, bs), 0).astype(F32)
    sums = jnp.zeros((NDIST, 2 * half), F32) if start is None else start
    for x, pack in ((kept, own), (given, oth)):
        weight = pack[turnout_at : turnout_at + 1]
        member = names == pack[district_at : district_at + 1]
        member = member.astype(F32).astype(B16)
        terms = jnp.concatenate([x * weight, jnp.broadcast_to(weight, (half, bs))], axis=0)
        for part in halves(terms):
            sums = sums + lax.dot_general(
                member, part, (((1,), (1,)), ((), ())), preferred_element_type=F32
            )
    if not is_last:
        outs[0][...] = sums
        return
    held = outs.pop()
    held[...] = sums
    rows = NDIST // pairs
    for by, part in enumerate(outs):
        to = lax.rem(chip + by, pairs)
        part[...] = held[pl.ds(pl.multiple_of(to * rows, rows), rows), :]


def add_kernel(*refs):
    mine, theirs = refs[-2:]
    total = refs[0][...]
    for part in refs[1:-2]:
        total = total + part[...]
    rows = mine.shape[0]
    is_a = upper_here()
    mine[...] = jnp.where(is_a, total[rows:], total[:rows])
    theirs[...] = jnp.where(is_a, total[:rows], total[rows:])


def mean_kernel(mine, got, out):
    half = out.shape[1] // 2
    own, oth = (x[:, :half] / x[:, half:] for x in (mine, got))
    is_a = upper_here()
    out[...] = jnp.concatenate(
        [jnp.where(is_a, oth, own), jnp.where(is_a, own, oth)], axis=1
    )


def field_kernel(rows_here, *refs):
    keeps = refs[:rows_here]
    gots = refs[rows_here : 2 * rows_here]
    out = refs[2 * rows_here]
    is_a = upper_here()
    for r in range(rows_here):
        top = jnp.where(is_a, gots[r][...], keeps[r][...])
        bottom = jnp.where(is_a, keeps[r][...], gots[r][...])
        out[r, 0] = jnp.concatenate([top, bottom], axis=0).T


def body(rhs, lower_blocks, col_index, diag_inverse, turnout, district_of):
    n = lax.axis_size("blk")
    pairs = n // 2
    pieces = 1
    rows_here, _, bs, columns = rhs.shape
    slots = lower_blocks.shape[2]
    half = columns // 2
    width = half // pieces
    count = rows_here * pairs
    packed_rows = packed_places(slots, bs, columns)[-1]
    wide = shaped(width, 2 * bs)
    square = shaped(2 * bs, 2 * bs, dtype=B16)

    def call(kernel, name, outs, operands, mib, flops=0, moved=0, **more):
        several = isinstance(outs, tuple)
        return pl.pallas_call(
            kernel,
            out_shape=outs,
            in_specs=more.pop("in_specs", [VMEM_SPEC] * len(operands)),
            out_specs=more.pop("out_specs", (VMEM_SPEC,) * len(outs) if several else VMEM_SPEC),
            compiler_params=params(mib),
            cost_estimate=cost(flops, moved),
            name=name,
            **more,
        )(*operands)

    def swap(x):
        return lax.ppermute(x, "blk", [(i, i ^ 1) for i in range(n)])

    def shift(x, by):
        return lax.ppermute(x, "blk", [(i, (i + 2 * by) % n) for i in range(n)])

    def pass_on(x, lead, by):
        perm = []
        for k in range(lead, lead + 2 * pieces, 2):
            if by <= k < count:
                sender, target = k % pairs, (k - by) % pairs
                perm += [(2 * sender + c, 2 * target + c) for c in range(2)]
        return lax.ppermute(x, "blk", perm)

    def pack(rows, turnout=turnout):
        return call(
            functools.partial(pack_kernel, rows),
            "pack",
            (shaped(packed_rows, bs),) * len(rows),
            (jnp.transpose(col_index, (2, 1, 0)), turnout, district_of, lower_blocks, diag_inverse, rhs),
            56,
            moved=8 * packed_rows * bs * len(rows),
            in_specs=[SMEM_SPEC, VMEM_SPEC, VMEM_SPEC] + [HBM_SPEC] * 3,
            out_specs=(HBM_SPEC,) * len(rows),
            scratch_shapes=[
                pltpu.VMEM((len(rows), bs, columns), F32),
                pltpu.VMEM((len(rows), packed_rows, bs), F32),
                pltpu.SemaphoreType.DMA((len(rows) * (2 * slots + 4),)),
            ],
        )

    def setup(r):
        args = (r, n, slots, columns)
        held = shaped(4, bs, bs, dtype=B16)
        gh, gl, mh, ml, rt = call(
            functools.partial(near_setup_kernel, *args),
            "near_setup",
            (square, square, held, held, shaped(half, 2 * bs)),
            packs[r],
            10,
            14 * 3 * bs**3,
            24 * bs * bs * 4,
        )
        fh, fl = call(
            functools.partial(far_setup_kernel, *args),
            "far_setup",
            (square, square),
            (*packs[r], mh, ml),
            10,
            10 * 3 * bs**3,
            24 * bs * bs * 4,
        )
        return gh, gl, mh, ml, rt, fh, fl

    def finish(r, values, total):
        first = count - 1 - (r * pairs + pairs - 1)
        window = values[first : first + pairs + 2 * (pieces - 1)]
        is_last = r == 0
        outs = (shaped(half, bs), shaped(half, bs))
        outs += (shaped(NDIST // pairs, columns),) * pairs if is_last else (shaped(NDIST, columns),)
        extra = () if total is None else (total,)
        return call(
            functools.partial(
                finish_kernel, slots, pairs, pieces, len(window), total is not None, is_last
            ),
            "finish",
            outs,
            (*window, *fixed[r][2:4], *packs[r], *extra),
            8,
            6 * 3 * half * bs * bs,
            16 * bs * bs,
            scratch_shapes=[pltpu.VMEM((NDIST, columns), F32)] if is_last else [],
        )

    top = rows_here - 1
    packs, fixed = {}, {}
    (own,) = pack((top,))
    packs[top] = (own, swap(own))
    later, _ = lax.optimization_barrier((turnout, own))
    packed = pack(tuple(range(top)), later) if top else ()
    for r in range(top - 1, -1, -1):
        packs[r] = (packed[r], swap(packed[r]))
    fixed[top] = setup(top)

    keeps, gots = {}, {}
    values = []
    ordered = ()
    total = near = far_now = far_next = None
    steps = count + 2 * (pieces - 1)
    for step in range(steps):
        lead = count - 1 - step
        low = max(lead, 0) // pairs
        high = min(lead + 2 * (pieces - 1), count - 1) // pairs
        rows = range(low, high + 1)
        taken = [x for x in (far_now, near) if x is not None]
        has_near = step + 1 < steps
        has_far = step + 2 < steps
        operands = []
        for r in rows:
            gh, gl, _, _, rt, _, _ = fixed[r]
            operands += [rt, gh, gl] if has_near else [rt]
        place = (lead, pairs, pieces, high * pairs)
        v, *near_out = call(
            functools.partial(near_kernel, *place, len(ordered), len(taken), has_near),
            "near_terms",
            (wide, wide) if has_near else (wide,),
            (*ordered, *taken, *operands),
            4,
            6 * width * 4 * bs * bs,
            6 * width * bs * 4,
        )
        values.append(v)
        near = pass_on(near_out[0], lead, 1) if has_near else None
        far_now, far_next, ordered = far_next, None, ()
        if has_far:
            operands = [x for r in rows for x in fixed[r][5:]]
            far_out = call(
                functools.partial(far_kernel, *place),
                "far_terms",
                wide,
                (v, *operands),
                4,
                6 * width * 4 * bs * bs,
                6 * width * bs * 4,
            )
            ordered = (far_out,)
            r, chip = lead // pairs, lead % pairs
            if chip == pairs - 1 and r > 0:
                fixed[r - 1] = setup(r - 1)
            far_next = pass_on(far_out, lead, 2)
        done = lead + 2 * (pieces - 1)
        if done % pairs == 0 and 0 < done // pairs <= top:
            r = done // pairs
            keeps[r], give, total = finish(r, values, total)
            gots[r] = swap(give)
            near, total = lax.optimization_barrier((near, total))

    keeps[0], give, *parts = finish(0, values, total)
    gots[0] = swap(give)
    parts = [parts[0]] + [shift(parts[by], by) for by in range(1, pairs)]
    order = range(rows_here)
    field = call(
        functools.partial(field_kernel, rows_here),
        "field",
        shaped(rows_here, 1, bs, columns),
        (*[keeps[r] for r in order], *[gots[r] for r in order]),
        4,
        0,
        8 * rows_here * bs * columns,
    )
    parts, field = lax.optimization_barrier((parts, field))
    held = shaped(NDIST // n, columns)
    mine, theirs = call(add_kernel, "district_add", (held, held), tuple(parts), 4)
    mean = call(mean_kernel, "district_mean", held, (mine, swap(theirs)), 4)
    return field, mean


def solution(mesh):
    placed = (
        P(None, "blk", None, "sims"),
        P(None, "blk", None, None, None),
        P(None, "blk", None),
        P(None, "blk", None, None),
        P(None, "blk", None),
        P(None, "blk", None),
    )
    return jax.shard_map(
        body,
        mesh=mesh,
        in_specs=placed,
        out_specs=(P(None, "blk", None, "sims"), P("blk", "sims")),
        check_vma=False,
    )
```

```python
import functools

import jax
import jax.numpy as jnp
from jax import lax
from jax.experimental import pallas as pl
from jax.experimental.pallas import tpu as pltpu
from jax.sharding import PartitionSpec as P

NDIST = 256
F32 = jnp.float32
B16 = jnp.bfloat16
SMEM_SPEC = pl.BlockSpec(memory_space=pltpu.SMEM)
VMEM_SPEC = pl.BlockSpec(memory_space=pltpu.VMEM)
HBM_SPEC = pl.BlockSpec(memory_space=pltpu.HBM)


def params(mib):
    return pltpu.CompilerParams(vmem_limit_bytes=mib * 1024 * 1024)


def cost(flops, moved):
    return pl.CostEstimate(flops=flops, bytes_accessed=moved, transcendentals=0)


def shaped(*shape, dtype=F32):
    return jax.ShapeDtypeStruct(shape, dtype)


def halves(x):
    hi = x.astype(B16)
    lo = (x - hi.astype(F32)).astype(B16)
    return hi, lo


def dot(a, b):
    return jnp.dot(a, b, preferred_element_type=F32)


def dot3(x, y):
    rows = x[0].shape[0]
    both = dot(jnp.concatenate([x[0], x[1]], axis=0), y[0])
    return both[:rows] + both[rows:] + dot(x[0], y[1])


def packed_places(slots, bs, columns):
    rhs_at = (slots + 1) * bs
    col_at = rhs_at + columns
    turnout_at = col_at + 8 * slots
    district_at = turnout_at + 8
    return rhs_at, col_at, turnout_at, district_at, district_at + 8


def chip_now():
    return lax.div(lax.axis_index("blk").astype(jnp.int32), 2)


def upper_here():
    return lax.rem(lax.axis_index("blk").astype(jnp.int32), 2) == 1


def pack_kernel(rows, cols, turnout, district, l_ref, d_ref, r_ref, *refs):
    outs = refs[: len(rows)]
    held, passing, sems = refs[len(rows) :]
    slots, bs = l_ref.shape[2], l_ref.shape[3]
    columns = r_ref.shape[3]
    rhs_at, col_at, turnout_at, district_at, end = packed_places(slots, bs, columns)
    places = [pl.ds(k * bs, bs) for k in range(slots + 1)]
    tail = pl.ds(rhs_at, end - rhs_at)
    made = []

    def copy(source, target):
        made.append(pltpu.make_async_copy(source, target, sems.at[len(made)]))
        made[-1].start()
        return made[-1]

    arrivals = []
    for i, r in enumerate(rows):
        blocks = [l_ref.at[r, 0, k] for k in range(slots)] + [d_ref.at[r, 0]]
        first = copy(r_ref.at[r, 0], held.at[i])
        rest = [copy(x, passing.at[i, at]) for x, at in zip(blocks, places)]
        arrivals.append((first, rest))
    for i, r in enumerate(rows):
        for k in range(slots):
            at = col_at + 8 * k
            passing[i, at : at + 8] = jnp.full((8, bs), cols[k, 0, r].astype(F32))
        passing[i, turnout_at : turnout_at + 8] = jnp.broadcast_to(turnout[r], (8, bs))
        passing[i, district_at : district_at + 8] = jnp.broadcast_to(
            district[r].astype(F32), (8, bs)
        )
    leaving = []
    for i, (first, rest) in enumerate(arrivals):
        first.wait()
        passing[i, rhs_at:col_at] = held[i].T
        leaving.append(copy(passing.at[i, tail], outs[i].at[tail]))
        for arriving, at in zip(rest, places):
            arriving.wait()
            leaving.append(copy(passing.at[i, at], outs[i].at[at]))
    for x in leaving:
        x.wait()


def put(high, low, i, j, value):
    bs = value.shape[0]
    hi, lo = halves(value)
    high[i * bs : (i + 1) * bs, j * bs : (j + 1) * bs] = hi
    low[i * bs : (i + 1) * bs, j * bs : (j + 1) * bs] = lo


def blocks_of(r, n, slots, columns, own, oth):
    is_a = upper_here()
    bs = own.shape[1]
    _, col_at, _, _, _ = packed_places(slots, bs, columns)
    row_b = r * n + 2 * chip_now()
    row_a = row_b + 1

    def upper(at, size):
        return jnp.where(is_a, own[at : at + size], oth[at : at + size])

    def lower(at, size):
        return jnp.where(is_a, oth[at : at + size], own[at : at + size])

    def at_distance(side, row, d):
        found = jnp.zeros((bs, bs), F32)
        column = (row - d).astype(F32)
        for k in range(1, slots):
            col = side(col_at + 8 * k, 1)
            here = (col == column) & (col >= 0.0)
            found = jnp.where(here, side(k * bs, bs), found)
        return halves(found)

    return upper, lower, lambda d: at_distance(upper, row_a, d), lambda d: at_distance(lower, row_b, d)


def near_setup_kernel(r, n, slots, columns, own, oth, gh, gl, mh, ml, rt):
    bs = own.shape[1]
    half = columns // 2
    rhs_at, col_at, _, _, _ = packed_places(slots, bs, columns)
    upper, lower, upper_at, lower_at = blocks_of(r, n, slots, columns, own, oth)
    is_a = upper_here()
    da, db = halves(upper(slots * bs, bs)), halves(lower(slots * bs, bs))
    la1 = halves(upper(0, bs))
    lb1 = halves(jnp.where(lower(col_at, 1) >= 0.0, lower(0, bs), 0.0))
    w = dot3(da, la1)
    wh = halves(w)
    for place, pair in enumerate((da, db, la1, wh)):
        mh[place] = pair[0]
        ml[place] = pair[1]
    for j, (la, lb) in enumerate(((upper_at(2), lb1), (upper_at(3), lower_at(2)))):
        from_b = dot3(db, lb)
        put(gh, gl, 1, j, from_b)
        put(gh, gl, 0, j, dot3(da, la) - dot3(wh, halves(from_b)))
    ra, rb = upper(rhs_at, columns), lower(rhs_at, columns)
    rt[:, :bs] = jnp.where(is_a, ra[half:], ra[:half])
    rt[:, bs:] = jnp.where(is_a, rb[half:], rb[:half])


def far_setup_kernel(r, n, slots, columns, own, oth, mh, ml, fh, fl):
    _, _, upper_at, lower_at = blocks_of(r, n, slots, columns, own, oth)
    da, db, w = ((mh[k], ml[k]) for k in (0, 1, 3))
    for j, lb in enumerate((lower_at(3), lower_at(4))):
        from_b = dot3(db, lb)
        put(fh, fl, 1, j, from_b)
        from_a = -dot3(w, halves(from_b))
        if j == 0:
            from_a = from_a + dot3(da, upper_at(4))
        put(fh, fl, 0, j, from_a)


def near_kernel(part, ordered, has_far, received, has_near, *refs):
    refs = list(refs[ordered:])
    far = refs.pop(0) if has_far else None
    near = refs.pop(0) if received else None
    rt, *refs = refs
    v_out = refs[2] if has_near else refs[0]
    width = v_out.shape[0]
    rows = slice(part * width, (part + 1) * width)
    v = rt[rows, :]
    if has_far:
        v = v - far[rows, :]
    if received:
        v = v - near[...]
    v_out[...] = v
    if has_near:
        gh, gl, _, out = refs
        out[...] = dot3(halves(v), (gh[...], gl[...]))


def far_kernel(*refs):
    *values, fh, fl, out = refs
    v = jnp.concatenate([x[...] for x in values], axis=0)
    out[...] = dot3(halves(v), (fh[...], fl[...]))


def finish_kernel(slots, pairs, pieces, window, has_total, is_last, *refs):
    values = refs[:window]
    mh, ml, own, oth = refs[window : window + 4]
    refs = refs[window + 4 :]
    start = refs[0][...] if has_total else None
    keep, give, *outs = refs[1:] if has_total else refs
    chip, is_a = chip_now(), upper_here()
    bs = mh.shape[1]
    half = keep.shape[0]
    _, _, turnout_at, district_at, _ = packed_places(slots, bs, 2 * half)
    parts = []
    for m in range(pieces):
        v = values[pieces * (pairs - 1) + m][...]
        for q in range(1, pairs):
            v = jnp.where(chip == q, values[pieces * (pairs - 1 - q) + m][...], v)
        parts.append(v)
    v = jnp.concatenate(parts, axis=0)

    def m(k):
        return mh[k], ml[k]

    xa = dot3(halves(v[:, :bs]), m(0))
    xb = dot3(halves(v[:, bs:] - dot3(halves(xa), m(2))), m(1))
    kept, given = jnp.where(is_a, xa, xb), jnp.where(is_a, xb, xa)
    keep[...] = kept
    give[...] = given
    names = lax.broadcasted_iota(jnp.int32, (NDIST, bs), 0).astype(F32)
    sums = jnp.zeros((NDIST, 2 * half), F32) if start is None else start
    for x, pack in ((kept, own), (given, oth)):
        weight = pack[turnout_at : turnout_at + 1]
        member = names == pack[district_at : district_at + 1]
        member = member.astype(F32).astype(B16)
        terms = jnp.concatenate([x * weight, jnp.broadcast_to(weight, (half, bs))], axis=0)
        for part in halves(terms):
            sums = sums + lax.dot_general(
                member, part, (((1,), (1,)), ((), ())), preferred_element_type=F32
            )
    if not is_last:
        outs[0][...] = sums
        return
    held = outs.pop()
    held[...] = sums
    rows = NDIST // pairs
    for by, part in enumerate(outs):
        to = lax.rem(chip + by, pairs)
        part[...] = held[pl.ds(pl.multiple_of(to * rows, rows), rows), :]


def add_kernel(*refs):
    mine, theirs = refs[-2:]
    total = refs[0][...]
    for part in refs[1:-2]:
        total = total + part[...]
    rows = mine.shape[0]
    is_a = upper_here()
    mine[...] = jnp.where(is_a, total[rows:], total[:rows])
    theirs[...] = jnp.where(is_a, total[:rows], total[rows:])


def mean_kernel(mine, got, out):
    half = out.shape[1] // 2
    own, oth = (x[:, :half] / x[:, half:] for x in (mine, got))
    is_a = upper_here()
    out[...] = jnp.concatenate(
        [jnp.where(is_a, oth, own), jnp.where(is_a, own, oth)], axis=1
    )


def field_kernel(rows_here, *refs):
    keeps = refs[:rows_here]
    gots = refs[rows_here : 2 * rows_here]
    out = refs[2 * rows_here]
    is_a = upper_here()
    for r in range(rows_here):
        top = jnp.where(is_a, gots[r][...], keeps[r][...])
        bottom = jnp.where(is_a, keeps[r][...], gots[r][...])
        out[r, 0] = jnp.concatenate([top, bottom], axis=0).T


def body(rhs, lower_blocks, col_index, diag_inverse, turnout, district_of):
    n = lax.axis_size("blk")
    pairs = n // 2
    pieces = 2
    rows_here, _, bs, columns = rhs.shape
    slots = lower_blocks.shape[2]
    half = columns // 2
    width = half // pieces
    count = rows_here * pairs
    packed_rows = packed_places(slots, bs, columns)[-1]
    wide = shaped(width, 2 * bs)
    square = shaped(2 * bs, 2 * bs, dtype=B16)

    def call(kernel, name, outs, operands, mib, flops=0, moved=0, **more):
        several = isinstance(outs, tuple)
        return pl.pallas_call(
            kernel,
            out_shape=outs,
            in_specs=more.pop("in_specs", [VMEM_SPEC] * len(operands)),
            out_specs=more.pop("out_specs", (VMEM_SPEC,) * len(outs) if several else VMEM_SPEC),
            compiler_params=params(mib),
            cost_estimate=cost(flops, moved),
            name=name,
            **more,
        )(*operands)

    def swap(x):
        return lax.ppermute(x, "blk", [(i, i ^ 1) for i in range(n)])

    def shift(x, by):
        return lax.ppermute(x, "blk", [(i, (i + 2 * by) % n) for i in range(n)])

    def pass_on(x, lead, by):
        perm = []
        sender, target = lead % pairs, (lead - by) % pairs
        perm += [(2 * sender + c, 2 * target + c) for c in range(2)]
        return lax.ppermute(x, "blk", perm)

    def pack(rows, turnout=turnout):
        return call(
            functools.partial(pack_kernel, rows),
            "pack",
            (shaped(packed_rows, bs),) * len(rows),
            (jnp.transpose(col_index, (2, 1, 0)), turnout, district_of, lower_blocks, diag_inverse, rhs),
            56,
            moved=8 * packed_rows * bs * len(rows),
            in_specs=[SMEM_SPEC, VMEM_SPEC, VMEM_SPEC] + [HBM_SPEC] * 3,
            out_specs=(HBM_SPEC,) * len(rows),
            scratch_shapes=[
                pltpu.VMEM((len(rows), bs, columns), F32),
                pltpu.VMEM((len(rows), packed_rows, bs), F32),
                pltpu.SemaphoreType.DMA((len(rows) * (2 * slots + 4),)),
            ],
        )

    def setup(r):
        args = (r, n, slots, columns)
        held = shaped(4, bs, bs, dtype=B16)
        gh, gl, mh, ml, rt = call(
            functools.partial(near_setup_kernel, *args),
            "near_setup",
            (square, square, held, held, shaped(half, 2 * bs)),
            packs[r],
            10,
            14 * 3 * bs**3,
            24 * bs * bs * 4,
        )
        fh, fl = call(
            functools.partial(far_setup_kernel, *args),
            "far_setup",
            (square, square),
            (*packs[r], mh, ml),
            10,
            10 * 3 * bs**3,
            24 * bs * bs * 4,
        )
        return gh, gl, mh, ml, rt, fh, fl

    def finish(r, values, total):
        first = count - 1 - (r * pairs + pairs - 1)
        window = [x for step in values[first : first + pairs] for x in step]
        is_last = r == 0
        outs = (shaped(half, bs), shaped(half, bs))
        outs += (shaped(NDIST // pairs, columns),) * pairs if is_last else (shaped(NDIST, columns),)
        extra = () if total is None else (total,)
        return call(
            functools.partial(
                finish_kernel, slots, pairs, pieces, len(window), total is not None, is_last
            ),
            "finish",
            outs,
            (*window, *fixed[r][2:4], *packs[r], *extra),
            8,
            6 * 3 * half * bs * bs,
            16 * bs * bs,
            scratch_shapes=[pltpu.VMEM((NDIST, columns), F32)] if is_last else [],
        )

    top = rows_here - 1
    packs, fixed = {}, {}
    (own,) = pack((top,))
    packs[top] = (own, swap(own))
    later, _ = lax.optimization_barrier((turnout, own))
    packed = pack(tuple(range(top)), later) if top else ()
    for r in range(top - 1, -1, -1):
        packs[r] = (packed[r], swap(packed[r]))
    fixed[top] = setup(top)

    keeps, gots = {}, {}
    values = []
    ordered = ()
    total = far_now = far_next = None
    nears = [None] * pieces
    for step in range(count):
        lead = count - 1 - step
        r, chip = lead // pairs, lead % pairs
        has_near, has_far = lead >= 1, lead >= 2
        gh, gl, _, _, rt, fh, fl = fixed[r]
        halves_now = []
        for part in range(pieces):
            taken = [x for x in (far_now, nears[part]) if x is not None]
            v, *near_out = call(
                functools.partial(
                    near_kernel, part, len(ordered),
                    far_now is not None, nears[part] is not None, has_near,
                ),
                "near_terms",
                (wide, wide) if has_near else (wide,),
                (*ordered, *taken, rt, *((gh, gl) if has_near else ())),
                4,
                6 * width * 4 * bs * bs,
                6 * width * bs * 4,
            )
            halves_now.append(v)
            nears[part] = pass_on(near_out[0], lead, 1) if has_near else None
            ordered = tuple(near_out)
        values.append(halves_now)
        far_now, far_next, ordered = far_next, None, ()
        if has_far:
            far_out = call(
                far_kernel,
                "far_terms",
                shaped(half, 2 * bs),
                (*halves_now, fh, fl),
                4,
                6 * half * 4 * bs * bs,
                6 * half * bs * 4,
            )
            ordered = (far_out,)
            if chip == pairs - 1 and r > 0:
                fixed[r - 1] = setup(r - 1)
            far_next = pass_on(far_out, lead, 2)
        if chip == 0 and r > 0:
            keeps[r], give, total = finish(r, values, total)
            gots[r] = swap(give)
            nears[0], total = lax.optimization_barrier((nears[0], total))

    keeps[0], give, *parts = finish(0, values, total)
    gots[0] = swap(give)
    parts = [parts[0]] + [shift(parts[by], by) for by in range(1, pairs)]
    order = range(rows_here)
    field = call(
        functools.partial(field_kernel, rows_here),
        "field",
        shaped(rows_here, 1, bs, columns),
        (*[keeps[r] for r in order], *[gots[r] for r in order]),
        4,
        0,
        8 * rows_here * bs * columns,
    )
    parts, field = lax.optimization_barrier((parts, field))
    held = shaped(NDIST // n, columns)
    mine, theirs = call(add_kernel, "district_add", (held, held), tuple(parts), 4)
    mean = call(mean_kernel, "district_mean", held, (mine, swap(theirs)), 4)
    return field, mean


def solution(mesh):
    placed = (
        P(None, "blk", None, "sims"),
        P(None, "blk", None, None, None),
        P(None, "blk", None),
        P(None, "blk", None, None),
        P(None, "blk", None),
        P(None, "blk", None),
    )
    return jax.shard_map(
        body,
        mesh=mesh,
        in_specs=placed,
        out_specs=(P(None, "blk", None, "sims"), P("blk", "sims")),
        check_vma=False,
    )
```

```python
import functools

import jax
import jax.numpy as jnp
from jax import lax
from jax.experimental import pallas as pl
from jax.experimental.pallas import tpu as pltpu
from jax.sharding import PartitionSpec as P

NDIST = 256
F32 = jnp.float32
B16 = jnp.bfloat16
SMEM_SPEC = pl.BlockSpec(memory_space=pltpu.SMEM)
VMEM_SPEC = pl.BlockSpec(memory_space=pltpu.VMEM)
HBM_SPEC = pl.BlockSpec(memory_space=pltpu.HBM)


def params(mib):
    return pltpu.CompilerParams(vmem_limit_bytes=mib * 1024 * 1024)


def cost(flops, moved):
    return pl.CostEstimate(flops=flops, bytes_accessed=moved, transcendentals=0)


def shaped(*shape, dtype=F32):
    return jax.ShapeDtypeStruct(shape, dtype)


def halves(x):
    hi = x.astype(B16)
    lo = (x - hi.astype(F32)).astype(B16)
    return hi, lo


def dot(a, b):
    return jnp.dot(a, b, preferred_element_type=F32)


def dot3(x, y):
    rows = x[0].shape[0]
    both = dot(jnp.concatenate([x[0], x[1]], axis=0), y[0])
    return both[:rows] + both[rows:] + dot(x[0], y[1])


def packed_places(slots, bs, columns):
    rhs_at = (slots + 1) * bs
    col_at = rhs_at + columns
    turnout_at = col_at + 8 * slots
    district_at = turnout_at + 8
    return rhs_at, col_at, turnout_at, district_at, district_at + 8


def chip_now():
    return lax.div(lax.axis_index("blk").astype(jnp.int32), 2)


def upper_here():
    return lax.rem(lax.axis_index("blk").astype(jnp.int32), 2) == 1


def pack_kernel(rows, cols, turnout, district, l_ref, d_ref, r_ref, *refs):
    outs = refs[: len(rows)]
    held, passing, sems = refs[len(rows) :]
    slots, bs = l_ref.shape[2], l_ref.shape[3]
    columns = r_ref.shape[3]
    rhs_at, col_at, turnout_at, district_at, end = packed_places(slots, bs, columns)
    places = [pl.ds(k * bs, bs) for k in range(slots + 1)]
    tail = pl.ds(rhs_at, end - rhs_at)
    made = []

    def copy(source, target):
        made.append(pltpu.make_async_copy(source, target, sems.at[len(made)]))
        made[-1].start()
        return made[-1]

    arrivals = []
    for i, r in enumerate(rows):
        blocks = [l_ref.at[r, 0, k] for k in range(slots)] + [d_ref.at[r, 0]]
        first = copy(r_ref.at[r, 0], held.at[i])
        rest = [copy(x, passing.at[i, at]) for x, at in zip(blocks, places)]
        arrivals.append((first, rest))
    for i, r in enumerate(rows):
        for k in range(slots):
            at = col_at + 8 * k
            passing[i, at : at + 8] = jnp.full((8, bs), cols[k, 0, r].astype(F32))
        passing[i, turnout_at : turnout_at + 8] = jnp.broadcast_to(turnout[r], (8, bs))
        passing[i, district_at : district_at + 8] = jnp.broadcast_to(
            district[r].astype(F32), (8, bs)
        )
    leaving = []
    for i, (first, rest) in enumerate(arrivals):
        first.wait()
        passing[i, rhs_at:col_at] = held[i].T
        leaving.append(copy(passing.at[i, tail], outs[i].at[tail]))
        for arriving, at in zip(rest, places):
            arriving.wait()
            leaving.append(copy(passing.at[i, at], outs[i].at[at]))
    for x in leaving:
        x.wait()


def put(high, low, i, j, value):
    bs = value.shape[0]
    hi, lo = halves(value)
    high[i * bs : (i + 1) * bs, j * bs : (j + 1) * bs] = hi
    low[i * bs : (i + 1) * bs, j * bs : (j + 1) * bs] = lo


def blocks_of(r, n, slots, columns, own, oth):
    is_a = upper_here()
    bs = own.shape[1]
    _, col_at, _, _, _ = packed_places(slots, bs, columns)
    row_b = r * n + 2 * chip_now()
    row_a = row_b + 1

    def upper(at, size):
        return jnp.where(is_a, own[at : at + size], oth[at : at + size])

    def lower(at, size):
        return jnp.where(is_a, oth[at : at + size], own[at : at + size])

    def at_distance(side, row, d):
        found = jnp.zeros((bs, bs), F32)
        column = (row - d).astype(F32)
        for k in range(1, slots):
            col = side(col_at + 8 * k, 1)
            here = (col == column) & (col >= 0.0)
            found = jnp.where(here, side(k * bs, bs), found)
        return halves(found)

    return upper, lower, lambda d: at_distance(upper, row_a, d), lambda d: at_distance(lower, row_b, d)


def near_setup_kernel(r, n, slots, columns, own, oth, gh, gl, mh, ml, rt):
    bs = own.shape[1]
    half = columns // 2
    rhs_at, col_at, _, _, _ = packed_places(slots, bs, columns)
    upper, lower, upper_at, lower_at = blocks_of(r, n, slots, columns, own, oth)
    is_a = upper_here()
    da, db = halves(upper(slots * bs, bs)), halves(lower(slots * bs, bs))
    la1 = halves(upper(0, bs))
    lb1 = halves(jnp.where(lower(col_at, 1) >= 0.0, lower(0, bs), 0.0))
    w = dot3(da, la1)
    wh = halves(w)
    for place, pair in enumerate((da, db, la1, wh)):
        mh[place] = pair[0]
        ml[place] = pair[1]
    for j, (la, lb) in enumerate(((upper_at(2), lb1), (upper_at(3), lower_at(2)))):
        from_b = dot3(db, lb)
        put(gh, gl, 1, j, from_b)
        put(gh, gl, 0, j, dot3(da, la) - dot3(wh, halves(from_b)))
    ra, rb = upper(rhs_at, columns), lower(rhs_at, columns)
    rt[:, :bs] = jnp.where(is_a, ra[half:], ra[:half])
    rt[:, bs:] = jnp.where(is_a, rb[half:], rb[:half])


def far_setup_kernel(r, n, slots, columns, own, oth, mh, ml, fh, fl):
    _, _, upper_at, lower_at = blocks_of(r, n, slots, columns, own, oth)
    da, db, w = ((mh[k], ml[k]) for k in (0, 1, 3))
    for j, lb in enumerate((lower_at(3), lower_at(4))):
        from_b = dot3(db, lb)
        put(fh, fl, 1, j, from_b)
        from_a = -dot3(w, halves(from_b))
        if j == 0:
            from_a = from_a + dot3(da, upper_at(4))
        put(fh, fl, 0, j, from_a)


def place_of(lead, pairs, pieces):
    ahead = lax.rem(chip_now() - lead % pairs + pairs, pairs)
    piece = jnp.minimum(lax.div(ahead, 2), pieces - 1)
    return piece, lead + ahead


def choose(choices, pair, split, run):
    if len(choices) == 1:
        run(*choices[0])
        return

    @pl.when(pair < split)
    def _():
        run(*choices[0])

    @pl.when(pair >= split)
    def _():
        run(*choices[1])


def near_kernel(lead, pairs, pieces, split, ordered, received, has_near, *refs):
    refs = refs[ordered:]
    taken = refs[:received]
    outs = refs[-2:] if has_near else refs[-1:]
    refs = refs[received : -len(outs)]
    each = 3 if has_near else 1
    choices = [refs[i : i + each] for i in range(0, len(refs), each)]
    v_out = outs[0]
    width = v_out.shape[0]
    piece, pair = place_of(lead, pairs, pieces)
    rows = pl.ds(pl.multiple_of(piece * width, width), width)

    def run(rt, gh=None, gl=None):
        v = rt[rows, :]
        for x in taken:
            v = v - x[...]
        v_out[...] = v
        if has_near:
            outs[1][...] = dot3(halves(v), (gh[...], gl[...]))

    choose(choices, pair, split, run)


def far_kernel(lead, pairs, pieces, split, v_ref, *refs):
    out = refs[-1]
    refs = refs[:-1]
    _, pair = place_of(lead, pairs, pieces)

    def run(fh, fl):
        out[...] = dot3(halves(v_ref[...]), (fh[...], fl[...]))

    choose([refs[i : i + 2] for i in range(0, len(refs), 2)], pair, split, run)


def finish_kernel(slots, pairs, pieces, window, has_total, is_last, *refs):
    values = refs[:window]
    mh, ml, own, oth = refs[window : window + 4]
    refs = refs[window + 4 :]
    start = refs[0][...] if has_total else None
    keep, give, *outs = refs[1:] if has_total else refs
    chip, is_a = chip_now(), upper_here()
    bs = mh.shape[1]
    half = keep.shape[0]
    _, _, turnout_at, district_at, _ = packed_places(slots, bs, 2 * half)
    parts = []
    for m in range(pieces):
        v = values[pairs - 1 + 2 * m][...]
        for q in range(1, pairs):
            v = jnp.where(chip == q, values[pairs - 1 - q + 2 * m][...], v)
        parts.append(v)
    v = jnp.concatenate(parts, axis=0)

    def m(k):
        return mh[k], ml[k]

    xa = dot3(halves(v[:, :bs]), m(0))
    xb = dot3(halves(v[:, bs:] - dot3(halves(xa), m(2))), m(1))
    kept, given = jnp.where(is_a, xa, xb), jnp.where(is_a, xb, xa)
    keep[...] = kept
    give[...] = given
    names = lax.broadcasted_iota(jnp.int32, (NDIST, bs), 0).astype(F32)
    sums = jnp.zeros((NDIST, 2 * half), F32) if start is None else start
    for x, pack in ((kept, own), (given, oth)):
        weight = pack[turnout_at : turnout_at + 1]
        member = names == pack[district_at : district_at + 1]
        member = member.astype(F32).astype(B16)
        terms = jnp.concatenate([x * weight, jnp.broadcast_to(weight, (half, bs))], axis=0)
        for part in halves(terms):
            sums = sums + lax.dot_general(
                member, part, (((1,), (1,)), ((), ())), preferred_element_type=F32
            )
    if not is_last:
        outs[0][...] = sums
        return
    held = outs.pop()
    held[...] = sums
    rows = NDIST // (2 * pairs)
    core = jnp.where(is_a, 1, 0)
    for i, part in enumerate(outs):
        to = 2 * lax.rem(chip + i // 2, pairs) + (core if i % 2 == 0 else 1 - core)
        part[...] = held[pl.ds(pl.multiple_of(to * rows, rows), rows), :]


def mean_kernel(*refs):
    *parts, out = refs
    half = out.shape[1] // 2
    own, oth = parts[0][...], parts[1][...]
    for i in range(2, len(parts), 2):
        own = own + parts[i][...]
        oth = oth + parts[i + 1][...]
    own, oth = (x[:, :half] / x[:, half:] for x in (own, oth))
    is_a = upper_here()
    out[...] = jnp.concatenate(
        [jnp.where(is_a, oth, own), jnp.where(is_a, own, oth)], axis=1
    )


def field_kernel(rows_here, *refs):
    keeps = refs[:rows_here]
    gots = refs[rows_here : 2 * rows_here]
    out = refs[2 * rows_here]
    is_a = upper_here()
    for r in range(rows_here):
        top = jnp.where(is_a, gots[r][...], keeps[r][...])
        bottom = jnp.where(is_a, keeps[r][...], gots[r][...])
        out[r, 0] = jnp.concatenate([top, bottom], axis=0).T


def body(rhs, lower_blocks, col_index, diag_inverse, turnout, district_of):
    n = lax.axis_size("blk")
    pairs = n // 2
    pieces = 1
    rows_here, _, bs, columns = rhs.shape
    slots = lower_blocks.shape[2]
    half = columns // 2
    width = half // pieces
    count = rows_here * pairs
    packed_rows = packed_places(slots, bs, columns)[-1]
    wide = shaped(width, 2 * bs)
    square = shaped(2 * bs, 2 * bs, dtype=B16)

    def call(kernel, name, outs, operands, mib, flops=0, moved=0, **more):
        several = isinstance(outs, tuple)
        return pl.pallas_call(
            kernel,
            out_shape=outs,
            in_specs=more.pop("in_specs", [VMEM_SPEC] * len(operands)),
            out_specs=more.pop("out_specs", (VMEM_SPEC,) * len(outs) if several else VMEM_SPEC),
            compiler_params=params(mib),
            cost_estimate=cost(flops, moved),
            name=name,
            **more,
        )(*operands)

    def swap(x):
        return lax.ppermute(x, "blk", [(i, i ^ 1) for i in range(n)])

    def send(x, by, flip):
        perm = [(i, (i + 2 * by) % n ^ flip) for i in range(n)]
        return lax.ppermute(x, "blk", perm)

    def pass_on(x, lead, by):
        perm = []
        for k in range(lead, lead + 2 * pieces, 2):
            if by <= k < count:
                sender, target = k % pairs, (k - by) % pairs
                perm += [(2 * sender + c, 2 * target + c) for c in range(2)]
        return lax.ppermute(x, "blk", perm)

    def pack(rows, turnout=turnout):
        return call(
            functools.partial(pack_kernel, rows),
            "pack",
            (shaped(packed_rows, bs),) * len(rows),
            (jnp.transpose(col_index, (2, 1, 0)), turnout, district_of, lower_blocks, diag_inverse, rhs),
            56,
            moved=8 * packed_rows * bs * len(rows),
            in_specs=[SMEM_SPEC, VMEM_SPEC, VMEM_SPEC] + [HBM_SPEC] * 3,
            out_specs=(HBM_SPEC,) * len(rows),
            scratch_shapes=[
                pltpu.VMEM((len(rows), bs, columns), F32),
                pltpu.VMEM((len(rows), packed_rows, bs), F32),
                pltpu.SemaphoreType.DMA((len(rows) * (2 * slots + 4),)),
            ],
        )

    def setup(r):
        args = (r, n, slots, columns)
        held = shaped(4, bs, bs, dtype=B16)
        gh, gl, mh, ml, rt = call(
            functools.partial(near_setup_kernel, *args),
            "near_setup",
            (square, square, held, held, shaped(half, 2 * bs)),
            packs[r],
            10,
            14 * 3 * bs**3,
            24 * bs * bs * 4,
        )
        fh, fl = call(
            functools.partial(far_setup_kernel, *args),
            "far_setup",
            (square, square),
            (*packs[r], mh, ml),
            10,
            10 * 3 * bs**3,
            24 * bs * bs * 4,
        )
        return gh, gl, mh, ml, rt, fh, fl

    def finish(r, values, total):
        first = count - 1 - (r * pairs + pairs - 1)
        window = values[first : first + pairs + 2 * (pieces - 1)]
        is_last = r == 0
        outs = (shaped(half, bs), shaped(half, bs))
        outs += (shaped(NDIST // n, columns),) * n if is_last else (shaped(NDIST, columns),)
        extra = () if total is None else (total,)
        return call(
            functools.partial(
                finish_kernel, slots, pairs, pieces, len(window), total is not None, is_last
            ),
            "finish",
            outs,
            (*window, *fixed[r][2:4], *packs[r], *extra),
            8,
            6 * 3 * half * bs * bs,
            16 * bs * bs,
            scratch_shapes=[pltpu.VMEM((NDIST, columns), F32)] if is_last else [],
        )

    top = rows_here - 1
    packs, fixed = {}, {}
    (own,) = pack((top,))
    packs[top] = (own, swap(own))
    later, _ = lax.optimization_barrier((turnout, own))
    packed = pack(tuple(range(top)), later) if top else ()
    for r in range(top - 1, -1, -1):
        packs[r] = (packed[r], swap(packed[r]))
    fixed[top] = setup(top)

    keeps, gots = {}, {}
    values = []
    ordered = ()
    total = near = far_now = far_next = None
    steps = count + 2 * (pieces - 1)
    for step in range(steps):
        lead = count - 1 - step
        low = max(lead, 0) // pairs
        high = min(lead + 2 * (pieces - 1), count - 1) // pairs
        rows = range(low, high + 1)
        taken = [x for x in (far_now, near) if x is not None]
        has_near = step + 1 < steps
        has_far = step + 2 < steps
        operands = []
        for r in rows:
            gh, gl, _, _, rt, _, _ = fixed[r]
            operands += [rt, gh, gl] if has_near else [rt]
        place = (lead, pairs, pieces, high * pairs)
        v, *near_out = call(
            functools.partial(near_kernel, *place, len(ordered), len(taken), has_near),
            "near_terms",
            (wide, wide) if has_near else (wide,),
            (*ordered, *taken, *operands),
            4,
            6 * width * 4 * bs * bs,
            6 * width * bs * 4,
        )
        values.append(v)
        near = pass_on(near_out[0], lead, 1) if has_near else None
        far_now, far_next, ordered = far_next, None, ()
        if has_far:
            operands = [x for r in rows for x in fixed[r][5:]]
            far_out = call(
                functools.partial(far_kernel, *place),
                "far_terms",
                wide,
                (v, *operands),
                4,
                6 * width * 4 * bs * bs,
                6 * width * bs * 4,
            )
            ordered = (far_out,)
            r, chip = lead // pairs, lead % pairs
            if chip == pairs - 1 and r > 0:
                fixed[r - 1] = setup(r - 1)
            far_next = pass_on(far_out, lead, 2)
        done = lead + 2 * (pieces - 1)
        if done % pairs == 0 and 0 < done // pairs <= top:
            r = done // pairs
            keeps[r], give, total = finish(r, values, total)
            gots[r] = swap(give)
            near, total = lax.optimization_barrier((near, total))

    keeps[0], give, *parts = finish(0, values, total)
    gots[0] = swap(give)
    parts = [parts[0]] + [send(parts[i], i // 2, i % 2) for i in range(1, n)]
    order = range(rows_here)
    field = call(
        functools.partial(field_kernel, rows_here),
        "field",
        shaped(rows_here, 1, bs, columns),
        (*[keeps[r] for r in order], *[gots[r] for r in order]),
        4,
        0,
        8 * rows_here * bs * columns,
    )
    parts, field = lax.optimization_barrier((parts, field))
    mean = call(mean_kernel, "district_mean", shaped(NDIST // n, columns), tuple(parts), 4)
    return field, mean


def solution(mesh):
    placed = (
        P(None, "blk", None, "sims"),
        P(None, "blk", None, None, None),
        P(None, "blk", None),
        P(None, "blk", None, None),
        P(None, "blk", None),
        P(None, "blk", None),
    )
    return jax.shard_map(
        body,
        mesh=mesh,
        in_specs=placed,
        out_specs=(P(None, "blk", None, "sims"), P("blk", "sims")),
        check_vma=False,
    )
```

```python
import functools

import jax
import jax.numpy as jnp
from jax import lax
from jax.experimental import pallas as pl
from jax.experimental.pallas import tpu as pltpu
from jax.sharding import PartitionSpec as P

NDIST = 256
F32 = jnp.float32
B16 = jnp.bfloat16
SMEM_SPEC = pl.BlockSpec(memory_space=pltpu.SMEM)
VMEM_SPEC = pl.BlockSpec(memory_space=pltpu.VMEM)
HBM_SPEC = pl.BlockSpec(memory_space=pltpu.HBM)


def params(mib):
    return pltpu.CompilerParams(vmem_limit_bytes=mib * 1024 * 1024)


def cost(flops, moved):
    return pl.CostEstimate(flops=flops, bytes_accessed=moved, transcendentals=0)


def shaped(*shape, dtype=F32):
    return jax.ShapeDtypeStruct(shape, dtype)


def halves(x):
    hi = x.astype(B16)
    lo = (x - hi.astype(F32)).astype(B16)
    return hi, lo


def dot(a, b):
    return jnp.dot(a, b, preferred_element_type=F32)


def dot3(x, y):
    rows = x[0].shape[0]
    both = dot(jnp.concatenate([x[0], x[1]], axis=0), y[0])
    return both[:rows] + both[rows:] + dot(x[0], y[1])


def packed_places(slots, bs, columns):
    rhs_at = (slots + 1) * bs
    col_at = rhs_at + columns
    turnout_at = col_at + 8 * slots
    district_at = turnout_at + 8
    return rhs_at, col_at, turnout_at, district_at, district_at + 8


def chip_now():
    return lax.div(lax.axis_index("blk").astype(jnp.int32), 2)


def upper_here():
    return lax.rem(lax.axis_index("blk").astype(jnp.int32), 2) == 1


def pack_kernel(rows, cols, turnout, district, l_ref, d_ref, r_ref, *refs):
    outs = refs[: len(rows)]
    held, passing, sems = refs[len(rows) :]
    slots, bs = l_ref.shape[2], l_ref.shape[3]
    columns = r_ref.shape[3]
    rhs_at, col_at, turnout_at, district_at, end = packed_places(slots, bs, columns)
    places = [pl.ds(k * bs, bs) for k in range(slots + 1)]
    tail = pl.ds(rhs_at, end - rhs_at)
    made = []

    def copy(source, target):
        made.append(pltpu.make_async_copy(source, target, sems.at[len(made)]))
        made[-1].start()
        return made[-1]

    arrivals = []
    for i, r in enumerate(rows):
        blocks = [l_ref.at[r, 0, k] for k in range(slots)] + [d_ref.at[r, 0]]
        first = copy(r_ref.at[r, 0], held.at[i])
        rest = [copy(x, passing.at[i, at]) for x, at in zip(blocks, places)]
        arrivals.append((first, rest))
    for i, r in enumerate(rows):
        for k in range(slots):
            at = col_at + 8 * k
            passing[i, at : at + 8] = jnp.full((8, bs), cols[k, 0, r].astype(F32))
        passing[i, turnout_at : turnout_at + 8] = jnp.broadcast_to(turnout[r], (8, bs))
        passing[i, district_at : district_at + 8] = jnp.broadcast_to(
            district[r].astype(F32), (8, bs)
        )
    leaving = []
    for i, (first, rest) in enumerate(arrivals):
        first.wait()
        passing[i, rhs_at:col_at] = held[i].T
        leaving.append(copy(passing.at[i, tail], outs[i].at[tail]))
        for arriving, at in zip(rest, places):
            arriving.wait()
            leaving.append(copy(passing.at[i, at], outs[i].at[at]))
    for x in leaving:
        x.wait()


def put(high, low, i, j, value):
    bs = value.shape[0]
    hi, lo = halves(value)
    high[i * bs : (i + 1) * bs, j * bs : (j + 1) * bs] = hi
    low[i * bs : (i + 1) * bs, j * bs : (j + 1) * bs] = lo


def blocks_of(r, n, slots, columns, own, oth):
    is_a = upper_here()
    bs = own.shape[1]
    _, col_at, _, _, _ = packed_places(slots, bs, columns)
    row_b = r * n + 2 * chip_now()
    row_a = row_b + 1

    def upper(at, size):
        return jnp.where(is_a, own[at : at + size], oth[at : at + size])

    def lower(at, size):
        return jnp.where(is_a, oth[at : at + size], own[at : at + size])

    def at_distance(side, row, d):
        found = jnp.zeros((bs, bs), F32)
        column = (row - d).astype(F32)
        for k in range(1, slots):
            col = side(col_at + 8 * k, 1)
            here = (col == column) & (col >= 0.0)
            found = jnp.where(here, side(k * bs, bs), found)
        return halves(found)

    return upper, lower, lambda d: at_distance(upper, row_a, d), lambda d: at_distance(lower, row_b, d)


def near_setup_kernel(r, n, slots, columns, own, oth, gh, gl, mh, ml, rt):
    bs = own.shape[1]
    half = columns // 2
    rhs_at, col_at, _, _, _ = packed_places(slots, bs, columns)
    upper, lower, upper_at, lower_at = blocks_of(r, n, slots, columns, own, oth)
    is_a = upper_here()
    da, db = halves(upper(slots * bs, bs)), halves(lower(slots * bs, bs))
    la1 = halves(upper(0, bs))
    lb1 = halves(jnp.where(lower(col_at, 1) >= 0.0, lower(0, bs), 0.0))
    w = dot3(da, la1)
    wh = halves(w)
    for place, pair in enumerate((da, db, la1, wh)):
        mh[place] = pair[0]
        ml[place] = pair[1]
    for j, (la, lb) in enumerate(((upper_at(2), lb1), (upper_at(3), lower_at(2)))):
        from_b = dot3(db, lb)
        put(gh, gl, 1, j, from_b)
        put(gh, gl, 0, j, dot3(da, la) - dot3(wh, halves(from_b)))
    ra, rb = upper(rhs_at, columns), lower(rhs_at, columns)
    rt[:, :bs] = jnp.where(is_a, ra[half:], ra[:half])
    rt[:, bs:] = jnp.where(is_a, rb[half:], rb[:half])


def far_setup_kernel(r, n, slots, columns, own, oth, mh, ml, fh, fl):
    _, _, upper_at, lower_at = blocks_of(r, n, slots, columns, own, oth)
    da, db, w = ((mh[k], ml[k]) for k in (0, 1, 3))
    for j, lb in enumerate((lower_at(3), lower_at(4))):
        from_b = dot3(db, lb)
        put(fh, fl, 1, j, from_b)
        from_a = -dot3(w, halves(from_b))
        if j == 0:
            from_a = from_a + dot3(da, upper_at(4))
        put(fh, fl, 0, j, from_a)


def place_of(lead, pairs, pieces):
    ahead = lax.rem(chip_now() - lead % pairs + pairs, pairs)
    piece = jnp.minimum(lax.div(ahead, 2), pieces - 1)
    return piece, lead + ahead


def choose(choices, pair, split, run):
    if len(choices) == 1:
        run(*choices[0])
        return

    @pl.when(pair < split)
    def _():
        run(*choices[0])

    @pl.when(pair >= split)
    def _():
        run(*choices[1])


def near_kernel(lead, pairs, pieces, split, ordered, received, has_near, *refs):
    refs = refs[ordered:]
    taken = refs[:received]
    outs = refs[-2:] if has_near else refs[-1:]
    refs = refs[received : -len(outs)]
    each = 3 if has_near else 1
    choices = [refs[i : i + each] for i in range(0, len(refs), each)]
    v_out = outs[0]
    width = v_out.shape[0]
    piece, pair = place_of(lead, pairs, pieces)
    rows = pl.ds(pl.multiple_of(piece * width, width), width)

    def run(rt, gh=None, gl=None):
        v = rt[rows, :]
        for x in taken:
            v = v - x[...]
        v_out[...] = v
        if has_near:
            outs[1][...] = dot3(halves(v), (gh[...], gl[...]))

    choose(choices, pair, split, run)


def far_kernel(lead, pairs, pieces, split, v_ref, *refs):
    out = refs[-1]
    refs = refs[:-1]
    _, pair = place_of(lead, pairs, pieces)

    def run(fh, fl):
        out[...] = dot3(halves(v_ref[...]), (fh[...], fl[...]))

    choose([refs[i : i + 2] for i in range(0, len(refs), 2)], pair, split, run)


def finish_kernel(slots, pairs, pieces, window, has_total, is_last, *refs):
    values = refs[:window]
    mh, ml, own, oth = refs[window : window + 4]
    refs = refs[window + 4 :]
    start = refs[0][...] if has_total else None
    keep, give, *outs = refs[1:] if has_total else refs
    chip, is_a = chip_now(), upper_here()
    bs = mh.shape[1]
    half = keep.shape[0]
    _, _, turnout_at, district_at, _ = packed_places(slots, bs, 2 * half)
    parts = []
    for m in range(pieces):
        v = values[pairs - 1 + 2 * m][...]
        for q in range(1, pairs):
            v = jnp.where(chip == q, values[pairs - 1 - q + 2 * m][...], v)
        parts.append(v)
    v = jnp.concatenate(parts, axis=0)

    def m(k):
        return mh[k], ml[k]

    xa = dot3(halves(v[:, :bs]), m(0))
    xb = dot3(halves(v[:, bs:] - dot3(halves(xa), m(2))), m(1))
    kept, given = jnp.where(is_a, xa, xb), jnp.where(is_a, xb, xa)
    keep[...] = kept
    give[...] = given
    names = lax.broadcasted_iota(jnp.int32, (NDIST, bs), 0).astype(F32)
    sums = jnp.zeros((NDIST, 2 * half), F32) if start is None else start
    for x, pack in ((kept, own), (given, oth)):
        weight = pack[turnout_at : turnout_at + 1]
        member = names == pack[district_at : district_at + 1]
        member = member.astype(F32).astype(B16)
        terms = jnp.concatenate([x * weight, jnp.broadcast_to(weight, (half, bs))], axis=0)
        for part in halves(terms):
            sums = sums + lax.dot_general(
                member, part, (((1,), (1,)), ((), ())), preferred_element_type=F32
            )
    if not is_last:
        outs[0][...] = sums
        return
    held = outs.pop()
    held[...] = sums
    rows = NDIST // pairs
    for by, part in enumerate(outs):
        to = lax.rem(chip + by, pairs)
        part[...] = held[pl.ds(pl.multiple_of(to * rows, rows), rows), :]


def add_kernel(*refs):
    mine, theirs = refs[-2:]
    total = refs[0][...]
    for part in refs[1:-2]:
        total = total + part[...]
    rows = mine.shape[0]
    is_a = upper_here()
    mine[...] = jnp.where(is_a, total[rows:], total[:rows])
    theirs[...] = jnp.where(is_a, total[:rows], total[rows:])


def mean_kernel(mine, got, out):
    half = out.shape[1] // 2
    own, oth = (x[:, :half] / x[:, half:] for x in (mine, got))
    is_a = upper_here()
    out[...] = jnp.concatenate(
        [jnp.where(is_a, oth, own), jnp.where(is_a, own, oth)], axis=1
    )


def field_kernel(rows_here, *refs):
    keeps = refs[:rows_here]
    gots = refs[rows_here : 2 * rows_here]
    out = refs[2 * rows_here]
    is_a = upper_here()
    for r in range(rows_here):
        top = jnp.where(is_a, gots[r][...], keeps[r][...])
        bottom = jnp.where(is_a, keeps[r][...], gots[r][...])
        out[r, 0] = jnp.concatenate([top, bottom], axis=0).T


def body(rhs, lower_blocks, col_index, diag_inverse, turnout, district_of):
    n = lax.axis_size("blk")
    pairs = n // 2
    pieces = 1
    rows_here, _, bs, columns = rhs.shape
    slots = lower_blocks.shape[2]
    half = columns // 2
    width = half // pieces
    count = rows_here * pairs
    packed_rows = packed_places(slots, bs, columns)[-1]
    wide = shaped(width, 2 * bs)
    square = shaped(2 * bs, 2 * bs, dtype=B16)

    def call(kernel, name, outs, operands, mib, flops=0, moved=0, **more):
        several = isinstance(outs, tuple)
        return pl.pallas_call(
            kernel,
            out_shape=outs,
            in_specs=more.pop("in_specs", [VMEM_SPEC] * len(operands)),
            out_specs=more.pop("out_specs", (VMEM_SPEC,) * len(outs) if several else VMEM_SPEC),
            compiler_params=params(mib),
            cost_estimate=cost(flops, moved),
            name=name,
            **more,
        )(*operands)

    def swap(x):
        return lax.ppermute(x, "blk", [(i, i ^ 1) for i in range(n)])

    def shift(x, by):
        return lax.ppermute(x, "blk", [(i, (i + 2 * by) % n) for i in range(n)])

    def pass_on(x, lead, by):
        perm = []
        for k in range(lead, lead + 2 * pieces, 2):
            if by <= k < count:
                sender, target = k % pairs, (k - by) % pairs
                perm += [(2 * sender + c, 2 * target + c) for c in range(2)]
        return lax.ppermute(x, "blk", perm)

    def pack(rows, turnout=turnout):
        return call(
            functools.partial(pack_kernel, rows),
            "pack",
            (shaped(packed_rows, bs),) * len(rows),
            (jnp.transpose(col_index, (2, 1, 0)), turnout, district_of, lower_blocks, diag_inverse, rhs),
            56,
            moved=8 * packed_rows * bs * len(rows),
            in_specs=[SMEM_SPEC, VMEM_SPEC, VMEM_SPEC] + [HBM_SPEC] * 3,
            out_specs=(HBM_SPEC,) * len(rows),
            scratch_shapes=[
                pltpu.VMEM((len(rows), bs, columns), F32),
                pltpu.VMEM((len(rows), packed_rows, bs), F32),
                pltpu.SemaphoreType.DMA((len(rows) * (2 * slots + 4),)),
            ],
        )

    def setup(r):
        args = (r, n, slots, columns)
        held = shaped(4, bs, bs, dtype=B16)
        gh, gl, mh, ml, rt = call(
            functools.partial(near_setup_kernel, *args),
            "near_setup",
            (square, square, held, held, shaped(half, 2 * bs)),
            packs[r],
            10,
            14 * 3 * bs**3,
            24 * bs * bs * 4,
        )
        fh, fl = call(
            functools.partial(far_setup_kernel, *args),
            "far_setup",
            (square, square),
            (*packs[r], mh, ml),
            10,
            10 * 3 * bs**3,
            24 * bs * bs * 4,
        )
        return gh, gl, mh, ml, rt, fh, fl

    def finish(r, values, total):
        first = count - 1 - (r * pairs + pairs - 1)
        window = values[first : first + pairs + 2 * (pieces - 1)]
        is_last = r == 0
        outs = (shaped(half, bs), shaped(half, bs))
        outs += (shaped(NDIST // pairs, columns),) * pairs if is_last else (shaped(NDIST, columns),)
        extra = () if total is None else (total,)
        return call(
            functools.partial(
                finish_kernel, slots, pairs, pieces, len(window), total is not None, is_last
            ),
            "finish",
            outs,
            (*window, *fixed[r][2:4], *packs[r], *extra),
            8,
            6 * 3 * half * bs * bs,
            16 * bs * bs,
            scratch_shapes=[pltpu.VMEM((NDIST, columns), F32)] if is_last else [],
        )

    top = rows_here - 1
    packs, fixed = {}, {}
    (own,) = pack((top,))
    packs[top] = (own, swap(own))
    later, _ = lax.optimization_barrier((turnout, own))
    packed = pack(tuple(range(top)), later) if top else ()
    for r in range(top - 1, -1, -1):
        packs[r] = (packed[r], swap(packed[r]))
    fixed[top] = setup(top)

    keeps, gots = {}, {}
    values = []
    ordered = ()
    total = near = far_now = far_next = None
    steps = count + 2 * (pieces - 1)
    for step in range(steps):
        lead = count - 1 - step
        low = max(lead, 0) // pairs
        high = min(lead + 2 * (pieces - 1), count - 1) // pairs
        rows = range(low, high + 1)
        taken = [x for x in (far_now, near) if x is not None]
        has_near = step + 1 < steps
        has_far = step + 2 < steps
        operands = []
        for r in rows:
            gh, gl, _, _, rt, _, _ = fixed[r]
            operands += [rt, gh, gl] if has_near else [rt]
        place = (lead, pairs, pieces, high * pairs)
        v, *near_out = call(
            functools.partial(near_kernel, *place, len(ordered), len(taken), has_near),
            "near_terms",
            (wide, wide) if has_near else (wide,),
            (*ordered, *taken, *operands),
            4,
            6 * width * 4 * bs * bs,
            6 * width * bs * 4,
        )
        values.append(v)
        near = pass_on(near_out[0], lead, 1) if has_near else None
        far_now, far_next, ordered = far_next, None, ()
        if has_far:
            operands = [x for r in rows for x in fixed[r][5:]]
            far_out = call(
                functools.partial(far_kernel, *place),
                "far_terms",
                wide,
                (v, *operands),
                4,
                6 * width * 4 * bs * bs,
                6 * width * bs * 4,
            )
            ordered = (far_out,)
            r, chip = lead // pairs, lead % pairs
            if chip == pairs - 1 and r > 0:
                fixed[r - 1] = setup(r - 1)
            far_next = pass_on(far_out, lead, 2)
        done = lead + 2 * (pieces - 1)
        if done % pairs == 0 and 0 < done // pairs <= top:
            r = done // pairs
            keeps[r], give, total = finish(r, values, total)
            gots[r] = swap(give)
            near, total = lax.optimization_barrier((near, total))

    keeps[0], give, *parts = finish(0, values, total)
    gots[0] = swap(give)
    parts = [parts[0]] + [shift(parts[by], by) for by in range(pairs - 1, 0, -1)]
    order = range(rows_here)
    field = call(
        functools.partial(field_kernel, rows_here),
        "field",
        shaped(rows_here, 1, bs, columns),
        (*[keeps[r] for r in order], *[gots[r] for r in order]),
        4,
        0,
        8 * rows_here * bs * columns,
    )
    parts, field = lax.optimization_barrier((parts, field))
    held = shaped(NDIST // n, columns)
    mine, theirs = call(add_kernel, "district_add", (held, held), tuple(parts), 4)
    mean = call(mean_kernel, "district_mean", held, (mine, swap(theirs)), 4)
    return field, mean


def solution(mesh):
    placed = (
        P(None, "blk", None, "sims"),
        P(None, "blk", None, None, None),
        P(None, "blk", None),
        P(None, "blk", None, None),
        P(None, "blk", None),
        P(None, "blk", None),
    )
    return jax.shard_map(
        body,
        mesh=mesh,
        in_specs=placed,
        out_specs=(P(None, "blk", None, "sims"), P("blk", "sims")),
        check_vma=False,
    )
```
